32 devices in a mesh: dp: 4 (over z), tensor: 8 (over y, x, core).
Axes of the slice: x: 2, y: 2, z: 4, core: 2. Of those that a mesh axis runs over, the one named last changes fastest.
Arguments:
- tokens: bfloat16 [8192, 2048], P(('dp', 'tensor')), may hold values from -6 to 6
- attn_gain: float32 [2048], replicated, may hold values from 0.25 to 1.75
- ffn_gain: float32 [2048], replicated, may hold values from 0.25 to 1.75
- qkv_base: bfloat16 [3, 2048, 2048], P(None, None, 'tensor'), may hold values from -0.125 to 0.125
- qkv_first: float32 [3, 2048, 16], replicated, may hold values from -0.125 to 0.125
- qkv_second: float32 [3, 16, 2048], P(None, None, 'tensor'), may hold values from -0.36 to 0.36
- qkv_magnitude: float32 [3, 2048], P(None, 'tensor'), may hold values from 0.25 to 1.75
- output_frozen_weight: bfloat16 [2048, 2048], P('tensor'), may hold values from -0.125 to 0.125
- output_first: float32 [2048, 16], P('tensor'), may hold values from -0.125 to 0.125
- output_upper_map: float32 [16, 2048], replicated, may hold values from -0.36 to 0.36
- output_magnitude: float32 [2048], replicated, may hold values from 6 to 14
- gate_up_base: bfloat16 [2, 2048, 5632], P(None, None, 'tensor'), may hold values from -0.125 to 0.125
- gate_up_first: float32 [2, 2048, 16], replicated, may hold values from -0.125 to 0.125
- gate_up_second: float32 [2, 16, 5632], P(None, None, 'tensor'), may hold values from -0.36 to 0.36
- gate_up_magnitude: float32 [2, 5632], P(None, 'tensor'), may hold values from 0.25 to 1.75
- down_frozen_weight: bfloat16 [5632, 2048], P('tensor'), may hold values from -0.078125 to 0.078125
- down_first: float32 [5632, 16], P('tensor'), may hold values from -0.078125 to 0.078125
- down_upper_map: float32 [16, 2048], replicated, may hold values from -0.36 to 0.36
- down_magnitude: float32 [2048], replicated, may hold values from 1 to 3
- lengths: int32 [4], P('dp'), may hold values from 512 to 2048, as said below
- cotangent: bfloat16 [8192, 2048], P(('dp', 'tensor')), may hold values from -6 to 6
Outputs:
- result: bfloat16 [8192, 2048], P(('dp', 'tensor'))
- tokens_grad: float32 [8192, 2048], P(('dp', 'tensor'))
- qkv_first_grad: float32 [3, 2048, 16], replicated
- qkv_second_grad: float32 [3, 16, 2048], P(None, None, 'tensor')
- qkv_magnitude_grad: float32 [3, 2048], P(None, 'tensor')
- output_first_grad: float32 [2048, 16], P('tensor')
- output_upper_gradient: float32 [16, 2048], replicated
- output_magnitude_grad: float32 [2048], replicated
- gate_up_first_grad: float32 [2, 2048, 16], replicated
- gate_up_second_grad: float32 [2, 16, 5632], P(None, None, 'tensor')
- gate_up_magnitude_grad: float32 [2, 5632], P(None, 'tensor')
- down_lower_gradient: float32 [5632, 16], P('tensor')
- down_upper_gradient: float32 [16, 2048], replicated
- down_magnitude_grad: float32 [2048], replicated
The draws below stay inside these ranges and needn't reach their ends.
Inputs may be any that keep to these rules, and one draw needn't show every extreme that they name: `lengths`: one sequence in all has exactly 2048 used positions.
All inputs are finite; a program needn't handle non-finite values.
Results may differ from the reference program's by a relative error of at most 0.023.
Values may be sent and summed in bfloat16 or wider, within the bound.
A program may use at most 256 MiB of HBM per device.

```python
import jax
import jax.numpy as jnp
from jax import lax

D = 2048
HEADS = 16
HDIM = 128
FF = 5632
RANK = 16
BUCKET = 2048
TOKENS = 8192
SEQS = 4


def draw_lengths(key, part):
    key = jax.random.fold_in(key, 7)
    length_key, pick_key = jax.random.split(key)
    drawn = jax.random.randint(length_key, (SEQS,), BUCKET // 4, BUCKET + 1)
    chosen = jax.random.randint(pick_key, (), 0, SEQS)
    return jnp.where(jnp.arange(SEQS) == chosen, BUCKET, drawn).astype(jnp.int32)


def level_of(key, shape, shards, least, largest):
    def one(axis_at, shards_of):
        heights = jax.random.uniform(jax.random.fold_in(jax.random.fold_in(key, 6), axis_at), (shards_of,), jnp.float32, least / len(shards), largest / len(shards))
        return jnp.repeat(jnp.exp(heights), shape[axis_at] // shards_of).reshape((-1,) + (1,) * (len(shape) - axis_at - 1))

    level = one(*shards[0])
    for cut in shards[1:]:
        level = level * one(*cut)
    return level


def gaussian(own_key, extent, scale, reach, cuts=(), kind=jnp.bfloat16):
    values = scale * jax.random.normal(own_key, extent, jnp.float32)
    if cuts:
        values = values * level_of(own_key, extent, cuts, -0.22, 0.18)
    return jnp.clip(values, -reach, reach).astype(kind)


def setup_inputs(seed: int = 0) -> dict:
    seeds = jax.random.split(jax.random.key(seed), 22)
    tokens = gaussian(seeds[0], (TOKENS, D), 1.0, 6.0, ((0, 32),))
    attn_gain = jnp.clip(1.0 + 0.15 * jax.random.normal(seeds[1], (D,), jnp.float32), 0.25, 1.75)
    ffn_gain = jnp.clip(1.0 + 0.15 * jax.random.normal(seeds[2], (D,), jnp.float32), 0.25, 1.75)
    qkv_base = gaussian(seeds[3], (3, D, HEADS * HDIM), D ** -0.5, 0.125, ((2, 8),))
    qkv_first = gaussian(seeds[4], (3, D, RANK), D ** -0.5, 0.125, (), jnp.float32)
    qkv_second = gaussian(seeds[5], (3, RANK, HEADS * HDIM), 0.06, 0.36, ((2, 8),), jnp.float32)
    qkv_magnitude = jnp.clip(1.0 + 0.15 * jax.random.normal(seeds[6], (3, HEADS * HDIM), jnp.float32), 0.25, 1.75)
    output_frozen_weight = gaussian(seeds[7], (HEADS * HDIM, D), (HEADS * HDIM) ** -0.5, 0.125, ((0, 8),))
    output_first = gaussian(seeds[8], (HEADS * HDIM, RANK), (HEADS * HDIM) ** -0.5, 0.125, ((0, 8),), jnp.float32)
    output_upper_map = gaussian(seeds[9], (RANK, D), 0.06, 0.36, (), jnp.float32)
    output_magnitude = jnp.clip(jax.random.uniform(seeds[10], (D,), jnp.float32, 6.0, 14.0), 6.0, 14.0)
    gate_up_base = gaussian(seeds[11], (2, D, FF), D ** -0.5, 0.125, ((2, 8),))
    gate_up_first = gaussian(seeds[12], (2, D, RANK), D ** -0.5, 0.125, (), jnp.float32)
    gate_up_second = gaussian(seeds[13], (2, RANK, FF), 0.06, 0.36, ((2, 8),), jnp.float32)
    gate_up_magnitude = jnp.clip(1.0 + 0.15 * jax.random.normal(seeds[14], (2, FF), jnp.float32), 0.25, 1.75)
    down_frozen_weight = gaussian(seeds[15], (FF, D), FF ** -0.5, 0.078125, ((0, 8),))
    down_first = gaussian(seeds[16], (FF, RANK), FF ** -0.5, 0.078125, ((0, 8),), jnp.float32)
    down_upper_map = gaussian(seeds[17], (RANK, D), 0.06, 0.36, (), jnp.float32)
    down_magnitude = jnp.clip(jax.random.uniform(seeds[18], (D,), jnp.float32, 1.0, 3.0), 1.0, 3.0)
    lengths = draw_lengths(jax.random.fold_in(seeds[21], 71), 0)
    cotangent = gaussian(seeds[20], (TOKENS, D), 1.0, 6.0, ((0, 32),))
    return dict(tokens=tokens, attn_gain=attn_gain, ffn_gain=ffn_gain, qkv_base=qkv_base, qkv_first=qkv_first, qkv_second=qkv_second, qkv_magnitude=qkv_magnitude, output_frozen_weight=output_frozen_weight, output_first=output_first, output_upper_map=output_upper_map, output_magnitude=output_magnitude, gate_up_base=gate_up_base, gate_up_first=gate_up_first, gate_up_second=gate_up_second, gate_up_magnitude=gate_up_magnitude, down_frozen_weight=down_frozen_weight, down_first=down_first, down_upper_map=down_upper_map, down_magnitude=down_magnitude, lengths=lengths, cotangent=cotangent)


@jax.custom_vjp
def reduced_value(v):
    return lax.optimization_barrier(v.astype(jnp.bfloat16)).astype(jnp.float32)

@jax.custom_vjp
def reduced_backward(v):
    return v

def low_keep(v):
    return (reduced_value(v), None)

def low_pass(kept, grad):
    return (grad,)

def back_keep(v):
    return (v, None)

def back_low(kept, grad):
    return (reduced_value(grad),)
reduced_value.defvjp(low_keep, low_pass)
reduced_backward.defvjp(back_keep, back_low)
exact_product = lax.Precision.HIGHEST
NORM_EPS = 1e-05
ADAPTER_SCALE = 2.0
ROPE_THETA = 10000.0
MASKED = -1e+30

def matrix_product(left_side, right_side):
    return jnp.dot(left_side, right_side, precision=exact_product)

def rms_norm(values, norm_gain):
    return values * lax.rsqrt(lax.optimization_barrier(jnp.mean(values * values, axis=-1, keepdims=True)) + NORM_EPS) * norm_gain

def rotate(values, positions, unit_direction):
    row_count = values.shape[0]
    half_dim = HDIM // 2
    shaped = values.reshape(row_count, -1, HDIM)
    frequency = jnp.exp(-jnp.log(ROPE_THETA) * jnp.arange(half_dim).astype(jnp.float32) / half_dim)
    angles = positions.astype(jnp.float32)[:, None] * frequency[None, :]
    cosine = jnp.cos(angles)[:, None, :]
    sine_part = unit_direction * jnp.sin(angles)[:, None, :]
    first_half = shaped[..., :half_dim]
    second_half = shaped[..., half_dim:]
    turned = jnp.concatenate([first_half * cosine - second_half * sine_part, second_half * cosine + first_half * sine_part], axis=-1)
    return turned.reshape(row_count, -1)

def decomposed_linear(input_rows, frozen_base_weight, adapter_lower_map, adapter_upper_map, column_magnitude):
    unit_direction = frozen_base_weight + ADAPTER_SCALE * matrix_product(adapter_lower_map, adapter_upper_map)
    scaling = column_magnitude / jnp.sqrt(lax.optimization_barrier(jnp.sum(unit_direction * unit_direction, axis=0)))
    reduced_rank_term = reduced_backward(reduced_value(matrix_product(input_rows, reduced_value(adapter_lower_map))))
    pre_adapter_output = reduced_backward(matrix_product(input_rows, frozen_base_weight) + ADAPTER_SCALE * matrix_product(reduced_rank_term, reduced_value(adapter_upper_map)))
    return pre_adapter_output * scaling

def attend_slot(packed):
    query_rows, key_rows, value_rows, seq_length = packed
    places = jnp.arange(BUCKET)
    allowed = (places[None, :] <= places[:, None]) & (places[None, :] < seq_length)
    scores = jnp.einsum('qhd,khd->hqk', query_rows, key_rows, precision=exact_product) * HDIM ** (-0.5)
    scores = jnp.where(allowed[None], reduced_backward(scores), MASKED)
    highest = lax.optimization_barrier(jnp.max(scores, axis=-1, keepdims=True))
    powered = jnp.exp(scores - highest)
    weights = powered / lax.optimization_barrier(jnp.sum(powered, axis=-1, keepdims=True))
    return jnp.einsum('hqk,khd->qhd', reduced_value(weights), value_rows, precision=exact_product)

def reference(tokens, attn_gain, ffn_gain, qkv_base, qkv_first, qkv_second, qkv_magnitude, output_frozen_weight, output_first, output_upper_map, output_magnitude, gate_up_base, gate_up_first, gate_up_second, gate_up_magnitude, down_frozen_weight, down_first, down_upper_map, down_magnitude, lengths, cotangent):
    row_index = jnp.arange(TOKENS)
    positions = row_index % BUCKET
    row_length = lengths[row_index // BUCKET]
    valid_rows = (positions < row_length).astype(jnp.float32)
    qkv_wide = qkv_base.astype(jnp.float32)
    output_wide = output_frozen_weight.astype(jnp.float32)
    gate_up_wide = gate_up_base.astype(jnp.float32)
    down_wide = down_frozen_weight.astype(jnp.float32)
    slot_shape = (SEQS, BUCKET, HEADS, HDIM)

    def forward(input_rows, q_first, q_second, q_mag, o_first, o_second, o_mag, g_first, g_second, g_mag, d_first, d_second, d_mag):
        normed = reduced_value(rms_norm(input_rows, attn_gain))
        projected = [decomposed_linear(normed, qkv_wide[member], q_first[member], q_second[member], q_mag[member]) for member in range(3)]
        queries = reduced_value(rotate(projected[0], positions, 1.0))
        key_rows = reduced_value(rotate(projected[1], positions, 1.0))
        value_rows = reduced_value(projected[2])
        attended = lax.map(jax.checkpoint(attend_slot), (queries.reshape(slot_shape), key_rows.reshape(slot_shape), value_rows.reshape(slot_shape), lengths))
        attended = reduced_backward(reduced_value(attended.reshape(TOKENS, HEADS * HDIM)))
        hidden = input_rows + decomposed_linear(attended, output_wide, o_first, o_second, o_mag)
        ffn_normed = reduced_value(rms_norm(hidden, ffn_gain))
        gate_value = decomposed_linear(ffn_normed, gate_up_wide[0], g_first[0], g_second[0], g_mag[0])
        up_value = decomposed_linear(ffn_normed, gate_up_wide[1], g_first[1], g_second[1], g_mag[1])
        swiglu = reduced_backward(reduced_value(jax.nn.silu(gate_value) * up_value))
        return hidden + decomposed_linear(swiglu, down_wide, d_first, d_second, d_mag)
    result, pull = jax.vjp(forward, tokens.astype(jnp.float32), qkv_first, qkv_second, qkv_magnitude, output_first, output_upper_map, output_magnitude, gate_up_first, gate_up_second, gate_up_magnitude, down_first, down_upper_map, down_magnitude)
    grads = pull(cotangent.astype(jnp.float32) * valid_rows[:, None])
    return (result.astype(jnp.bfloat16), grads[0], grads[1], grads[2], grads[3], grads[4], grads[5], grads[6], grads[7], grads[8], grads[9], grads[10], grads[11], grads[12])
```

```python
import functools

import jax
import jax.numpy as jnp
import numpy as np
from jax import lax
from jax.experimental import pallas as pl
from jax.experimental.pallas import tpu as pltpu
from jax.sharding import PartitionSpec as P

HDIM = 128
F32 = jnp.float32
BF16 = jnp.bfloat16
EXACT = lax.Precision.HIGHEST
NORM_EPS = 1e-05
ROPE_THETA = 10000.0
MASKED = -1e30
SOFTMAX_SCALE = HDIM**-0.5
LOG2E = 1.4426950408889634
VMEM_LIMIT = 60 * 2**20
TILE = 256
ANY = pl.BlockSpec(memory_space=pl.ANY)
VMEM = pl.BlockSpec(memory_space=pltpu.VMEM)
SMEM = pl.BlockSpec(memory_space=pltpu.SMEM)
MESH = pl.DeviceIdType.MESH
DMA = pltpu.SemaphoreType.DMA


def nn(left, right, precision=None):
    return jnp.dot(left, right, preferred_element_type=F32, precision=precision)


def nt(left, right, precision=None):
    return lax.dot_general(
        left, right, (((1,), (1,)), ((), ())), preferred_element_type=F32, precision=precision
    )


def tn(left, right):
    return lax.dot_general(left, right, (((0,), (0,)), ((), ())), preferred_element_type=F32)


def shape(dims, dtype):
    return jax.ShapeDtypeStruct(dims, dtype)


def tiles(size):
    return [(begin, min(TILE, size - begin)) for begin in range(0, size, TILE)]


def slots_of(count):
    if count == 8:
        return [(0, 0), (2, 4), (6, 6), (4, 2)]
    return [(mask, mask) for mask in range(0, count, 2)]


class Sender:
    def __init__(self):
        self.place = lax.axis_index("dp")
        self.me = lax.axis_index("tensor")

    def meet(self, masks, places=()):
        barrier = pltpu.get_barrier_semaphore()
        for mask in masks:
            pl.semaphore_signal(
                barrier, inc=1, device_id=(self.place, self.me ^ mask), device_id_type=MESH
            )
        for place in places:
            pl.semaphore_signal(
                barrier, inc=1, device_id=(self.place ^ place, self.me), device_id_type=MESH
            )
        pl.semaphore_wait(barrier, len(masks) + len(places))

    def copy(self, source, target, sems, mask, flip=0, step=0):
        place = self.place ^ flip if flip else self.place + step if step else self.place
        return pltpu.make_async_remote_copy(
            src_ref=source,
            dst_ref=target,
            send_sem=sems[0],
            recv_sem=sems[1],
            device_id=(place, self.me ^ mask if mask else self.me),
            device_id_type=MESH,
        )


def gather_stages(sender, count, own, slots, sems, begin=1, end=None):
    half = own.shape[0] // 2

    def rows(ref, slot, h):
        return ref.at[slot, pl.ds(h * half, half)]

    def message(slot, h, source, mask):
        return sender.copy(
            source, rows(slots, slot, h), (sems.at[0, slot, h], sems.at[1, slot, h]), mask
        )

    mine = [own.at[pl.ds(h * half, half)] for h in range(2)]
    if count != 8:
        stages = range(begin, end or count // 2)
        return {s: [message(s, h, mine[h], 2 * s) for h in range(2)] for s in stages}
    routes = {
        1: [(mine[0], 2), (mine[1], 4)],
        2: [(rows(slots, 1, 0), 4), (rows(slots, 1, 1), 2)],
        3: [(mine[0], 4), (mine[1], 2)],
    }
    return {s: [message(s, h, *routes[s][h]) for h in range(2)] for s in range(begin, end or 4)}


def reduce_stages(sender, count, parts, landed, sems, last=3, begin=1, end=4):
    half = parts.shape[1] // 2

    def message(slot, h, mask):
        at = pl.ds(h * half, half)
        return sender.copy(
            parts.at[last if slot == 3 and count == 8 else slot, at], landed.at[slot, at], (sems.at[0, slot, h], sems.at[1, slot, h]), mask
        )

    if count != 8:
        return {s: [message(s, h, 2 * s) for h in range(2)] for s in range(1, count // 2)}
    routes = {1: (2, 4), 2: (2, 4), 3: (4, 2)}
    return {s: [message(s, h, routes[s][h]) for h in range(2)] for s in range(begin, end)}


def relay(part, landed, sums):
    arrive(sums[2])
    part[...] = (part[...].astype(F32) + landed[2].astype(F32)).astype(BF16)
    start(sums[3])


def finish_reduce(count, part, landed, sums, out):
    slots = count // 2
    added = (1, 3) if count == 8 else tuple(range(1, slots))
    for slot in added:
        arrive(sums[slot])

    def columns(step, carry):
        d = pl.ds(pl.multiple_of(step * TILE, TILE), TILE)
        total = part[:, d].astype(F32)
        for slot in added:
            total = total + landed[slot, :, d].astype(F32)
        return out(d, total, carry)

    return columns


def leave_stages(sums):
    for copies in sums.values():
        leave(copies)


def norm_statistics(values_of, grads_of, features, rows):
    def columns(step, carry):
        squares, products = carry
        d = pl.ds(pl.multiple_of(step * TILE, TILE), TILE)
        values = values_of(d)
        squares = squares + jnp.sum(values * values, axis=1, keepdims=True)
        products = products + jnp.sum(values * grads_of(d), axis=1, keepdims=True)
        return squares, products

    zero = jnp.zeros((rows, 1), F32)
    squares, products = lax.fori_loop(0, features // TILE, columns, (zero, zero))
    scale = lax.rsqrt(squares * (1.0 / features) + NORM_EPS)
    return scale, products * (1.0 / features) * scale * scale * scale


class Totals:
    def __init__(self, sender, count, depth, pay, along_in, part, group_in, block, span, main, sems):
        self.sender, self.count, self.depth = sender, count, depth
        self.pay, self.along_in, self.part, self.group_in = pay, along_in, part, group_in
        self.block, self.whole, self.main, self.sems = block, span, main, sems
        self.others, self.flips = range(1, count), range(1, depth)
        self.width = part.shape[1]
        self.height, self.length = block.shape
        self.high = part.shape[0] // self.height
        self.place = sender.place

    def columns(self, place):
        return pl.ds(pl.multiple_of(place * self.width, self.width), self.width)

    def block_of(self, ref, index):
        row = lax.rem(index, self.high) * self.height
        lane = lax.div(index, self.high) * self.length
        return ref.at[
            pl.ds(pl.multiple_of(row, self.height), self.height),
            pl.ds(pl.multiple_of(lane, self.length), self.length),
        ]

    def pair(self, step, which):
        return self.sems.at[0, step, which], self.sems.at[1, step, which]

    def to_place(self, flip):
        source = self.pay.at[:, self.columns(self.place ^ flip)]
        return self.sender.copy(source, self.along_in.at[flip], self.pair(0, flip), 0, flip)

    def to_owner(self, mask):
        source = self.block_of(self.part, self.sender.me ^ mask)
        return self.sender.copy(source, self.group_in.at[mask], self.pair(1, mask), mask)

    def to_group(self, mask, index):
        return self.sender.copy(self.block, self.block_of(self.whole, index), self.pair(2, mask), mask)

    def to_all(self, flip, place):
        return self.sender.copy(self.whole, self.main.at[:, self.columns(place)], self.pair(3, flip), 0, flip)

    def give(self):
        for flip in self.flips:
            self.to_place(flip).start()

    def add_along(self):
        total = self.pay[:, self.columns(self.place)].astype(F32)
        for flip in self.flips:
            self.to_place(flip).wait_recv()
            total = total + self.along_in[flip].astype(F32)
        self.part[...] = total.astype(BF16)
        for mask in self.others:
            self.to_owner(mask).start()

    def add_group(self):
        me = self.sender.me
        total = self.block_of(self.part, me)[...].astype(F32)
        for mask in self.others:
            self.to_owner(mask).wait_recv()
            total = total + self.group_in[mask].astype(F32)
        self.block[...] = total.astype(BF16)
        for mask in self.others:
            self.to_group(mask, me).start()
        self.block_of(self.whole, me)[...] = self.block[...]

    def share(self):
        for mask in self.others:
            self.to_group(mask, self.sender.me ^ mask).wait_recv()
        for flip in self.flips:
            self.to_all(flip, self.place).start()
        self.main[:, self.columns(self.place)] = self.whole[...]

    def take(self):
        for flip in self.flips:
            self.to_all(flip, self.place ^ flip).wait_recv()

    def end(self):
        for flip in self.flips:
            self.to_place(flip).wait_send()
            self.to_all(flip, self.place).wait_send()
        for mask in self.others:
            self.to_owner(mask).wait_send()
            self.to_group(mask, self.sender.me).wait_send()


def along_total(sender, depth, ref):
    total = ref[sender.place].astype(F32)
    for index in range(1, depth):
        total = total + ref[sender.place ^ index].astype(F32)
    return total


def totals_scratch(rows, features, count, depth):
    height = 16
    width = features // depth
    if width * (rows // height) // count < HDIM:
        rows = 8 * height
    length = width * rows // height // count
    return [
        pltpu.VMEM((rows, features), BF16),
        pltpu.VMEM((depth, rows, width), BF16),
        pltpu.VMEM((rows, width), BF16),
        pltpu.VMEM((count, height, length), BF16),
        pltpu.VMEM((height, length), BF16),
        pltpu.VMEM((rows, width), BF16),
        pltpu.VMEM((rows, features), BF16),
        DMA((2, 4, max(count, depth))),
    ]


class Mover:
    def __init__(self, sems):
        self.sems, self.many = sems, 0

    def __call__(self, source, target):
        copy = pltpu.make_async_copy(source, target, self.sems.at[self.many])
        self.many += 1
        copy.start()
        return copy


def start(copies):
    for copy in copies:
        copy.start()


def arrive(copies):
    for copy in copies:
        copy.wait_recv()


def leave(copies):
    for copy in copies:
        copy.wait_send()


def start_all(pairs, sems):
    copies = []
    for at, (source, target) in enumerate(pairs):
        copy = pltpu.make_async_copy(source, target, sems.at[at])
        copy.start()
        copies.append(copy)
    return copies


def call(body, name, out_shape, in_specs, out_specs, scratch, flops, moved, operands, identity):
    return pl.pallas_call(
        body,
        name=name,
        out_shape=out_shape,
        in_specs=in_specs,
        out_specs=out_specs,
        scratch_shapes=scratch,
        compiler_params=pltpu.CompilerParams(
            vmem_limit_bytes=VMEM_LIMIT, collective_id=identity, has_side_effects=True
        ),
        cost_estimate=pl.CostEstimate(flops=flops, bytes_accessed=moved, transcendentals=0),
    )(*operands)


def split(value):
    high = value.astype(BF16)
    return high, (value - high.astype(F32)).astype(BF16)


def left_stack(value):
    high, low = split(value)
    return jnp.concatenate([high, high, low], axis=0)


def right_stack(value):
    high, low = split(value)
    return jnp.concatenate([high, low, high], axis=0)


def first_direction(wide, first_t, second):
    rank = second.shape[0]
    gram = nt(first_t, first_t, EXACT)
    return wide[:rank] + wide[rank:] + 2.0 * nn(gram, second, EXACT)


def second_direction(factored, second, base, first_t):
    rank = second.shape[0]
    wide = nt(jnp.concatenate(split(factored), axis=0), base)
    gram = nt(factored, second, EXACT)
    return wide[:rank] + wide[rank:] + 2.0 * nn(gram, first_t, EXACT)


def line_forward(sender, depth, source, target, part, back, sems):
    place, last = sender.place, depth - 1

    def rows(ref, at):
        return ref.at[pl.ds(1, 3), pl.ds(pl.multiple_of(at * part, part), part)]

    def sends(act):
        @pl.when((place >= back) & (place < last))
        def _():
            at = place - back
            act(sender.copy(rows(source, at), rows(target, at), (sems.at[0, 0], sems.at[1, 0]), 0, 0, 1))

        @pl.when((place <= last - back) & (place > 0))
        def _():
            at = place + back
            act(sender.copy(rows(source, at), rows(target, at), (sems.at[0, 1], sems.at[1, 1]), 0, 0, -1))

    def arrivals(act):
        @pl.when(place > back)
        def _():
            at = place - back - 1
            act(sender.copy(rows(target, at), rows(target, at), (sems.at[0, 0], sems.at[1, 0]), 0, 0, -1))

        @pl.when(place < last - back)
        def _():
            at = place + back + 1
            act(sender.copy(rows(target, at), rows(target, at), (sems.at[0, 1], sems.at[1, 1]), 0, 0, 1))

    return sends, arrivals


def project_body(
    count, depth, lengths, tokens, gain, cot, w_own, gu_own, d_own, o_own,
    qa, qb, qmag, ga, gb, gmag, oa, ob, da, db,
    heads, rows_all, w_par, gu_par, d_par, wq, at_all, q_stat, g_stat, r_stat, upstream,
    u, w, wgu, wd, wo, to_par, to_own, second_own, second_par, b_par, sq_all,
    sems, gather_sems, par_sems, head_sems, own_sems, weight_sems, piece_sems, line_sems, small_sems,
):
    sender = Sender()
    slots = slots_of(count)
    maps, _, width = w_own.shape
    rows, features = tokens.shape
    half = rows // 2
    units = d_own.shape[0]
    rank = qb.shape[1]
    shared = count == 8 and depth == 4
    heights = o_own.shape[0]
    part = heights // depth if shared else heights
    others = list(range(1, count))
    sender.meet(others, range(1, depth) if shared else ())

    pieces = []
    for slot in range(1, count // 2):
        at = pl.ds(pl.multiple_of(sender.place * part, part), part) if shared else pl.ds(0, heights)
        pieces.append(
            sender.copy(
                o_own.at[at], wq.at[slot, at], (piece_sems.at[0, slot], piece_sems.at[1, slot]), 2 * slot
            )
        )
    start(pieces)
    stages = gather_stages(sender, count, u.at[0], u, gather_sems)
    weights = [
        sender.copy(source, target, (weight_sems.at[0, at], weight_sems.at[1, at]), 1)
        for at, (source, target) in enumerate(
            ((w_own, w_par), (qb, b_par), (gu_own, gu_par), (d_own, d_par))
        )
    ]
    start(weights[:2])
    smalls = [
        sender.copy(
            oa, at_all.at[mask], (small_sems.at[0, 0, mask], small_sems.at[1, 0, mask]), mask
        )
        for mask in others
    ]
    start(smalls)
    at_all[0] = oa[...]
    local = start_all(
        [(w_own, w.at[pl.ds(0, maps)]), (d_own, wd), (o_own, wo), (gu_own, wgu), (o_own, wq.at[0])],
        sems,
    )
    squares = jnp.zeros((rows, 1), F32)
    for begin in range(0, features, TILE):
        values = tokens[:, pl.ds(begin, TILE)].astype(F32)
        squares = squares + jnp.sum(values * values, axis=1, keepdims=True)
    scale = lax.rsqrt(squares * (1.0 / features) + NORM_EPS)
    for begin in range(0, features, TILE):
        d = pl.ds(begin, TILE)
        u[0, :, d] = (tokens[:, d].astype(F32) * scale * gain[:, d]).astype(BF16)
    start(stages[1])
    if count != 8:
        for slot in range(2, len(slots)):
            start(stages[slot])
    second_own[...] = jnp.zeros_like(second_own)
    second_par[...] = jnp.zeros_like(second_par)
    for s in range(maps):
        second_own[pl.ds(s * rank, rank), pl.ds(s * width, width)] = (2.0 * qb[s]).astype(BF16)
    first_t = qa[...].reshape(maps * rank, features).astype(BF16)
    local[0].wait()
    pending, sent = [], []

    def one_slot(slot):
        masks = slots[slot]
        keep = pltpu.make_async_copy(u.at[slot], rows_all.at[slot], own_sems.at[slot])
        keep.start()
        pending.append(keep)
        lowrank = nt(u[slot], first_t).astype(BF16)
        for s in range(maps):
            lanes = pl.ds(s * width, width)
            to_own[slot, :, lanes] = (nn(u[slot], w[s]) + nn(lowrank, second_own[:, lanes])).astype(BF16)
        if slot == 0:
            arrive(weights[:2])
            load = pltpu.make_async_copy(w_par, w.at[pl.ds(maps, maps)], sems.at[5])
            load.start()
            for s in range(maps):
                second_par[pl.ds(s * rank, rank), pl.ds(s * width, width)] = (2.0 * b_par[s]).astype(BF16)
            load.wait()
        for s in range(maps):
            lanes = pl.ds(s * width, width)
            to_par[slot, :, lanes] = (
                nn(u[slot], w[maps + s]) + nn(lowrank, second_par[:, lanes])
            ).astype(BF16)
        for h, mask in enumerate(masks):
            at = pl.ds(h * half, half)
            keep = pltpu.make_async_copy(
                to_own.at[slot, at], heads.at[mask, at], head_sems.at[slot, h]
            )
            send = sender.copy(
                to_par.at[slot, at],
                heads.at[mask ^ 1, at],
                (par_sems.at[0, slot, h], par_sems.at[1, slot, h]),
                1,
            )
            send.start()
            keep.start()
            pending.append(keep)
            sent.append(send)

    def next_slot(slot):
        arrive(stages[slot])
        if count == 8 and slot + 1 < len(slots):
            start(stages[slot + 1])
        one_slot(slot)

    one_slot(0)
    place = sender.me * rows + lax.broadcasted_iota(jnp.int32, (rows, 1), 0)
    upstream[...] = jnp.where(place < lengths[0], cot[...].astype(F32), 0.0).astype(BF16)

    local[1].wait()
    local[2].wait()
    down_left, down_right = left_stack(da[...]), right_stack(db[...])
    total = jnp.zeros((1, features), F32)
    for begin, span in tiles(units):
        direction = wd[pl.ds(begin, span), :].astype(F32) + 2.0 * tn(
            down_left[:, begin : begin + span], down_right
        )
        total = total + jnp.sum(direction * direction, axis=0, keepdims=True)
    sq_all[0, 1:2, :] = total
    direction = wo[...].astype(F32) + 2.0 * tn(left_stack(oa[...]), right_stack(ob[...]))
    sq_all[0, 0:1, :] = jnp.sum(direction * direction, axis=0, keepdims=True)
    squares = [
        sender.copy(
            sq_all.at[0], sq_all.at[mask], (small_sems.at[0, 1, mask], small_sems.at[1, 1, mask]), mask
        )
        for mask in others
    ]
    start(squares)
    r_stat[0, 8 : 8 + rank] = jnp.zeros((rank, features), F32)
    r_stat[1, 8 : 8 + rank] = first_direction(
        nn(jnp.concatenate(split(da[...]), axis=0), wd[...]), da[...], db[...]
    )
    arrive(pieces)
    start(weights[2:])
    if shared:
        sends0, arrivals0 = line_forward(sender, depth, wq, wq, part, 0, line_sems.at[0])
        sends1, arrivals1 = line_forward(sender, depth, wq, wq, part, 1, line_sems.at[1])
        sends0(lambda copy: copy.start())

    for s in range(maps):
        left, right = left_stack(qa[s]), right_stack(qb[s])
        total = jnp.zeros((1, width), F32)
        for begin in range(0, features, 512):
            direction = w[s, pl.ds(begin, 512), :].astype(F32) + 2.0 * tn(
                left[:, begin : begin + 512], right
            )
            total = total + jnp.sum(direction * direction, axis=0, keepdims=True)
        norm = jnp.sqrt(total)
        q_stat[s, 0:1] = norm
        q_stat[s, 1:2] = qmag[s : s + 1] / norm
        q_stat[s, 8 : 8 + rank] = first_direction(
            nn(jnp.concatenate(split(qa[s]), axis=0), w[s]), qa[s], qb[s]
        )
    next_slot(1)

    local[3].wait()
    ones = jnp.ones((8, HDIM), BF16)
    for s in range(2):
        left, right = left_stack(gb[s]), right_stack(ga[s])
        for begin, span in tiles(units):
            direction = wgu[s, pl.ds(begin, span), :].astype(F32) + 2.0 * tn(
                left[:, begin : begin + span], right
            )
            direction = direction * direction
            folded = direction[:, :HDIM]
            for lane in range(HDIM, features, HDIM):
                folded = folded + direction[:, lane : lane + HDIM]
            high, low = split(folded)
            norm = jnp.sqrt((nt(ones, high) + nt(ones, low))[:1])
            f = pl.ds(begin, span)
            g_stat[s, 0:1, f] = norm
            g_stat[s, 1:2, f] = gmag[s : s + 1, f] / norm
        g_stat[s, 8 : 8 + rank] = first_direction(
            nt(jnp.concatenate(split(ga[s]), axis=0), wgu[s]), ga[s], gb[s]
        )
        if shared and s == 0:
            arrivals0(lambda copy: copy.wait_recv())
            sends1(lambda copy: copy.start())
    for slot in range(2, len(slots)):
        next_slot(slot)
    arrive(squares)
    total = jnp.zeros((2, features), F32)
    for index in range(count):
        total = total + sq_all[sender.me ^ index]
    norm = jnp.sqrt(total)
    r_stat[0, 0:1] = norm[0:1]
    r_stat[1, 0:1] = norm[1:2]

    for copy in pending:
        copy.wait()
    local[4].wait()
    arrive(sent + weights[2:] + smalls)
    leave(sent + weights + smalls + squares + pieces)
    for slot in range(1, len(slots)):
        leave(stages[slot])
    if shared:
        arrivals1(lambda copy: copy.wait_recv())
        sends0(lambda copy: copy.wait_send())
        sends1(lambda copy: copy.wait_send())


def project(lengths, tokens, gain, cot, w_own, gu_own, d_own, o_own, small):
    rows, features = tokens.shape
    count, depth = lax.axis_size("tensor"), lax.axis_size("dp")
    slots = count // 2
    maps, _, width = w_own.shape
    units = d_own.shape[0]
    rank = small[1].shape[1]
    return call(
        functools.partial(project_body, count, depth),
        "project",
        (
            shape((count, rows, maps * width), BF16),
            shape((slots, rows, features), BF16),
            shape(w_own.shape, BF16),
            shape(gu_own.shape, BF16),
            shape(d_own.shape, BF16),
            shape((slots, width, features), BF16),
            shape((count, rank, width), F32),
            shape((maps, 8 + rank, width), F32),
            shape((2, 8 + rank, units), F32),
            shape((2, 8 + rank, features), F32),
            shape((rows, features), BF16),
        ),
        [SMEM] + [VMEM] * 3 + [ANY] * 4 + [VMEM] * len(small),
        (ANY,) * 6 + (VMEM,) * 5,
        [
            pltpu.VMEM((slots, rows, features), BF16),
            pltpu.VMEM((2 * maps, features, width), BF16),
            pltpu.VMEM(gu_own.shape, BF16),
            pltpu.VMEM(d_own.shape, BF16),
            pltpu.VMEM(o_own.shape, BF16),
            pltpu.VMEM((slots, rows, maps * width), BF16),
            pltpu.VMEM((slots, rows, maps * width), BF16),
            pltpu.VMEM((maps * rank, maps * width), BF16),
            pltpu.VMEM((maps * rank, maps * width), BF16),
            pltpu.VMEM((maps, rank, width), F32),
            pltpu.VMEM((count, 2, features), F32),
            DMA((6,)),
            DMA((2, slots, 2)),
            DMA((2, slots, 2)),
            DMA((slots, 2)),
            DMA((slots,)),
            DMA((2, 4)),
            DMA((2, slots)),
            DMA((2, 2, 2)),
            DMA((2, 2, count)),
        ],
        4 * slots * rows * features * maps * width,
        8 * features * maps * width,
        (lengths, tokens, gain, cot, w_own, gu_own, d_own, o_own, *small),
        1,
    )


def turn(values, cosine, sine):
    return values * cosine + pltpu.roll(values, HDIM // 2, 1) * sine


def rms_scale(values):
    return lax.rsqrt(jnp.mean(values * values, axis=1, keepdims=True) + NORM_EPS)


def load_head(count, rows, h, xs, q_stat, cosine, sine, q, k, v):
    lane = pl.ds(pl.multiple_of(h * HDIM, HDIM), HDIM)
    heads = xs.shape[1] // (3 * HDIM)
    for a in range(count):
        at = pl.ds(a * rows, rows)
        cos, sin = cosine[at], sine[at]
        for part, target in enumerate((q, k, v)):
            lanes = pl.ds(pl.multiple_of((part * heads + h) * HDIM, HDIM), HDIM)
            values = xs[at, lanes].astype(F32) * q_stat[part, 1:2, lane]
            if part < 2:
                values = turn(values, cos, sin)
            target[at] = values.astype(BF16)


def attend_forward_body(
    count, depth, lengths, q_stat, cosine_in, sine_in, blocks, wq, at_all, ob, o_mag, r_stat, tokens_in, gain, grads,
    attended_out, logsum, joined_out, w_all, hidden_out, before_out, normed_out, lowrank, c_some,
    xs, q, k, v, wv, cosine, sine, tokens, attended, joined, hidden, before, normed, move_sems, sems, part_sems, line_sems, pair_sems, swap_sems, own_sems, c_sems, w_sems,
):
    sender = Sender()
    me, place = sender.me, sender.place
    length = lengths[0]
    _, rows, width = blocks.shape
    heads = width // (3 * HDIM)
    total = rows * count
    half = rows // 2
    features = ob.shape[1]
    shared = count == 8 and depth == 4
    part = wq.shape[1] // depth
    others = list(range(1, count))
    move = Mover(move_sems)
    copies = start_all(
        [
            (blocks.at[mask], xs.at[pl.ds(pl.multiple_of((me ^ mask) * rows, rows), rows)])
            for mask in range(count)
        ],
        sems,
    )
    copies = copies + [move(cosine_in, cosine), move(sine_in, sine)]
    tokens_load = move(tokens_in, tokens)
    sender.meet(others, range(1, depth) if shared else ())

    stages = gather_stages(sender, count, grads, c_some, c_sems, 1, 3)
    start(stages[1])

    def rows_of(ref, at):
        return ref.at[pl.ds(1, 3), pl.ds(pl.multiple_of(at * part, part), part)]

    if shared:
        whole = pltpu.make_async_copy(wq.at[0], wv.at[0, 0], part_sems.at[depth])
        whole_pair = sender.copy(
            wq.at[0], wv.at[1, 0], (pair_sems.at[0, depth], pair_sems.at[1, depth]), 1
        )
        whole.start()
        whole_pair.start()

        def near(act, act_pair):
            for at in range(depth):

                @pl.when((place - at <= 2) & (at - place <= 2))
                def _():
                    if act is not None:
                        act(pltpu.make_async_copy(rows_of(wq, at), rows_of(wv.at[0], at), part_sems.at[at]))
                    act_pair(
                        sender.copy(
                            rows_of(wq, at), rows_of(wv.at[1], at), (pair_sems.at[0, at], pair_sems.at[1, at]), 1
                        )
                    )

        def far(act):
            for at, other in ((0, depth - 1), (depth - 1, 0)):

                @pl.when(place == other)
                def _():
                    act(
                        sender.copy(
                            rows_of(wv.at[0], at), rows_of(wv.at[1], at),
                            (pair_sems.at[0, at], pair_sems.at[1, at]), 1,
                        )
                    )

        def line_sends(act):
            @pl.when(place == 2)
            def _():
                act(
                    sender.copy(
                        rows_of(wq, 0), rows_of(wv.at[0], 0), (line_sems.at[0, 0], line_sems.at[1, 0]), 0, 0, 1
                    )
                )

            @pl.when(place == 1)
            def _():
                act(
                    sender.copy(
                        rows_of(wq, 3), rows_of(wv.at[0], 3), (line_sems.at[0, 1], line_sems.at[1, 1]), 0, 0, -1
                    )
                )

        def line_arrivals(act):
            @pl.when(place == 3)
            def _():
                act(
                    sender.copy(
                        rows_of(wv.at[0], 0), rows_of(wv.at[0], 0), (line_sems.at[0, 0], line_sems.at[1, 0]), 0, 0, -1
                    )
                )

            @pl.when(place == 0)
            def _():
                act(
                    sender.copy(
                        rows_of(wv.at[0], 3), rows_of(wv.at[0], 3), (line_sems.at[0, 1], line_sems.at[1, 1]), 0, 0, 1
                    )
                )

        line_sends(lambda copy: copy.start())
        near(lambda copy: copy.start(), lambda copy: copy.start())
    else:
        whole = pltpu.make_async_copy(wq, wv.at[0], part_sems.at[0])
        whole_pair = sender.copy(wq, wv.at[1], (pair_sems.at[0, 0], pair_sems.at[1, 0]), 1)
        whole.start()
        whole_pair.start()

    for copy in copies:
        copy.wait()
    factor = SOFTMAX_SCALE * LOG2E
    bias = jnp.where(lax.broadcasted_iota(jnp.int32, (1, total), 1) < length, 0.0, MASKED)
    kept = lax.broadcasted_iota(jnp.int32, (rows, rows), 1) <= lax.broadcasted_iota(
        jnp.int32, (rows, rows), 0
    )

    def exchange(h, mask):
        lane = pl.ds(pl.multiple_of(h * HDIM, HDIM), HDIM)
        return sender.copy(
            attended.at[mask, :, lane],
            joined.at[mask, :, lane],
            (swap_sems.at[0, h, mask], swap_sems.at[1, h, mask]),
            mask,
        )

    def one_head(h, carry):
        load_head(count, rows, h, xs, q_stat, cosine, sine, q, k, v)
        lane = pl.ds(pl.multiple_of(h * HDIM, HDIM), HDIM)
        for a in range(count):
            at = pl.ds(a * rows, rows)
            query = q[at]
            inner = nt(query, k[at]) * factor + bias[:, a * rows : (a + 1) * rows]
            inner = jnp.where(kept, inner, MASKED)
            highest = jnp.max(inner, axis=1, keepdims=True)
            if a:
                earlier = pl.ds(0, a * rows)
                outer = nt(query, k[earlier]) * factor + bias[:, : a * rows]
                highest = jnp.maximum(highest, jnp.max(outer, axis=1, keepdims=True))
            inner = jnp.exp2(inner - highest)
            sums = jnp.sum(inner, axis=1, keepdims=True)
            result = nn(inner.astype(BF16), v[at])
            if a:
                outer = jnp.exp2(outer - highest)
                sums = sums + jnp.sum(outer, axis=1, keepdims=True)
                result = result + nn(outer.astype(BF16), v[earlier])
            attended[a ^ me, :, lane] = (result * (1.0 / sums)).astype(BF16)
            column = jnp.broadcast_to(highest + jnp.log2(sums), (rows, HDIM))
            logsum[h, :, at] = jnp.transpose(column)[:1]
        for mask in others:
            exchange(h, mask).start()
        return carry

    lax.fori_loop(0, heads, one_head, 0)
    joined[0] = attended[0]
    outs = [move(attended, attended_out)]
    if shared:
        line_arrivals(lambda copy: copy.wait_recv())
        far(lambda copy: copy.start())
        whole.wait()
        near(lambda copy: copy.wait(), lambda copy: copy.wait_recv())
        far(lambda copy: copy.wait_recv())
    else:
        whole.wait()
    arrive([whole_pair])
    keeps = start_all(
        [(wv.at[mask % 2, mask // 2], w_all.at[mask]) for mask in range(count)], w_sems
    )
    for h in range(heads):
        arrive([exchange(h, mask) for mask in others])
    arrive(stages[1])
    start(stages[2])
    outs.append(move(joined, joined_out))
    tokens_load.wait()

    low = jnp.zeros((rows, ob.shape[0]), F32)
    for mask in range(count):
        low = low + nt(joined[mask], at_all[mask].astype(BF16))
    low = low.astype(BF16)
    lowrank[...] = low

    def columns(step, squares):
        d = pl.ds(pl.multiple_of(step * TILE, TILE), TILE)
        result = nn(low, (2.0 * ob[:, d]).astype(BF16))
        for mask in range(count):
            result = result + nn(joined[mask], wv[mask % 2, mask // 2, :, d])
        before[:, d] = result.astype(BF16)
        result = tokens[:, d].astype(F32) + result * (o_mag[:, d] / r_stat[0, 0:1, d])
        hidden[:, d] = result
        return squares + jnp.sum(result * result, axis=1, keepdims=True)

    squares = lax.fori_loop(0, features // TILE, columns, jnp.zeros((rows, 1), F32))
    scale = lax.rsqrt(squares * (1.0 / features) + NORM_EPS)
    outs += [move(hidden, hidden_out), move(before, before_out)]
    normed[...] = (hidden[...] * scale * gain[...]).astype(BF16)
    outs.append(move(normed, normed_out))
    for copy in keeps + outs:
        copy.wait()
    arrive(stages[2])
    leave(stages[1] + stages[2] + [whole_pair])
    for h in range(heads):
        leave([exchange(h, mask) for mask in others])
    if shared:
        line_sends(lambda copy: copy.wait_send())
        near(None, lambda copy: copy.wait_send())
        far(lambda copy: copy.wait_send())


def attend_forward(lengths, q_stat, cosine, sine, blocks, wq, at_all, ob, o_mag, r_stat, tokens, gain, grads):
    count, rows, width = blocks.shape
    depth = lax.axis_size("dp")
    head_width = width // 3
    heads = head_width // HDIM
    total = count * rows
    features = ob.shape[1]
    slots = count // 2
    return call(
        functools.partial(attend_forward_body, count, depth),
        "attend_forward",
        (
            shape((count, rows, head_width), BF16),
            shape((heads, 1, total), F32),
            shape((count, rows, head_width), BF16),
            shape((count, head_width, features), BF16),
            shape((rows, features), F32),
            shape((rows, features), BF16),
            shape((rows, features), BF16),
            shape((rows, ob.shape[0]), BF16),
            shape((3, rows, features), BF16),
        ),
        [SMEM, VMEM, ANY, ANY, ANY, ANY] + [VMEM] * 4 + [ANY, VMEM, ANY],
        (ANY, VMEM, ANY, ANY, ANY, ANY, ANY, VMEM, ANY),
        [pltpu.VMEM((total, width), BF16)]
        + [pltpu.VMEM((total, HDIM), BF16)] * 3
        + [
            pltpu.VMEM((2, slots, head_width, features), BF16),
            pltpu.VMEM((total, HDIM), F32),
            pltpu.VMEM((total, HDIM), F32),
            pltpu.VMEM((rows, features), BF16),
            pltpu.VMEM((count, rows, head_width), BF16),
            pltpu.VMEM((count, rows, head_width), BF16),
            pltpu.VMEM((rows, features), F32),
            pltpu.VMEM((rows, features), BF16),
            pltpu.VMEM((rows, features), BF16),
            DMA((8,)),
            DMA((count,)),
            DMA((depth + 1,)),
            DMA((2, 2)),
            DMA((2, depth + 1)),
            DMA((2, heads, count)),
            DMA((1,)),
            DMA((2, 3, 2)),
            DMA((count,)),
        ],
        4 * heads * total * total * HDIM + 2 * rows * features * features,
        2 * total * width * 2,
        (lengths, q_stat, cosine, sine, blocks, wq, at_all, ob, o_mag, r_stat, tokens, gain, grads),
        2,
    )


def ffn_body(
    count, own, c_own, c_some, gu_own, gu_par, d_own, d_par,
    ga, gb, gmag, da, db, g_stat, r_stat, d_mag,
    down_all, dx_sum, g_first, side, g_down_second,
    u, c, wgu, wd, grad_low, sw, bg, down, parts, landed, second, second_par, da_par, scale_par, scale_own, d_second,
    g_second, g_down_first, drift, second_landed, first_landed, drift_landed,
    sems, down_sems, gather_sems, c_sems, reduce_sems, pair_sems,
):
    sender = Sender()
    slots = count // 2
    rows, features = own.shape
    units = d_own.shape[0]
    rank = da.shape[0]
    sender.meet([1] + list(range(2, count, 2)))
    stages = gather_stages(sender, count, own, u, gather_sems)
    c_stages = gather_stages(sender, count, c_own, c, c_sems, 3)
    sums = reduce_stages(sender, count, parts, landed, reduce_sems)
    start(stages[1])
    scale_own[...] = g_stat[:, 1]
    pairs = [
        sender.copy(source, target, (pair_sems.at[0, at], pair_sems.at[1, at]), 1)
        for at, (source, target) in enumerate(((gb, second_par), (da, da_par), (scale_own, scale_par)))
    ]
    start(pairs)
    local = start_all(
        [(own, u.at[0]), (c_own, c.at[0])]
        + [(gu_own, wgu.at[0]), (d_own, wd.at[0]), (gu_par, wgu.at[1]), (d_par, wd.at[1])]
        + [(c_some.at[slot], c.at[slot]) for slot in (1, 2)],
        sems,
    )
    if count != 8:
        for slot in range(2, slots):
            start(stages[slot])
        for slot in range(3, slots):
            start(c_stages[slot])
    first_t = ga[...].reshape(2 * rank, features).astype(BF16)
    d_scale = d_mag[...] / r_stat[1, 0:1]
    d_second[...] = (2.0 * db[...]).astype(BF16)
    second[...] = jnp.zeros_like(second)
    for part in range(2):
        second[0, part, pl.ds(part * rank, rank), :] = (2.0 * gb[part]).astype(BF16)
    arrive(pairs)
    for part in range(2):
        second[1, part, pl.ds(part * rank, rank), :] = (2.0 * second_par[part]).astype(BF16)
    da_low = (da[...].astype(BF16), da_par[...].astype(BF16))
    for ref in (g_first, g_second, g_down_first, g_down_second, drift):
        ref[...] = jnp.zeros_like(ref)
    local[0].wait()
    local[1].wait()
    rooms = down.shape[0]

    def store(slot):
        return pltpu.make_async_copy(down.at[slot % rooms], down_all.at[slot], down_sems.at[slot])

    def one_slot(slot, carry):
        room = lax.rem(slot, rooms)
        if slots > rooms:

            @pl.when(slot >= rooms)
            def _():
                store(slot - rooms).wait()

        for at in range(1, slots):

            @pl.when(slot == at)
            def _():
                if at in (1, 2):
                    local[5 + at].wait()
                else:
                    arrive(c_stages[at])
                if count == 8 and at == 3:
                    start(sums[2])
                    start(sums[1])

        lowrank = nt(u[slot], first_t).astype(BF16)
        lowrank_t = nt(first_t, u[slot]).astype(BF16)
        grad_low[...] = (c[slot].astype(F32) * d_scale).astype(BF16)
        d_low_grad = nt(grad_low[...], d_second[...]).astype(BF16)
        d_low_grad_t = nt(d_second[...], grad_low[...]).astype(BF16)
        d_low = jnp.zeros((rows, rank), F32)
        d_low_t = jnp.zeros((rank, rows), F32)
        u_low = jnp.zeros((rows, 2 * rank), F32)
        u_low_t = jnp.zeros((2 * rank, rows), F32)
        for which, scale in enumerate((scale_own, scale_par)):

            @pl.when(slot == 0)
            def _():
                local[2 + 2 * which].wait()
                local[3 + 2 * which].wait()

            for at in range(1, slots) if which else ():

                @pl.when(slot == at - 1)
                def _():
                    arrive(stages[at])
                    if count == 8 and at + 1 < slots:
                        start(stages[at + 1])
                    if count == 8 and at == 2:
                        start(c_stages[3])

            for begin, span in tiles(units):
                f = pl.ds(begin, span)
                gate_before = nt(u[slot], wgu[which, 0, f, :]) + nn(lowrank, second[which, 0, :, f])
                up_before = nt(u[slot], wgu[which, 1, f, :]) + nn(lowrank, second[which, 1, :, f])
                gate = gate_before * scale[0:1, f]
                up = up_before * scale[1:2, f]
                sigmoid = 1.0 / (1.0 + jnp.exp(-gate))
                silu = gate * sigmoid
                swiglu = (silu * up).astype(BF16)
                swiglu_grad = nt(grad_low[...], wd[which, f, :]) + nn(
                    d_low_grad, da_low[which][:, begin : begin + span]
                )
                swiglu_grad = swiglu_grad.astype(BF16).astype(F32)
                gate_grad = swiglu_grad * up * (sigmoid * (1.0 + gate * (1.0 - sigmoid)))
                up_grad = swiglu_grad * silu
                drift[which, 0:1, f] += jnp.sum(gate_grad * gate_before, axis=0, keepdims=True)
                drift[which, 1:2, f] += jnp.sum(up_grad * up_before, axis=0, keepdims=True)
                sw[which, :, f] = swiglu
                bg[which, 0, :, f] = (gate_grad * scale[0:1, f]).astype(BF16)
                bg[which, 1, :, f] = (up_grad * scale[1:2, f]).astype(BF16)
            d_low = d_low + nt(sw[which], da_low[which])
            d_low_t = d_low_t + nt(da_low[which], sw[which])
            for part in range(2):
                u_low = u_low + nt(bg[which, part], second[which, part])
                u_low_t = u_low_t + nt(second[which, part], bg[which, part])
                g_second[which, part] += 2.0 * nn(
                    lowrank_t[part * rank : (part + 1) * rank], bg[which, part]
                )
            g_down_first[which] += nn(d_low_grad_t, sw[which])
        d_low = d_low.astype(BF16)
        d_low_t = d_low_t.astype(BF16)
        u_low = u_low.astype(BF16)
        u_low_t = u_low_t.astype(BF16)

        for begin in range(0, features, TILE):
            d = pl.ds(begin, TILE)
            dx = nn(u_low, first_t[:, begin : begin + TILE])
            for which in range(2):
                for part in range(2):
                    dx = dx + nn(bg[which, part], wgu[which, part, :, d])
            parts[slot, :, d] = dx.astype(BF16)
            g_first[:, d] += nn(u_low_t, u[slot, :, d])
            total = nn(sw[0], wd[0, :, d]) + nn(sw[1], wd[1, :, d]) + nn(d_low, d_second[:, d])
            down[room, :, d] = total.astype(BF16)
            g_down_second[:, d] += 2.0 * nn(d_low_t, grad_low[:, d])

        store(slot).start()
        if count != 8:
            for at in range(1, slots):

                @pl.when(slot == at)
                def _():
                    start(sums[at])

        return carry

    lax.fori_loop(0, slots, one_slot, 0)

    gives = [
        sender.copy(source, target, (pair_sems.at[0, at], pair_sems.at[1, at]), 1)
        for at, source, target in (
            (3, g_second.at[1], second_landed),
            (4, g_down_first.at[1], first_landed),
            (5, drift.at[1], drift_landed),
        )
    ]
    start(gives)
    if count == 8:
        relay(parts.at[3], landed, sums)
    arrive(gives)
    total_drift = drift[0] + drift_landed[...]
    side[...] = jnp.zeros_like(side)
    side[2 * rank : 3 * rank] = g_down_first[0] + first_landed[...]
    for part in range(2):
        norm = g_stat[part, 0:1]
        one = total_drift[part : part + 1]
        factor = -one * gmag[part : part + 1] / (norm * norm * norm)
        at = pl.ds(part * rank, rank)
        side[at] = g_second[0, part] + second_landed[part] + 2.0 * g_stat[part, 8 : 8 + rank] * factor
        side[3 * rank + part : 3 * rank + part + 1] = one / norm
        factored = gb[part] * factor
        wide = nn(jnp.concatenate(split(factored), axis=0), wgu[0, part])
        gram = nt(factored, gb[part], EXACT)
        g_first[at] += 2.0 * (wide[:rank] + wide[rank:] + 2.0 * nn(gram, ga[part], EXACT))

    def out(d, value, carry):
        dx_sum[:, d] = value.astype(BF16)
        return carry

    lax.fori_loop(0, features // TILE, finish_reduce(count, parts.at[0], landed, sums, out), 0)
    for slot in range(max(0, slots - rooms), slots):
        store(slot).wait()
    leave(pairs + gives)
    for copies in (sums, stages, c_stages):
        leave_stages(copies)


def ffn(own, c_own, c_some, gu_own, gu_par, d_own, d_par, small):
    rows, features = own.shape
    count = lax.axis_size("tensor")
    slots = count // 2
    units = d_own.shape[0]
    rank = small[3].shape[0]
    many = pltpu.VMEM((slots, rows, features), BF16)
    return call(
        functools.partial(ffn_body, count),
        "ffn",
        (
            shape((slots, rows, features), BF16),
            shape((rows, features), BF16),
            shape((2 * rank, features), F32),
            shape((4 * rank, units), F32),
            shape((rank, features), F32),
        ),
        [ANY] * 7 + [VMEM] * len(small),
        (ANY,) + (VMEM,) * 4,
        [
            many,
            many,
            pltpu.VMEM((2, 2, units, features), BF16),
            pltpu.VMEM((2, units, features), BF16),
            pltpu.VMEM((rows, features), BF16),
            pltpu.VMEM((2, rows, units), BF16),
            pltpu.VMEM((2, 2, rows, units), BF16),
            pltpu.VMEM((min(slots, 4), rows, features), BF16),
            many,
            many,
            pltpu.VMEM((2, 2, 2 * rank, units), BF16),
            pltpu.VMEM((2, rank, units), F32),
            pltpu.VMEM((rank, units), F32),
            pltpu.VMEM((2, units), F32),
            pltpu.VMEM((2, units), F32),
            pltpu.VMEM((rank, features), BF16),
            pltpu.VMEM((2, 2, rank, units), F32),
            pltpu.VMEM((2, rank, units), F32),
            pltpu.VMEM((2, 2, units), F32),
            pltpu.VMEM((2, rank, units), F32),
            pltpu.VMEM((rank, units), F32),
            pltpu.VMEM((2, units), F32),
            DMA((8,)),
            DMA((slots,)),
            DMA((2, slots, 2)),
            DMA((2, slots, 2)),
            DMA((2, slots, 2)),
            DMA((2, 6)),
        ],
        24 * slots * rows * features * units,
        12 * features * units,
        (own, c_own, c_some, gu_own, gu_par, d_own, d_par, *small),
        3,
    )


def attend_backward_body(
    count, depth, lengths, q_stat, cosine_in, sine_in, blocks, attended_in, logsum, joined_in, w_all, at_all, ob, o_mag,
    r_stat, hidden_in, before_in, lowrank, cot_in, dx_in, gain, d_mag, down_all, gu_first, d_second, side,
    out_all, drift, hidden_grad_out, result_out, d_drift, gu_total, upper, o_mag_grad, d_sums, o_total, side_total,
    xs, dos, q, k, v, dq, centre, wv, og, ag, parts, landed, side_line,
    cosine, sine, attended, joined, hidden, before, cot, dx_sum, out, hidden_grad, result,
    pay, along_in, part, group_in, block, span_sum, main, total_sems,
    move_sems, sems, w_sems, part_sems, swap_sems, reduce_sems, side_sems,
):
    sender = Sender()
    me = sender.me
    length = lengths[0]
    _, rows, width = blocks.shape
    heads = width // (3 * HDIM)
    total = rows * count
    features = ob.shape[1]
    rank = ob.shape[0]
    slots = count // 2
    others = list(range(1, count))
    flips = list(range(1, depth))
    order = others + [0]
    move = Mover(move_sems)
    early = [move(hidden_in, hidden), move(dx_in, dx_sum), move(cot_in, cot), move(before_in, before)]
    loads = dict(
        zip(order, start_all([(w_all.at[mask], wv.at[mask]) for mask in order], w_sems))
    )
    joined_load = move(joined_in, joined)
    late = [move(cosine_in, cosine), move(sine_in, sine), move(attended_in, attended)]
    sender.meet(others, flips)
    sums = reduce_stages(sender, count, down_all, landed, reduce_sems, end=3)
    if count == 8:
        sums.update(reduce_stages(sender, count, parts, landed, reduce_sems, 1, 3))
        start(sums[2])
    else:
        for slot in range(1, slots):
            start(sums[slot])
    copies = start_all(
        [
            (blocks.at[mask], xs.at[pl.ds(pl.multiple_of((me ^ mask) * rows, rows), rows)])
            for mask in range(count)
        ],
        sems,
    )
    kept_parts = (0, 3) if count == 8 else (0,)
    part_loads = start_all(
        [(down_all.at[slot], parts.at[at]) for at, slot in enumerate(kept_parts)], part_sems
    )

    for copy in early[:2]:
        copy.wait()
    scale, back = norm_statistics(
        lambda d: hidden[:, d], lambda d: dx_sum[:, d].astype(F32) * gain[:, d], features, rows
    )

    for copy in early[2:]:
        copy.wait()

    def rows_grad(step, carry):
        d = pl.ds(pl.multiple_of(step * TILE, TILE), TILE)
        grad = cot[:, d].astype(F32) + scale * (dx_sum[:, d].astype(F32) * gain[:, d]) - hidden[:, d] * back
        hidden_grad[:, d] = grad
        upper[0:1, d] = jnp.sum(grad * before[:, d].astype(F32), axis=0, keepdims=True)
        og[:, d] = (grad * (o_mag[:, d] / r_stat[0, 0:1, d])).astype(BF16)
        return carry

    lax.fori_loop(0, features // TILE, rows_grad, 0)
    outs = [move(hidden_grad, hidden_grad_out)]
    o_drift = upper[0:1]
    second = (2.0 * ob[...]).astype(BF16)
    low_grad = nt(og[...], second).astype(BF16)
    mine = pl.ds(pl.multiple_of(me * rows, rows), rows)

    def exchange(h, mask, at=None):
        lane = pl.ds(pl.multiple_of(h * HDIM, HDIM), HDIM)
        return sender.copy(
            ag.at[mask, :, lane],
            dos.at[mine if at is None else at, lane],
            (swap_sems.at[0, h, mask], swap_sems.at[1, h, mask]),
            mask,
        )

    def landing(h, mask):
        return exchange(h, mask, pl.ds(pl.multiple_of((me ^ mask) * rows, rows), rows))

    for mask in order:
        loads[mask].wait()
        grad = nt(og[...], wv[mask]) + nn(low_grad, at_all[mask].astype(BF16))
        if mask:
            ag[mask] = grad.astype(BF16)
            exchange(0, mask).start()
        else:
            dos[mine] = grad.astype(BF16)
    for h in range(1, heads):
        for mask in others:
            exchange(h, mask).start()

    low_grad_t = nt(second, og[...]).astype(BF16)
    norm = r_stat[0, 0:1]
    factor = -o_drift * o_mag[...] / (norm * norm * norm)
    factored = ob[...] * factor
    wide = jnp.zeros((2 * rank, features), F32)
    gram = jnp.zeros((rank, rank), F32)
    joined_load.wait()
    for mask in range(count):
        first = at_all[mask]
        span = pl.ds(pl.multiple_of((me ^ mask) * (width // 3), width // 3), width // 3)
        pay[6 * rank : 7 * rank, span] = (
            nn(low_grad_t, joined[mask]) + 2.0 * second_direction(factored, ob[...], wv[mask], first)
        ).astype(BF16)
        wide = wide + nn(jnp.concatenate(split(first), axis=0), wv[mask])
        gram = gram + nt(first, first, EXACT)
    product = wide[:rank] + wide[rank:] + 2.0 * nn(gram, ob[...], EXACT)
    pay[0 : 2 * rank] = gu_first[...].astype(BF16)
    pay[2 * rank : 3 * rank] = d_second[...].astype(BF16)
    pay[3 * rank : 4 * rank] = r_stat[1, 8 : 8 + rank].astype(BF16)
    pay[4 * rank : 5 * rank] = (
        2.0 * tn(lowrank[...], og[...]) + 2.0 * product * factor
    ).astype(BF16)
    pay[5 * rank : 6 * rank] = jnp.broadcast_to(o_drift, (rank, features)).astype(BF16)
    pay[7 * rank :] = jnp.zeros_like(pay[7 * rank :])
    totals = Totals(
        sender, count, depth, pay, along_in, part, group_in, block, span_sum, main, total_sems
    )
    totals.give()
    side_line[0] = side[...].astype(BF16)
    sides = [
        sender.copy(
            side_line.at[0], side_line.at[flip], (side_sems.at[0, flip], side_sems.at[1, flip]), 0, flip
        )
        for flip in flips
    ]
    start(sides)
    for load in part_loads:
        load.wait()
    if count == 8:
        relay(parts.at[1], landed, sums)
    for copy in copies + late:
        copy.wait()

    short = total <= 2048
    factor2 = SOFTMAX_SCALE * LOG2E
    kept = lax.broadcasted_iota(jnp.int32, (rows, rows), 0) <= lax.broadcasted_iota(
        jnp.int32, (rows, rows), 1
    )

    def one_head(h, carry):
        load_head(count, rows, h, xs, q_stat, cosine, sine, q, k, v)
        for mask in others:
            landing(h, mask).wait_recv()
        own = pl.ds(pl.multiple_of(h * HDIM, HDIM), HDIM)

        def lanes(part):
            return pl.ds(pl.multiple_of((part * heads + h) * HDIM, HDIM), HDIM)

        for a in range(count):
            at = pl.ds(a * rows, rows)
            values = dos[at, own].astype(F32) * attended[a ^ me, :, own].astype(F32)
            column = jnp.sum(values, axis=1, keepdims=True)
            centre[:, at] = jnp.transpose(jnp.broadcast_to(column, (rows, HDIM)))[:8]

        def finish(a, part, grad):
            at = pl.ds(a * rows if isinstance(a, int) else pl.multiple_of(a * rows, rows), rows)
            if part < 2:
                grad = turn(grad, cosine[at], -sine[at])
            out[a ^ me, :, lanes(part)] = (grad * q_stat[part, 1:2, own]).astype(BF16)
            return jnp.sum(grad * xs[at, lanes(part)].astype(F32), axis=0, keepdims=True)

        def pair_grads(at, after, bias, keep):
            key = k[at]
            weights = jnp.exp2(nt(key, q[after]) * factor2 + (bias - logsum[h, :, after]))
            weights = keep(weights)
            score_grad = weights * (nt(v[at], dos[after, own]) - centre[:1, after])
            score_grad = score_grad.astype(BF16)
            value_grad = nn(weights.astype(BF16), dos[after, own])
            return nn(score_grad, q[after]), value_grad, tn(score_grad, key)

        zero = jnp.zeros((1, HDIM), F32)
        iota = lax.broadcasted_iota(jnp.int32, (rows, 1), 0)
        if short:
            key_drift, value_drift = zero, zero
            for a in range(count):
                bias = jnp.where(a * rows + iota < length, 0.0, MASKED)

                def keep(weights):
                    first = jnp.where(kept, weights[:, :rows], 0.0)
                    if a == count - 1:
                        return first
                    return jnp.concatenate([first, weights[:, rows:]], axis=1)

                at, after = pl.ds(a * rows, rows), pl.ds(a * rows, total - a * rows)
                key_grad, value_grad, query_part = pair_grads(at, after, bias, keep)
                if a == 0:
                    dq[...] = query_part
                else:
                    dq[after] += query_part
                key_drift = key_drift + finish(a, 1, key_grad * SOFTMAX_SCALE)
                value_drift = value_drift + finish(a, 2, value_grad)
        else:
            dq[...] = jnp.zeros_like(dq)

            def one_block(a, drifts):
                start_at = pl.multiple_of(a * rows, rows)
                at = pl.ds(start_at, rows)
                bias = jnp.where(start_at + iota < length, 0.0, MASKED)

                def one_pair(i, grads):
                    after = pl.ds(pl.multiple_of(i * rows, rows), rows)
                    ahead = (i - a) * rows

                    def keep(weights):
                        return jnp.where(kept | (ahead > 0), weights, 0.0)

                    key_part, value_part, query_part = pair_grads(at, after, bias, keep)
                    dq[after] += query_part
                    return grads[0] + key_part, grads[1] + value_part

                none = jnp.zeros((rows, HDIM), F32)
                key_grad, value_grad = lax.fori_loop(a, count, one_pair, (none, none))
                return (
                    drifts[0] + finish(a, 1, key_grad * SOFTMAX_SCALE),
                    drifts[1] + finish(a, 2, value_grad),
                )

            key_drift, value_drift = lax.fori_loop(0, count, one_block, (zero, zero))
        query_drift = zero
        for a in range(count):
            query_drift = query_drift + finish(a, 0, dq[pl.ds(a * rows, rows)] * SOFTMAX_SCALE)
        drift[0, :, own] = query_drift
        drift[1, :, own] = key_drift
        drift[2, :, own] = value_drift

        @pl.when(h == 0)
        def _():
            totals.add_along()

        return carry

    lax.fori_loop(0, heads, one_head, 0)
    outs.append(move(out, out_all))
    totals.add_group()
    if count == 8:
        start(sums[1])
    arrive(sides)
    side_total[...] = along_total(sender, depth, side_line)
    totals.share()

    def rows_out(d, value, carry):
        result[:, d] = (hidden[:, d] + value * (d_mag[:, d] / r_stat[1, 0:1, d])).astype(BF16)
        d_drift[:, d] = jnp.sum(cot[:, d].astype(F32) * value, axis=0, keepdims=True)
        return carry

    lax.fori_loop(0, features // TILE, finish_reduce(count, parts.at[0], landed, sums, rows_out), 0)
    outs.append(move(result, result_out))
    totals.take()
    o_total[...] = main[
        6 * rank : 7 * rank, pl.ds(pl.multiple_of(me * (width // 3), width // 3), width // 3)
    ].astype(F32)
    gu_total[...] = main[0 : 2 * rank].astype(F32)
    d_sums[...] = main[2 * rank : 4 * rank].astype(F32)
    upper[...] = main[4 * rank : 5 * rank].astype(F32)
    o_mag_grad[...] = main[5 * rank : 6 * rank].astype(F32)[:1] / norm
    totals.end()
    for copy in outs:
        copy.wait()
    leave(sides)
    leave_stages(sums)
    for h in range(heads):
        for mask in others:
            exchange(h, mask).wait_send()


def attend_backward(blocks, features, rank, units, operands):
    count, rows, width = blocks.shape
    depth = lax.axis_size("dp")
    head_width = width // 3
    heads = head_width // HDIM
    total = count * rows
    slots = count // 2
    many = pltpu.VMEM((slots, rows, features), BF16)
    return call(
        functools.partial(attend_backward_body, count, depth),
        "attend_backward",
        (
            shape((count, rows, width), BF16),
            shape((3, 1, head_width), F32),
            shape((rows, features), F32),
            shape((rows, features), BF16),
            shape((1, features), F32),
            shape((2 * rank, features), F32),
            shape((rank, features), F32),
            shape((1, features), F32),
            shape((2 * rank, features), F32),
            shape((rank, head_width), F32),
            shape((4 * rank, units), F32),
        ),
        [SMEM, VMEM, ANY, ANY, ANY, ANY, VMEM, ANY, ANY] + [VMEM] * 4
        + [ANY, ANY, VMEM, ANY, ANY, VMEM, VMEM, ANY] + [VMEM] * 3,
        (ANY, VMEM, ANY, ANY) + (VMEM,) * 7,
        [pltpu.VMEM((total, width), BF16), pltpu.VMEM((total, head_width), BF16)]
        + [pltpu.VMEM((total, HDIM), BF16)] * 3
        + [
            pltpu.VMEM((total, HDIM), F32),
            pltpu.VMEM((8, total), F32),
            pltpu.VMEM((count, head_width, features), BF16),
            pltpu.VMEM((rows, features), BF16),
            pltpu.VMEM((count, rows, head_width), BF16),
            pltpu.VMEM((2 if count == 8 else 1, rows, features), BF16),
            many,
            pltpu.VMEM((depth, 4 * rank, units), BF16),
            pltpu.VMEM((total, HDIM), F32),
            pltpu.VMEM((total, HDIM), F32),
            pltpu.VMEM((count, rows, head_width), BF16),
            pltpu.VMEM((count, rows, head_width), BF16),
            pltpu.VMEM((rows, features), F32),
            pltpu.VMEM((rows, features), BF16),
            pltpu.VMEM((rows, features), BF16),
            pltpu.VMEM((rows, features), BF16),
            pltpu.VMEM((count, rows, width), BF16),
            pltpu.VMEM((rows, features), F32),
            pltpu.VMEM((rows, features), BF16),
        ]
        + totals_scratch(8 * rank, features, count, depth)
        + [
            DMA((11,)),
            DMA((count,)),
            DMA((count,)),
            DMA((2,)),
            DMA((2, heads, count)),
            DMA((2, slots, 2)),
            DMA((2, depth)),
        ],
        10 * heads * total * total * HDIM + 2 * rows * features * features,
        2 * total * width * 4,
        operands,
        4,
    )


def qkv_backward_body(
    count, depth, grads, u_all, w_own, w_par, d_own, qa, qb, qmag, q_stat, drift, r_stat, da, db, d_mag,
    d_sums, d_drift, side_total, tokens_in, gain, hidden_grad_in,
    tokens_grad_out, first_grad, own_total, upper, lower, d_mag_grad,
    u, w, wd, b_own, b_par, parts, landed, second_own, second_par, qb_par, g_first, g_own, g_par, g_landed, own_line,
    lows, dx_sum, tokens, hidden_grad, tokens_grad,
    pay, along_in, part, group_in, block, span_sum, main, total_sems,
    move_sems, sems, u_sems, own_sems, par_sems, reduce_sems, small_sems, line_sems,
):
    sender = Sender()
    slots = slots_of(count)
    order = [2, 1, 3, 0] if count == 8 else list(range(len(slots) - 1, -1, -1))
    maps, features, width = w_own.shape
    rank = qb.shape[1]
    rows = grads.shape[1]
    half = rows // 2
    others = list(range(1, count))
    flips = list(range(1, depth))
    move = Mover(move_sems)
    loads = {slot: pltpu.make_async_copy(u_all.at[slot], u.at[slot], u_sems.at[slot]) for slot in order}
    loads[order[0]].start()
    local = start_all([(w_own, w.at[pl.ds(0, maps)]), (w_par, w.at[pl.ds(maps, maps)]), (d_own, wd)], sems)
    for slot in order[1:]:
        loads[slot].start()
    late = [move(tokens_in, tokens), move(hidden_grad_in, hidden_grad)]
    sender.meet(others, flips)
    sums = reduce_stages(sender, count, parts, landed, reduce_sems)
    small = sender.copy(qb, qb_par, (small_sems.at[0, 0], small_sems.at[1, 0]), 1)
    small.start()
    keeps, sends = {}, {}
    for slot in order:
        for h, mask in enumerate(slots[slot]):
            at = pl.ds(h * half, half)
            send = sender.copy(
                grads.at[mask ^ 1, at],
                b_par.at[slot, at],
                (par_sems.at[0, slot, h], par_sems.at[1, slot, h]),
                1,
            )
            keep = pltpu.make_async_copy(
                grads.at[mask, at], b_own.at[slot, at], own_sems.at[slot, h]
            )
            send.start()
            keep.start()
            sends.setdefault(slot, []).append(send)
            keeps.setdefault(slot, []).append(keep)
    first_t = qa[...].reshape(maps * rank, features).astype(BF16)
    second_own[...] = jnp.zeros_like(second_own)
    second_par[...] = jnp.zeros_like(second_par)
    small.wait_recv()
    for s in range(maps):
        at, lanes = pl.ds(s * rank, rank), pl.ds(s * width, width)
        second_own[at, lanes] = (2.0 * qb[s]).astype(BF16)
        second_par[at, lanes] = (2.0 * qb_par[s]).astype(BF16)

    def low_rank(slot, first):
        for keep in keeps[slot]:
            keep.wait()
        arrive(sends[slot])
        loads[slot].wait()
        own, par = b_own.at[slot], b_par.at[slot]
        lows[slot] = (nt(own[...], second_own[...]) + nt(par[...], second_par[...])).astype(BF16)
        low_t = (nt(second_own[...], own[...]) + nt(second_par[...], par[...])).astype(BF16)
        lowrank_t = nt(first_t, u[slot]).astype(BF16)
        for s in range(maps):
            lanes = pl.ds(s * width, width)
            piece = lowrank_t[s * rank : (s + 1) * rank]
            own_part, par_part = 2.0 * nn(piece, own[:, lanes]), 2.0 * nn(piece, par[:, lanes])
            if first:
                g_own[s], g_par[s] = own_part, par_part
            else:
                g_own[s] += own_part
                g_par[s] += par_part
        part = nn(low_t, u[slot])
        if first:
            g_first[...] = part
        else:
            g_first[...] += part

    def input_grad(slot):
        own, par = b_own.at[slot], b_par.at[slot]
        for begin in range(0, features, TILE):
            d = pl.ds(begin, TILE)
            dx = nn(lows[slot], first_t[:, begin : begin + TILE])
            for s in range(maps):
                lanes = pl.ds(s * width, width)
                dx = dx + nt(own[:, lanes], w[s, d, :]) + nt(par[:, lanes], w[maps + s, d, :])
            parts[slot, :, d] = dx.astype(BF16)
        if slot and (count != 8 or slot == 2):
            start(sums[slot])

    low_rank(order[0], True)
    local[0].wait()
    local[1].wait()
    input_grad(order[0])
    for slot in order[1:]:
        low_rank(slot, False)

    give = sender.copy(g_par, g_landed, (small_sems.at[0, 1], small_sems.at[1, 1]), 1)
    give.start()
    factors = []
    for s in range(maps):
        norm = q_stat[s, 0:1]
        factor = -drift[s] * qmag[s : s + 1] / (norm * norm * norm)
        factors.append(factor)
        pay[s * rank : (s + 1) * rank] = (
            g_first[s * rank : (s + 1) * rank]
            + 2.0 * second_direction(qb[s] * factor, qb[s], w[s], qa[s])
        ).astype(BF16)
    at = maps * rank
    pay[at : at + rank] = jnp.broadcast_to(d_drift[...], (rank, features)).astype(BF16)
    if at + rank < pay.shape[0]:
        pay[at + rank :] = jnp.zeros_like(pay[at + rank :])
    totals = Totals(
        sender, count, depth, pay, along_in, part, group_in, block, span_sum, main, total_sems
    )
    totals.give()
    if len(order) > 2:
        input_grad(order[1])
    give.wait_recv()
    for s in range(maps):
        own_line[0, s * rank : (s + 1) * rank] = (
            g_own[s] + g_landed[s] + 2.0 * q_stat[s, 8 : 8 + rank] * factors[s]
        ).astype(BF16)
    magnitudes = [drift[s] / q_stat[s, 0:1] for s in range(maps)]
    magnitudes = jnp.concatenate(magnitudes + [jnp.zeros((rank - maps, width), F32)], axis=0)
    own_line[0, maps * rank :] = magnitudes.astype(BF16)
    along = [
        sender.copy(
            own_line.at[0], own_line.at[flip], (line_sems.at[0, flip], line_sems.at[1, flip]), 0, flip
        )
        for flip in flips
    ]
    start(along)
    for slot in order[2:]:
        input_grad(slot)
    totals.add_along()
    if count == 8:
        relay(parts.at[3], landed, sums)
    totals.add_group()
    if count == 8:
        start(sums[1])
    arrive(along)
    own_total[...] = along_total(sender, depth, own_line)
    totals.share()
    totals.take()
    first_grad[...] = main[0 : maps * rank].astype(F32)
    total_drift = main[maps * rank : (maps + 1) * rank].astype(F32)[:1]
    norm = r_stat[1, 0:1]
    factor = -total_drift * d_mag[...] / (norm * norm * norm)
    d_mag_grad[...] = total_drift / norm
    upper[...] = d_sums[0:rank] + (2.0 / depth) * d_sums[rank:] * factor
    local[2].wait()
    lower[...] = side_total[2 * rank : 3 * rank] + 2.0 * second_direction(
        db[...] * factor, db[...], wd[...], da[...]
    )

    def out(d, value, carry):
        dx_sum[:, d] = value
        return carry

    lax.fori_loop(0, features // TILE, finish_reduce(count, parts.at[0], landed, sums, out), 0)
    for copy in late:
        copy.wait()
    scale, back = norm_statistics(
        lambda d: tokens[:, d].astype(F32), lambda d: dx_sum[:, d] * gain[:, d], features, rows
    )

    def rows_grad(step, carry):
        d = pl.ds(pl.multiple_of(step * TILE, TILE), TILE)
        tokens_grad[:, d] = (
            hidden_grad[:, d] + scale * (dx_sum[:, d] * gain[:, d]) - tokens[:, d].astype(F32) * back
        )
        return carry

    lax.fori_loop(0, features // TILE, rows_grad, 0)
    last = move(tokens_grad, tokens_grad_out)
    totals.end()
    last.wait()
    leave(along + [small, give])
    leave_stages(sums)
    leave_stages(sends)


def qkv_backward(grads, u_all, w_own, w_par, d_own, small):
    count, rows, _ = grads.shape
    depth = lax.axis_size("dp")
    slots = count // 2
    maps, features, width = w_own.shape
    qb = small[1]
    rank = qb.shape[1]
    ranks = maps * rank
    units = d_own.shape[0]
    many = pltpu.VMEM((slots, rows, features), BF16)
    return call(
        functools.partial(qkv_backward_body, count, depth),
        "qkv_backward",
        (
            shape((rows, features), F32),
            shape((ranks, features), F32),
            shape((ranks + rank, width), F32),
            shape((rank, features), F32),
            shape((rank, units), F32),
            shape((1, features), F32),
        ),
        [ANY] * 5 + [VMEM] * (len(small) - 3) + [ANY, VMEM, ANY],
        (ANY,) + (VMEM,) * 5,
        [
            many,
            pltpu.VMEM((2 * maps, features, width), BF16),
            pltpu.VMEM((units, features), BF16),
            pltpu.VMEM((slots, rows, maps * width), BF16),
            pltpu.VMEM((slots, rows, maps * width), BF16),
            many,
            many,
            pltpu.VMEM((ranks, maps * width), BF16),
            pltpu.VMEM((ranks, maps * width), BF16),
            pltpu.VMEM(qb.shape, F32),
            pltpu.VMEM((ranks, features), F32),
            pltpu.VMEM(qb.shape, F32),
            pltpu.VMEM(qb.shape, F32),
            pltpu.VMEM(qb.shape, F32),
            pltpu.VMEM((depth, ranks + rank, width), BF16),
            pltpu.VMEM((slots, rows, ranks), BF16),
            pltpu.VMEM((rows, features), F32),
            pltpu.VMEM((rows, features), BF16),
            pltpu.VMEM((rows, features), F32),
            pltpu.VMEM((rows, features), F32),
        ]
        + totals_scratch(ranks + rank, features, count, depth)
        + [
            DMA((3,)),
            DMA((3,)),
            DMA((slots,)),
            DMA((slots, 2)),
            DMA((2, slots, 2)),
            DMA((2, slots, 2)),
            DMA((2, 2)),
            DMA((2, depth)),
        ],
        4 * slots * rows * features * maps * width,
        8 * features * maps * width,
        (grads, u_all, w_own, w_par, d_own, *small),
        5,
    )


def results_body(
    maps, first, own, upper, o_mag, gu, side, o_first, d_upper, d_lower, d_mag,
    first_out, second_out, mag_out, o_first_out, upper_out, o_mag_out, gu_first_out, gu_second_out, gu_mag_out,
    d_lower_out, d_upper_out, d_mag_out,
):
    rank = upper.shape[0]
    for s in range(maps):
        at = pl.ds(s * rank, rank)
        first_out[s] = first[at]
        second_out[s] = own[at]
    for s in range(2):
        at = pl.ds(s * rank, rank)
        gu_first_out[s] = gu[at]
        gu_second_out[s] = side[at]
    mag_out[...] = own[maps * rank : maps * rank + maps]
    gu_mag_out[...] = side[3 * rank : 3 * rank + 2]
    o_first_out[...] = o_first[...]
    upper_out[...] = upper[...]
    o_mag_out[...] = o_mag[...]
    d_lower_out[...] = d_lower[...]
    d_upper_out[...] = d_upper[...]
    d_mag_out[...] = d_mag[...]


def results(maps, values):
    first, own, upper, o_mag, gu, side, o_first, d_upper, d_lower, d_mag = values
    rank, features = upper.shape
    units, width = side.shape[1], own.shape[1]
    return pl.pallas_call(
        functools.partial(results_body, maps),
        name="results",
        out_shape=(
            shape((maps, rank, features), F32),
            shape((maps, rank, width), F32),
            shape((maps, width), F32),
            shape(o_first.shape, F32),
            shape(upper.shape, F32),
            shape(o_mag.shape, F32),
            shape((2, rank, features), F32),
            shape((2, rank, units), F32),
            shape((2, units), F32),
            shape(d_lower.shape, F32),
            shape(d_upper.shape, F32),
            shape(d_mag.shape, F32),
        ),
        in_specs=[VMEM] * len(values),
        out_specs=(VMEM,) * 12,
    )(*values)


def rope_tables(total):
    half = HDIM // 2
    frequency = np.exp(-np.log(ROPE_THETA) * np.arange(half) / half)
    angles = np.arange(total)[:, None] * frequency[None, :]
    cosine, sine = np.cos(angles), np.sin(angles)
    return (
        jnp.asarray(np.concatenate([cosine, cosine], axis=1), F32),
        jnp.asarray(np.concatenate([-sine, sine], axis=1), F32),
    )


def body(
    tokens,
    attn_gain,
    ffn_gain,
    qkv_base,
    qkv_first,
    qkv_second,
    qkv_magnitude,
    output_frozen_weight,
    output_first,
    output_upper_map,
    output_magnitude,
    gate_up_base,
    gate_up_first,
    gate_up_second,
    gate_up_magnitude,
    down_frozen_weight,
    down_first,
    down_upper_map,
    down_magnitude,
    lengths,
    cotangent,
):
    rows, features = tokens.shape
    total = rows * lax.axis_size("tensor")
    rank = qkv_first.shape[2]
    units = down_frozen_weight.shape[0]
    cosine, sine = rope_tables(total)
    qkv_first_t = jnp.swapaxes(qkv_first, 1, 2)
    gu_first_t = jnp.swapaxes(gate_up_first, 1, 2)
    gu_base_t = jnp.swapaxes(gate_up_base, 1, 2)
    out_first_t = output_first.T
    down_first_t = down_first.T
    out_mag, down_mag = output_magnitude[None], down_magnitude[None]

    blocks, normed_all, qkv_other, gu_other, down_other, out_parts, at_all, q_stat, g_stat, r_stat, upstream = project(
        lengths,
        tokens,
        attn_gain[None],
        cotangent,
        qkv_base,
        gu_base_t,
        down_frozen_weight,
        output_frozen_weight,
        (
            qkv_first_t,
            qkv_second,
            qkv_magnitude,
            gu_first_t,
            gate_up_second,
            gate_up_magnitude,
            out_first_t,
            output_upper_map,
            down_first_t,
            down_upper_map,
        ),
    )
    attended, logsum, joined, out_weight, hidden, out_before, ffn_normed, out_lowrank, cot_some = attend_forward(
        lengths, q_stat, cosine, sine, blocks, out_parts, at_all, output_upper_map, out_mag, r_stat, tokens,
        ffn_gain[None], upstream,
    )
    down_all, ffn_normed_grad, gu_first_part, side, down_second_part = ffn(
        ffn_normed, upstream, cot_some, gu_base_t, gu_other, down_frozen_weight, down_other,
        (
            gu_first_t, gate_up_second, gate_up_magnitude, down_first_t, down_upper_map, g_stat, r_stat,
            down_mag,
        ),
    )
    (
        head_grads, qkv_drift, hidden_grad, result, down_drift, gate_up_first_grad, output_upper_gradient,
        output_magnitude_grad, down_sums, output_first_grad, side_total,
    ) = attend_backward(
        blocks,
        features,
        rank,
        units,
        (
            lengths, q_stat, cosine, sine, blocks, attended, logsum, joined, out_weight, at_all,
            output_upper_map, out_mag, r_stat, hidden, out_before, out_lowrank, upstream,
            ffn_normed_grad, ffn_gain[None], down_mag, down_all, gu_first_part, down_second_part, side,
        ),
    )
    (
        tokens_grad, qkv_first_grad, own_total, down_upper_gradient, down_lower_gradient, down_magnitude_grad,
    ) = qkv_backward(
        head_grads, normed_all, qkv_base, qkv_other, down_frozen_weight,
        (
            qkv_first_t, qkv_second, qkv_magnitude, q_stat, qkv_drift, r_stat, down_first_t,
            down_upper_map, down_mag, down_sums, down_drift, side_total, tokens, attn_gain[None],
            hidden_grad,
        ),
    )
    (
        qkv_first_grad, qkv_second_grad, qkv_magnitude_grad, output_first_grad, output_upper_gradient,
        output_magnitude_grad, gate_up_first_grad, gate_up_second_grad, gate_up_magnitude_grad,
        down_lower_gradient, down_upper_gradient, down_magnitude_grad,
    ) = results(
        3,
        (
            qkv_first_grad, own_total, output_upper_gradient, output_magnitude_grad, gate_up_first_grad, side_total,
            output_first_grad, down_upper_gradient, down_lower_gradient, down_magnitude_grad,
        ),
    )
    return (
        result,
        tokens_grad,
        jnp.swapaxes(qkv_first_grad, 1, 2),
        qkv_second_grad,
        qkv_magnitude_grad,
        output_first_grad.T,
        output_upper_gradient,
        output_magnitude_grad[0],
        jnp.swapaxes(gate_up_first_grad, 1, 2),
        gate_up_second_grad,
        gate_up_magnitude_grad,
        down_lower_gradient.T,
        down_upper_gradient,
        down_magnitude_grad[0],
    )


def solution(mesh):
    placed = (
        P(("dp", "tensor"), None),
        P(),
        P(),
        P(None, None, "tensor"),
        P(),
        P(None, None, "tensor"),
        P(None, "tensor"),
        P("tensor", None),
        P("tensor", None),
        P(),
        P(),
        P(None, None, "tensor"),
        P(),
        P(None, None, "tensor"),
        P(None, "tensor"),
        P("tensor", None),
        P("tensor", None),
        P(),
        P(),
        P("dp"),
        P(("dp", "tensor"), None),
    )
    return jax.shard_map(
        body,
        mesh=mesh,
        in_specs=placed,
        out_specs=(
            P(("dp", "tensor"), None),
            P(("dp", "tensor"), None),
            P(),
            P(None, None, "tensor"),
            P(None, "tensor"),
            P("tensor", None),
            P(),
            P(),
            P(),
            P(None, None, "tensor"),
            P(None, "tensor"),
            P("tensor", None),
            P(),
            P(),
        ),
        check_vma=False,
    )
```

```python
import functools

import jax
import jax.numpy as jnp
import numpy as np
from jax import lax
from jax.experimental import pallas as pl
from jax.experimental.pallas import tpu as pltpu
from jax.sharding import PartitionSpec as P

HDIM = 128
F32 = jnp.float32
BF16 = jnp.bfloat16
EXACT = lax.Precision.HIGHEST
NORM_EPS = 1e-05
ROPE_THETA = 10000.0
MASKED = -1e30
SOFTMAX_SCALE = HDIM**-0.5
LOG2E = 1.4426950408889634
VMEM_LIMIT = 60 * 2**20
TILE = 256
ANY = pl.BlockSpec(memory_space=pl.ANY)
VMEM = pl.BlockSpec(memory_space=pltpu.VMEM)
SMEM = pl.BlockSpec(memory_space=pltpu.SMEM)
MESH = pl.DeviceIdType.MESH
DMA = pltpu.SemaphoreType.DMA


def nn(left, right, precision=None):
    return jnp.dot(left, right, preferred_element_type=F32, precision=precision)


def nt(left, right, precision=None):
    return lax.dot_general(
        left, right, (((1,), (1,)), ((), ())), preferred_element_type=F32, precision=precision
    )


def tn(left, right):
    return lax.dot_general(left, right, (((0,), (0,)), ((), ())), preferred_element_type=F32)


def shape(dims, dtype):
    return jax.ShapeDtypeStruct(dims, dtype)


def tiles(size):
    return [(begin, min(TILE, size - begin)) for begin in range(0, size, TILE)]


def slots_of(count):
    if count == 8:
        return [(0, 0), (2, 4), (6, 6), (4, 2)]
    return [(mask, mask) for mask in range(0, count, 2)]


class Sender:
    def __init__(self):
        self.place = lax.axis_index("dp")
        self.me = lax.axis_index("tensor")

    def meet(self, masks, places=()):
        barrier = pltpu.get_barrier_semaphore()
        for mask in masks:
            pl.semaphore_signal(
                barrier, inc=1, device_id=(self.place, self.me ^ mask), device_id_type=MESH
            )
        for place in places:
            pl.semaphore_signal(
                barrier, inc=1, device_id=(self.place ^ place, self.me), device_id_type=MESH
            )
        pl.semaphore_wait(barrier, len(masks) + len(places))

    def copy(self, source, target, sems, mask, flip=0, step=0):
        place = self.place ^ flip if flip else self.place + step if step else self.place
        return pltpu.make_async_remote_copy(
            src_ref=source,
            dst_ref=target,
            send_sem=sems[0],
            recv_sem=sems[1],
            device_id=(place, self.me ^ mask if mask else self.me),
            device_id_type=MESH,
        )


def gather_stages(sender, count, own, slots, sems, begin=1, end=None):
    half = own.shape[0] // 2

    def rows(ref, slot, h):
        return ref.at[slot, pl.ds(h * half, half)]

    def message(slot, h, source, mask):
        return sender.copy(
            source, rows(slots, slot, h), (sems.at[0, slot, h], sems.at[1, slot, h]), mask
        )

    mine = [own.at[pl.ds(h * half, half)] for h in range(2)]
    if count != 8:
        stages = range(begin, end or count // 2)
        return {s: [message(s, h, mine[h], 2 * s) for h in range(2)] for s in stages}
    routes = {
        1: [(mine[0], 2), (mine[1], 4)],
        2: [(rows(slots, 1, 0), 4), (rows(slots, 1, 1), 2)],
        3: [(mine[0], 4), (mine[1], 2)],
    }
    return {s: [message(s, h, *routes[s][h]) for h in range(2)] for s in range(begin, end or 4)}


def reduce_stages(sender, count, parts, landed, sems, last=3, begin=1, end=4):
    half = parts.shape[1] // 2

    def message(slot, h, mask):
        at = pl.ds(h * half, half)
        return sender.copy(
            parts.at[last if slot == 3 and count == 8 else slot, at], landed.at[slot, at], (sems.at[0, slot, h], sems.at[1, slot, h]), mask
        )

    if count != 8:
        return {s: [message(s, h, 2 * s) for h in range(2)] for s in range(1, count // 2)}
    routes = {1: (2, 4), 2: (2, 4), 3: (4, 2)}
    return {s: [message(s, h, routes[s][h]) for h in range(2)] for s in range(begin, end)}


def relay(part, landed, sums):
    arrive(sums[2])
    part[...] = (part[...].astype(F32) + landed[2].astype(F32)).astype(BF16)
    start(sums[3])


def finish_reduce(count, part, landed, sums, out):
    slots = count // 2
    added = (1, 3) if count == 8 else tuple(range(1, slots))
    for slot in added:
        arrive(sums[slot])

    def columns(step, carry):
        d = pl.ds(pl.multiple_of(step * TILE, TILE), TILE)
        total = part[:, d].astype(F32)
        for slot in added:
            total = total + landed[slot, :, d].astype(F32)
        return out(d, total, carry)

    return columns


def leave_stages(sums):
    for copies in sums.values():
        leave(copies)


def norm_statistics(values_of, grads_of, features, rows):
    def columns(step, carry):
        squares, products = carry
        d = pl.ds(pl.multiple_of(step * TILE, TILE), TILE)
        values = values_of(d)
        squares = squares + jnp.sum(values * values, axis=1, keepdims=True)
        products = products + jnp.sum(values * grads_of(d), axis=1, keepdims=True)
        return squares, products

    zero = jnp.zeros((rows, 1), F32)
    squares, products = lax.fori_loop(0, features // TILE, columns, (zero, zero))
    scale = lax.rsqrt(squares * (1.0 / features) + NORM_EPS)
    return scale, products * (1.0 / features) * scale * scale * scale


class Totals:
    def __init__(self, sender, count, depth, pay, along_in, part, group_in, block, span, main, sems):
        self.sender, self.count, self.depth = sender, count, depth
        self.pay, self.along_in, self.part, self.group_in = pay, along_in, part, group_in
        self.block, self.whole, self.main, self.sems = block, span, main, sems
        self.others, self.flips = range(1, count), range(1, depth)
        self.width = part.shape[1]
        self.height, self.length = block.shape
        self.high = part.shape[0] // self.height
        self.place = sender.place

    def columns(self, place):
        return pl.ds(pl.multiple_of(place * self.width, self.width), self.width)

    def block_of(self, ref, index):
        row = lax.rem(index, self.high) * self.height
        lane = lax.div(index, self.high) * self.length
        return ref.at[
            pl.ds(pl.multiple_of(row, self.height), self.height),
            pl.ds(pl.multiple_of(lane, self.length), self.length),
        ]

    def pair(self, step, which):
        return self.sems.at[0, step, which], self.sems.at[1, step, which]

    def to_place(self, flip):
        source = self.pay.at[:, self.columns(self.place ^ flip)]
        return self.sender.copy(source, self.along_in.at[flip], self.pair(0, flip), 0, flip)

    def to_owner(self, mask):
        source = self.block_of(self.part, self.sender.me ^ mask)
        return self.sender.copy(source, self.group_in.at[mask], self.pair(1, mask), mask)

    def to_group(self, mask, index):
        return self.sender.copy(self.block, self.block_of(self.whole, index), self.pair(2, mask), mask)

    def to_all(self, flip, place):
        return self.sender.copy(self.whole, self.main.at[:, self.columns(place)], self.pair(3, flip), 0, flip)

    def give(self):
        for flip in self.flips:
            self.to_place(flip).start()

    def add_along(self):
        total = self.pay[:, self.columns(self.place)].astype(F32)
        for flip in self.flips:
            self.to_place(flip).wait_recv()
            total = total + self.along_in[flip].astype(F32)
        self.part[...] = total.astype(BF16)
        for mask in self.others:
            self.to_owner(mask).start()

    def add_group(self):
        me = self.sender.me
        total = self.block_of(self.part, me)[...].astype(F32)
        for mask in self.others:
            self.to_owner(mask).wait_recv()
            total = total + self.group_in[mask].astype(F32)
        self.block[...] = total.astype(BF16)
        for mask in self.others:
            self.to_group(mask, me).start()
        self.block_of(self.whole, me)[...] = self.block[...]

    def group(self):
        for mask in self.others:
            self.to_group(mask, self.sender.me ^ mask).wait_recv()

    def share(self):
        for flip in self.flips:
            self.to_all(flip, self.place).start()
        self.main[:, self.columns(self.place)] = self.whole[...]

    def take(self):
        for flip in self.flips:
            self.to_all(flip, self.place ^ flip).wait_recv()

    def end(self):
        for flip in self.flips:
            self.to_place(flip).wait_send()
        for mask in self.others:
            self.to_owner(mask).wait_send()
            self.to_group(mask, self.sender.me).wait_send()

    def end_share(self):
        for flip in self.flips:
            self.to_all(flip, self.place).wait_send()


def along_total(sender, depth, ref):
    total = ref[sender.place].astype(F32)
    for index in range(1, depth):
        total = total + ref[sender.place ^ index].astype(F32)
    return total


def totals_scratch(rows, features, count, depth):
    height = 16
    width = features // depth
    if width * (rows // height) // count < HDIM:
        rows = 8 * height
    length = width * rows // height // count
    return [
        pltpu.VMEM((rows, features), BF16),
        pltpu.VMEM((depth, rows, width), BF16),
        pltpu.VMEM((rows, width), BF16),
        pltpu.VMEM((count, height, length), BF16),
        pltpu.VMEM((height, length), BF16),
        pltpu.VMEM((rows, width), BF16),
        pltpu.VMEM((rows, features), BF16),
        DMA((2, 4, max(count, depth))),
    ]


class Mover:
    def __init__(self, sems):
        self.sems, self.many = sems, 0

    def __call__(self, source, target):
        copy = pltpu.make_async_copy(source, target, self.sems.at[self.many])
        self.many += 1
        copy.start()
        return copy


def start(copies):
    for copy in copies:
        copy.start()


def arrive(copies):
    for copy in copies:
        copy.wait_recv()


def leave(copies):
    for copy in copies:
        copy.wait_send()


def start_all(pairs, sems):
    copies = []
    for at, (source, target) in enumerate(pairs):
        copy = pltpu.make_async_copy(source, target, sems.at[at])
        copy.start()
        copies.append(copy)
    return copies


def call(body, name, out_shape, in_specs, out_specs, scratch, flops, moved, operands, identity):
    return pl.pallas_call(
        body,
        name=name,
        out_shape=out_shape,
        in_specs=in_specs,
        out_specs=out_specs,
        scratch_shapes=scratch,
        compiler_params=pltpu.CompilerParams(
            vmem_limit_bytes=VMEM_LIMIT, collective_id=identity, has_side_effects=True
        ),
        cost_estimate=pl.CostEstimate(flops=flops, bytes_accessed=moved, transcendentals=0),
    )(*operands)


def split(value):
    high = value.astype(BF16)
    return high, (value - high.astype(F32)).astype(BF16)


def left_stack(value):
    high, low = split(value)
    return jnp.concatenate([high, high, low], axis=0)


def right_stack(value):
    high, low = split(value)
    return jnp.concatenate([high, low, high], axis=0)


def first_direction(wide, first_t, second):
    rank = second.shape[0]
    gram = nt(first_t, first_t, EXACT)
    return wide[:rank] + wide[rank:] + 2.0 * nn(gram, second, EXACT)


def second_direction(factored, second, base, first_t):
    rank = second.shape[0]
    wide = nt(jnp.concatenate(split(factored), axis=0), base)
    gram = nt(factored, second, EXACT)
    return wide[:rank] + wide[rank:] + 2.0 * nn(gram, first_t, EXACT)


def line_forward(sender, depth, source, target, part, back, sems):
    place, last = sender.place, depth - 1

    def rows(ref, at):
        return ref.at[pl.ds(1, 3), pl.ds(pl.multiple_of(at * part, part), part)]

    def sends(act):
        @pl.when((place >= back) & (place < last))
        def _():
            at = place - back
            act(sender.copy(rows(source, at), rows(target, at), (sems.at[0, 0], sems.at[1, 0]), 0, 0, 1))

        @pl.when((place <= last - back) & (place > 0))
        def _():
            at = place + back
            act(sender.copy(rows(source, at), rows(target, at), (sems.at[0, 1], sems.at[1, 1]), 0, 0, -1))

    def arrivals(act):
        @pl.when(place > back)
        def _():
            at = place - back - 1
            act(sender.copy(rows(target, at), rows(target, at), (sems.at[0, 0], sems.at[1, 0]), 0, 0, -1))

        @pl.when(place < last - back)
        def _():
            at = place + back + 1
            act(sender.copy(rows(target, at), rows(target, at), (sems.at[0, 1], sems.at[1, 1]), 0, 0, 1))

    return sends, arrivals


def project_body(
    count, depth, lengths, tokens, gain, cot, w_own, gu_own, d_own, o_own,
    qa, qb, qmag, ga, gb, gmag, oa, ob, da, db,
    heads, rows_all, w_par, gu_par, d_par, wq, at_all, q_stat, g_stat, r_stat, upstream,
    u, w, wgu, wd, wo, to_par, to_own, second_own, second_par, b_par, sq_all,
    sems, gather_sems, par_sems, head_sems, own_sems, weight_sems, piece_sems, line_sems, small_sems,
):
    sender = Sender()
    slots = slots_of(count)
    maps, _, width = w_own.shape
    rows, features = tokens.shape
    half = rows // 2
    units = d_own.shape[0]
    rank = qb.shape[1]
    shared = count == 8 and depth == 4
    heights = o_own.shape[0]
    part = heights // depth if shared else heights
    others = list(range(1, count))
    sender.meet(others, range(1, depth) if shared else ())

    stages = gather_stages(sender, count, u.at[0], u, gather_sems)
    weights = [
        sender.copy(source, target, (weight_sems.at[0, at], weight_sems.at[1, at]), 1)
        for at, (source, target) in enumerate(
            ((w_own, w_par), (qb, b_par), (gu_own, gu_par), (d_own, d_par))
        )
    ]
    start(weights)
    pieces = []
    for slot in (1, 2) if shared else range(1, count // 2):
        at = pl.ds(pl.multiple_of(sender.place * part, part), part) if shared else pl.ds(0, heights)
        pieces.append(
            sender.copy(
                o_own.at[at], wq.at[slot, at], (piece_sems.at[0, slot], piece_sems.at[1, slot]), 2 * slot
            )
        )
    start(pieces)
    across = []
    if shared:
        for h, (slot, mask) in enumerate(((1, 4), (2, 2))):
            half_part = part // 2
            begin = pl.multiple_of(sender.place * part + h * half_part, half_part)
            at = pl.ds(begin, half_part)
            across.append(
                sender.copy(
                    wq.at[slot, at],
                    wq.at[3, at],
                    (piece_sems.at[0, 3 * h], piece_sems.at[1, 3 * h]),
                    mask,
                )
            )
    smalls = [
        sender.copy(
            oa, at_all.at[mask], (small_sems.at[0, 0, mask], small_sems.at[1, 0, mask]), mask
        )
        for mask in others
    ]
    start(smalls)
    at_all[0] = oa[...]
    local = start_all(
        [(w_own, w.at[pl.ds(0, maps)]), (d_own, wd), (o_own, wo), (gu_own, wgu), (o_own, wq.at[0])],
        sems,
    )
    squares = jnp.zeros((rows, 1), F32)
    for begin in range(0, features, TILE):
        values = tokens[:, pl.ds(begin, TILE)].astype(F32)
        squares = squares + jnp.sum(values * values, axis=1, keepdims=True)
    scale = lax.rsqrt(squares * (1.0 / features) + NORM_EPS)
    for begin in range(0, features, TILE):
        d = pl.ds(begin, TILE)
        u[0, :, d] = (tokens[:, d].astype(F32) * scale * gain[:, d]).astype(BF16)
    if shared:
        arrive(pieces)
        start(across)
    start(stages[1])
    if count != 8:
        for slot in range(2, len(slots)):
            start(stages[slot])
    second_own[...] = jnp.zeros_like(second_own)
    second_par[...] = jnp.zeros_like(second_par)
    for s in range(maps):
        second_own[pl.ds(s * rank, rank), pl.ds(s * width, width)] = (2.0 * qb[s]).astype(BF16)
    first_t = qa[...].reshape(maps * rank, features).astype(BF16)
    local[0].wait()
    pending, sent = [], []

    def one_slot(slot):
        masks = slots[slot]
        keep = pltpu.make_async_copy(u.at[slot], rows_all.at[slot], own_sems.at[slot])
        keep.start()
        pending.append(keep)
        lowrank = nt(u[slot], first_t).astype(BF16)
        for s in range(maps):
            lanes = pl.ds(s * width, width)
            to_own[slot, :, lanes] = (nn(u[slot], w[s]) + nn(lowrank, second_own[:, lanes])).astype(BF16)
        if slot == 0:
            arrive(weights[:2])
            load = pltpu.make_async_copy(w_par, w.at[pl.ds(maps, maps)], sems.at[5])
            load.start()
            for s in range(maps):
                second_par[pl.ds(s * rank, rank), pl.ds(s * width, width)] = (2.0 * b_par[s]).astype(BF16)
            load.wait()
        for s in range(maps):
            lanes = pl.ds(s * width, width)
            to_par[slot, :, lanes] = (
                nn(u[slot], w[maps + s]) + nn(lowrank, second_par[:, lanes])
            ).astype(BF16)
        for h, mask in enumerate(masks):
            at = pl.ds(h * half, half)
            keep = pltpu.make_async_copy(
                to_own.at[slot, at], heads.at[mask, at], head_sems.at[slot, h]
            )
            send = sender.copy(
                to_par.at[slot, at],
                heads.at[mask ^ 1, at],
                (par_sems.at[0, slot, h], par_sems.at[1, slot, h]),
                1,
            )
            send.start()
            keep.start()
            pending.append(keep)
            sent.append(send)

    def next_slot(slot):
        arrive(stages[slot])
        if count == 8 and slot == 1:
            start(stages[2])
            start(stages[3])
        one_slot(slot)

    one_slot(0)
    place = sender.me * rows + lax.broadcasted_iota(jnp.int32, (rows, 1), 0)
    upstream[...] = jnp.where(place < lengths[0], cot[...].astype(F32), 0.0).astype(BF16)

    local[1].wait()
    local[2].wait()
    down_left, down_right = left_stack(da[...]), right_stack(db[...])
    total = jnp.zeros((1, features), F32)
    for begin, span in tiles(units):
        direction = wd[pl.ds(begin, span), :].astype(F32) + 2.0 * tn(
            down_left[:, begin : begin + span], down_right
        )
        total = total + jnp.sum(direction * direction, axis=0, keepdims=True)
    sq_all[0, 1:2, :] = total
    direction = wo[...].astype(F32) + 2.0 * tn(left_stack(oa[...]), right_stack(ob[...]))
    sq_all[0, 0:1, :] = jnp.sum(direction * direction, axis=0, keepdims=True)
    squares = [
        sender.copy(
            sq_all.at[0], sq_all.at[mask], (small_sems.at[0, 1, mask], small_sems.at[1, 1, mask]), mask
        )
        for mask in others
    ]
    start(squares)
    r_stat[0, 8 : 8 + rank] = jnp.zeros((rank, features), F32)
    r_stat[1, 8 : 8 + rank] = first_direction(
        nn(jnp.concatenate(split(da[...]), axis=0), wd[...]), da[...], db[...]
    )
    arrive(across if shared else pieces)
    if shared:
        sends0, arrivals0 = line_forward(sender, depth, wq, wq, part, 0, line_sems.at[0])
        sends1, arrivals1 = line_forward(sender, depth, wq, wq, part, 1, line_sems.at[1])
        sends0(lambda copy: copy.start())

    for s in range(maps):
        left, right = left_stack(qa[s]), right_stack(qb[s])
        total = jnp.zeros((1, width), F32)
        for begin in range(0, features, 512):
            direction = w[s, pl.ds(begin, 512), :].astype(F32) + 2.0 * tn(
                left[:, begin : begin + 512], right
            )
            total = total + jnp.sum(direction * direction, axis=0, keepdims=True)
        norm = jnp.sqrt(total)
        q_stat[s, 0:1] = norm
        q_stat[s, 1:2] = qmag[s : s + 1] / norm
        q_stat[s, 8 : 8 + rank] = first_direction(
            nn(jnp.concatenate(split(qa[s]), axis=0), w[s]), qa[s], qb[s]
        )
    next_slot(1)

    local[3].wait()
    ones = jnp.ones((8, HDIM), BF16)
    for s in range(2):
        left, right = left_stack(gb[s]), right_stack(ga[s])
        for begin, span in tiles(units):
            direction = wgu[s, pl.ds(begin, span), :].astype(F32) + 2.0 * tn(
                left[:, begin : begin + span], right
            )
            direction = direction * direction
            folded = direction[:, :HDIM]
            for lane in range(HDIM, features, HDIM):
                folded = folded + direction[:, lane : lane + HDIM]
            high, low = split(folded)
            norm = jnp.sqrt((nt(ones, high) + nt(ones, low))[:1])
            f = pl.ds(begin, span)
            g_stat[s, 0:1, f] = norm
            g_stat[s, 1:2, f] = gmag[s : s + 1, f] / norm
        g_stat[s, 8 : 8 + rank] = first_direction(
            nt(jnp.concatenate(split(ga[s]), axis=0), wgu[s]), ga[s], gb[s]
        )
        if shared and s == 0:
            arrivals0(lambda copy: copy.wait_recv())
            sends1(lambda copy: copy.start())
    for slot in range(2, len(slots)):
        next_slot(slot)
    arrive(squares)
    total = jnp.zeros((2, features), F32)
    for index in range(count):
        total = total + sq_all[sender.me ^ index]
    norm = jnp.sqrt(total)
    r_stat[0, 0:1] = norm[0:1]
    r_stat[1, 0:1] = norm[1:2]

    for copy in pending:
        copy.wait()
    local[4].wait()
    arrive(sent + weights[2:] + smalls)
    leave(sent + weights + smalls + squares + pieces + across)
    for slot in range(1, len(slots)):
        leave(stages[slot])
    if shared:
        arrivals1(lambda copy: copy.wait_recv())
        sends0(lambda copy: copy.wait_send())
        sends1(lambda copy: copy.wait_send())


def project(lengths, tokens, gain, cot, w_own, gu_own, d_own, o_own, small):
    rows, features = tokens.shape
    count, depth = lax.axis_size("tensor"), lax.axis_size("dp")
    slots = count // 2
    maps, _, width = w_own.shape
    units = d_own.shape[0]
    rank = small[1].shape[1]
    return call(
        functools.partial(project_body, count, depth),
        "project",
        (
            shape((count, rows, maps * width), BF16),
            shape((slots, rows, features), BF16),
            shape(w_own.shape, BF16),
            shape(gu_own.shape, BF16),
            shape(d_own.shape, BF16),
            shape((slots, width, features), BF16),
            shape((count, rank, width), F32),
            shape((maps, 8 + rank, width), F32),
            shape((2, 8 + rank, units), F32),
            shape((2, 8 + rank, features), F32),
            shape((rows, features), BF16),
        ),
        [SMEM] + [VMEM] * 3 + [ANY] * 4 + [VMEM] * len(small),
        (ANY,) * 6 + (VMEM,) * 5,
        [
            pltpu.VMEM((slots, rows, features), BF16),
            pltpu.VMEM((2 * maps, features, width), BF16),
            pltpu.VMEM(gu_own.shape, BF16),
            pltpu.VMEM(d_own.shape, BF16),
            pltpu.VMEM(o_own.shape, BF16),
            pltpu.VMEM((slots, rows, maps * width), BF16),
            pltpu.VMEM((slots, rows, maps * width), BF16),
            pltpu.VMEM((maps * rank, maps * width), BF16),
            pltpu.VMEM((maps * rank, maps * width), BF16),
            pltpu.VMEM((maps, rank, width), F32),
            pltpu.VMEM((count, 2, features), F32),
            DMA((6,)),
            DMA((2, slots, 2)),
            DMA((2, slots, 2)),
            DMA((slots, 2)),
            DMA((slots,)),
            DMA((2, 4)),
            DMA((2, slots)),
            DMA((2, 2, 2)),
            DMA((2, 2, count)),
        ],
        4 * slots * rows * features * maps * width,
        8 * features * maps * width,
        (lengths, tokens, gain, cot, w_own, gu_own, d_own, o_own, *small),
        1,
    )


def turn(values, cosine, sine):
    return values * cosine + pltpu.roll(values, HDIM // 2, 1) * sine


def rms_scale(values):
    return lax.rsqrt(jnp.mean(values * values, axis=1, keepdims=True) + NORM_EPS)


def load_head(count, rows, h, xs, q_stat, cosine, sine, q, k, v):
    lane = pl.ds(pl.multiple_of(h * HDIM, HDIM), HDIM)
    heads = xs.shape[1] // (3 * HDIM)
    for a in range(count):
        at = pl.ds(a * rows, rows)
        cos, sin = cosine[at], sine[at]
        for part, target in enumerate((q, k, v)):
            lanes = pl.ds(pl.multiple_of((part * heads + h) * HDIM, HDIM), HDIM)
            values = xs[at, lanes].astype(F32) * q_stat[part, 1:2, lane]
            if part < 2:
                values = turn(values, cos, sin)
            target[at] = values.astype(BF16)


def attend_forward_body(
    count, depth, lengths, q_stat, cosine_in, sine_in, blocks, wq, at_all, ob, o_mag, r_stat, tokens_in, gain, grads,
    attended_out, logsum, joined_out, w_all, hidden_out, before_out, normed_out, lowrank, c_some,
    xs, q, k, v, wv, cosine, sine, tokens, attended, joined, hidden, before, normed, move_sems, sems, part_sems, line_sems, pair_sems, swap_sems, own_sems, c_sems, w_sems,
):
    sender = Sender()
    me, place = sender.me, sender.place
    length = lengths[0]
    _, rows, width = blocks.shape
    heads = width // (3 * HDIM)
    total = rows * count
    half = rows // 2
    features = ob.shape[1]
    shared = count == 8 and depth == 4
    part = wq.shape[1] // depth
    others = list(range(1, count))
    move = Mover(move_sems)
    copies = start_all(
        [
            (blocks.at[mask], xs.at[pl.ds(pl.multiple_of((me ^ mask) * rows, rows), rows)])
            for mask in range(count)
        ],
        sems,
    )
    copies = copies + [move(cosine_in, cosine), move(sine_in, sine)]
    tokens_load = move(tokens_in, tokens)
    sender.meet(others, range(1, depth) if shared else ())

    stages = gather_stages(sender, count, grads, c_some, c_sems, 1, 3)
    start(stages[1])

    def rows_of(ref, at):
        return ref.at[pl.ds(1, 3), pl.ds(pl.multiple_of(at * part, part), part)]

    if shared:
        whole = pltpu.make_async_copy(wq.at[0], wv.at[0, 0], part_sems.at[depth])
        whole_pair = sender.copy(
            wq.at[0], wv.at[1, 0], (pair_sems.at[0, depth], pair_sems.at[1, depth]), 1
        )
        whole.start()
        whole_pair.start()

        def near(act, act_pair):
            for at in range(depth):

                @pl.when((place - at <= 2) & (at - place <= 2))
                def _():
                    if act is not None:
                        act(pltpu.make_async_copy(rows_of(wq, at), rows_of(wv.at[0], at), part_sems.at[at]))
                    act_pair(
                        sender.copy(
                            rows_of(wq, at), rows_of(wv.at[1], at), (pair_sems.at[0, at], pair_sems.at[1, at]), 1
                        )
                    )

        def far(act):
            for at, other in ((0, depth - 1), (depth - 1, 0)):

                @pl.when(place == other)
                def _():
                    act(
                        sender.copy(
                            rows_of(wv.at[0], at), rows_of(wv.at[1], at),
                            (pair_sems.at[0, at], pair_sems.at[1, at]), 1,
                        )
                    )

        def line_sends(act):
            @pl.when(place == 2)
            def _():
                act(
                    sender.copy(
                        rows_of(wq, 0), rows_of(wv.at[0], 0), (line_sems.at[0, 0], line_sems.at[1, 0]), 0, 0, 1
                    )
                )

            @pl.when(place == 1)
            def _():
                act(
                    sender.copy(
                        rows_of(wq, 3), rows_of(wv.at[0], 3), (line_sems.at[0, 1], line_sems.at[1, 1]), 0, 0, -1
                    )
                )

        def line_arrivals(act):
            @pl.when(place == 3)
            def _():
                act(
                    sender.copy(
                        rows_of(wv.at[0], 0), rows_of(wv.at[0], 0), (line_sems.at[0, 0], line_sems.at[1, 0]), 0, 0, -1
                    )
                )

            @pl.when(place == 0)
            def _():
                act(
                    sender.copy(
                        rows_of(wv.at[0], 3), rows_of(wv.at[0], 3), (line_sems.at[0, 1], line_sems.at[1, 1]), 0, 0, 1
                    )
                )

        line_sends(lambda copy: copy.start())
        near(lambda copy: copy.start(), lambda copy: copy.start())
    else:
        whole = pltpu.make_async_copy(wq, wv.at[0], part_sems.at[0])
        whole_pair = sender.copy(wq, wv.at[1], (pair_sems.at[0, 0], pair_sems.at[1, 0]), 1)
        whole.start()
        whole_pair.start()

    for copy in copies:
        copy.wait()
    factor = SOFTMAX_SCALE * LOG2E
    bias = jnp.where(lax.broadcasted_iota(jnp.int32, (1, total), 1) < length, 0.0, MASKED)
    kept = lax.broadcasted_iota(jnp.int32, (rows, rows), 1) <= lax.broadcasted_iota(
        jnp.int32, (rows, rows), 0
    )

    def exchange(h, mask):
        lane = pl.ds(pl.multiple_of(h * HDIM, HDIM), HDIM)
        return sender.copy(
            attended.at[mask, :, lane],
            joined.at[mask, :, lane],
            (swap_sems.at[0, h, mask], swap_sems.at[1, h, mask]),
            mask,
        )

    def one_head(h, carry):
        load_head(count, rows, h, xs, q_stat, cosine, sine, q, k, v)
        lane = pl.ds(pl.multiple_of(h * HDIM, HDIM), HDIM)
        for a in range(count):
            at = pl.ds(a * rows, rows)
            query = q[at]
            inner = nt(query, k[at]) * factor + bias[:, a * rows : (a + 1) * rows]
            inner = jnp.where(kept, inner, MASKED)
            highest = jnp.max(inner, axis=1, keepdims=True)
            if a:
                earlier = pl.ds(0, a * rows)
                outer = nt(query, k[earlier]) * factor + bias[:, : a * rows]
                highest = jnp.maximum(highest, jnp.max(outer, axis=1, keepdims=True))
            inner = jnp.exp2(inner - highest)
            sums = jnp.sum(inner, axis=1, keepdims=True)
            result = nn(inner.astype(BF16), v[at])
            if a:
                outer = jnp.exp2(outer - highest)
                sums = sums + jnp.sum(outer, axis=1, keepdims=True)
                result = result + nn(outer.astype(BF16), v[earlier])
            attended[a ^ me, :, lane] = (result * (1.0 / sums)).astype(BF16)
            column = jnp.broadcast_to(highest + jnp.log2(sums), (rows, HDIM))
            logsum[h, :, at] = jnp.transpose(column)[:1]
        for mask in others:
            exchange(h, mask).start()
        return carry

    lax.fori_loop(0, heads, one_head, 0)
    arrive(stages[1])
    start(stages[2])
    joined[0] = attended[0]
    outs = [move(attended, attended_out)]
    if shared:
        line_arrivals(lambda copy: copy.wait_recv())
        far(lambda copy: copy.start())
        whole.wait()
        near(lambda copy: copy.wait(), lambda copy: copy.wait_recv())
        far(lambda copy: copy.wait_recv())
    else:
        whole.wait()
    arrive([whole_pair])
    keeps = start_all(
        [(wv.at[mask % 2, mask // 2], w_all.at[mask]) for mask in range(count)], w_sems
    )
    for h in range(heads):
        arrive([exchange(h, mask) for mask in others])
    outs.append(move(joined, joined_out))
    tokens_load.wait()

    low = jnp.zeros((rows, ob.shape[0]), F32)
    for mask in range(count):
        low = low + nt(joined[mask], at_all[mask].astype(BF16))
    low = low.astype(BF16)
    lowrank[...] = low

    def columns(step, squares):
        d = pl.ds(pl.multiple_of(step * TILE, TILE), TILE)
        result = nn(low, (2.0 * ob[:, d]).astype(BF16))
        for mask in range(count):
            result = result + nn(joined[mask], wv[mask % 2, mask // 2, :, d])
        before[:, d] = result.astype(BF16)
        result = tokens[:, d].astype(F32) + result * (o_mag[:, d] / r_stat[0, 0:1, d])
        hidden[:, d] = result
        return squares + jnp.sum(result * result, axis=1, keepdims=True)

    squares = lax.fori_loop(0, features // TILE, columns, jnp.zeros((rows, 1), F32))
    scale = lax.rsqrt(squares * (1.0 / features) + NORM_EPS)
    outs += [move(hidden, hidden_out), move(before, before_out)]
    normed[...] = (hidden[...] * scale * gain[...]).astype(BF16)
    outs.append(move(normed, normed_out))
    for copy in keeps + outs:
        copy.wait()
    arrive(stages[2])
    leave(stages[1] + stages[2] + [whole_pair])
    for h in range(heads):
        leave([exchange(h, mask) for mask in others])
    if shared:
        line_sends(lambda copy: copy.wait_send())
        near(None, lambda copy: copy.wait_send())
        far(lambda copy: copy.wait_send())


def attend_forward(lengths, q_stat, cosine, sine, blocks, wq, at_all, ob, o_mag, r_stat, tokens, gain, grads):
    count, rows, width = blocks.shape
    depth = lax.axis_size("dp")
    head_width = width // 3
    heads = head_width // HDIM
    total = count * rows
    features = ob.shape[1]
    slots = count // 2
    return call(
        functools.partial(attend_forward_body, count, depth),
        "attend_forward",
        (
            shape((count, rows, head_width), BF16),
            shape((heads, 1, total), F32),
            shape((count, rows, head_width), BF16),
            shape((count, head_width, features), BF16),
            shape((rows, features), F32),
            shape((rows, features), BF16),
            shape((rows, features), BF16),
            shape((rows, ob.shape[0]), BF16),
            shape((3, rows, features), BF16),
        ),
        [SMEM, VMEM, ANY, ANY, ANY, ANY] + [VMEM] * 4 + [ANY, VMEM, ANY],
        (ANY, VMEM, ANY, ANY, ANY, ANY, ANY, VMEM, ANY),
        [pltpu.VMEM((total, width), BF16)]
        + [pltpu.VMEM((total, HDIM), BF16)] * 3
        + [
            pltpu.VMEM((2, slots, head_width, features), BF16),
            pltpu.VMEM((total, HDIM), F32),
            pltpu.VMEM((total, HDIM), F32),
            pltpu.VMEM((rows, features), BF16),
            pltpu.VMEM((count, rows, head_width), BF16),
            pltpu.VMEM((count, rows, head_width), BF16),
            pltpu.VMEM((rows, features), F32),
            pltpu.VMEM((rows, features), BF16),
            pltpu.VMEM((rows, features), BF16),
            DMA((8,)),
            DMA((count,)),
            DMA((depth + 1,)),
            DMA((2, 2)),
            DMA((2, depth + 1)),
            DMA((2, heads, count)),
            DMA((1,)),
            DMA((2, 3, 2)),
            DMA((count,)),
        ],
        4 * heads * total * total * HDIM + 2 * rows * features * features,
        2 * total * width * 2,
        (lengths, q_stat, cosine, sine, blocks, wq, at_all, ob, o_mag, r_stat, tokens, gain, grads),
        2,
    )


def ffn_body(
    count, own, c_own, c_some, gu_own, gu_par, d_own, d_par,
    ga, gb, gmag, da, db, g_stat, r_stat, d_mag,
    down_all, dx_sum, g_first, side, g_down_second,
    u, c, wgu, wd, grad_low, sw, bg, down, parts, landed, second, second_par, da_par, scale_par, scale_own, d_second,
    g_second, g_down_first, drift, second_landed, first_landed, drift_landed,
    sems, down_sems, gather_sems, c_sems, reduce_sems, pair_sems,
):
    sender = Sender()
    slots = count // 2
    rows, features = own.shape
    units = d_own.shape[0]
    rank = da.shape[0]
    sender.meet([1] + list(range(2, count, 2)))
    stages = gather_stages(sender, count, own, u, gather_sems)
    c_stages = gather_stages(sender, count, c_own, c, c_sems, 3)
    sums = reduce_stages(sender, count, parts, landed, reduce_sems)
    scale_own[...] = g_stat[:, 1]
    pairs = [
        sender.copy(source, target, (pair_sems.at[0, at], pair_sems.at[1, at]), 1)
        for at, (source, target) in enumerate(((gb, second_par), (da, da_par), (scale_own, scale_par)))
    ]
    start(pairs)
    start(stages[1])
    local = start_all(
        [(own, u.at[0]), (c_own, c.at[0])]
        + [(gu_own, wgu.at[0]), (d_own, wd.at[0]), (gu_par, wgu.at[1]), (d_par, wd.at[1])]
        + [(c_some.at[slot], c.at[slot]) for slot in (1, 2)],
        sems,
    )
    if count != 8:
        for slot in range(2, slots):
            start(stages[slot])
        for slot in range(3, slots):
            start(c_stages[slot])
    first_t = ga[...].reshape(2 * rank, features).astype(BF16)
    d_scale = d_mag[...] / r_stat[1, 0:1]
    d_second[...] = (2.0 * db[...]).astype(BF16)
    second[...] = jnp.zeros_like(second)
    for part in range(2):
        second[0, part, pl.ds(part * rank, rank), :] = (2.0 * gb[part]).astype(BF16)
    arrive(pairs)
    for part in range(2):
        second[1, part, pl.ds(part * rank, rank), :] = (2.0 * second_par[part]).astype(BF16)
    da_low = (da[...].astype(BF16), da_par[...].astype(BF16))
    for ref in (g_first, g_second, g_down_first, g_down_second, drift):
        ref[...] = jnp.zeros_like(ref)
    local[0].wait()
    local[1].wait()
    rooms = down.shape[0]

    def store(slot):
        return pltpu.make_async_copy(down.at[slot % rooms], down_all.at[slot], down_sems.at[slot])

    def one_slot(slot, carry):
        room = lax.rem(slot, rooms)
        if slots > rooms:

            @pl.when(slot >= rooms)
            def _():
                store(slot - rooms).wait()

        for at in range(1, slots):

            @pl.when(slot == at)
            def _():
                if at in (1, 2):
                    local[5 + at].wait()
                else:
                    arrive(c_stages[at])

        lowrank = nt(u[slot], first_t).astype(BF16)
        lowrank_t = nt(first_t, u[slot]).astype(BF16)
        grad_low[...] = (c[slot].astype(F32) * d_scale).astype(BF16)
        d_low_grad = nt(grad_low[...], d_second[...]).astype(BF16)
        d_low_grad_t = nt(d_second[...], grad_low[...]).astype(BF16)
        d_low = jnp.zeros((rows, rank), F32)
        d_low_t = jnp.zeros((rank, rows), F32)
        u_low = jnp.zeros((rows, 2 * rank), F32)
        u_low_t = jnp.zeros((2 * rank, rows), F32)
        for which, scale in enumerate((scale_own, scale_par)):

            @pl.when(slot == 0)
            def _():
                local[2 + 2 * which].wait()
                local[3 + 2 * which].wait()

            for at in range(1, slots) if which else ():

                @pl.when(slot == at - 1)
                def _():
                    arrive(stages[at])
                    if count == 8 and at == 1:
                        start(stages[2])
                        start(stages[3])
                        start(c_stages[3])

            for begin, span in tiles(units):
                f = pl.ds(begin, span)
                gate_before = nt(u[slot], wgu[which, 0, f, :]) + nn(lowrank, second[which, 0, :, f])
                up_before = nt(u[slot], wgu[which, 1, f, :]) + nn(lowrank, second[which, 1, :, f])
                gate = gate_before * scale[0:1, f]
                up = up_before * scale[1:2, f]
                sigmoid = 1.0 / (1.0 + jnp.exp(-gate))
                silu = gate * sigmoid
                swiglu = (silu * up).astype(BF16)
                swiglu_grad = nt(grad_low[...], wd[which, f, :]) + nn(
                    d_low_grad, da_low[which][:, begin : begin + span]
                )
                swiglu_grad = swiglu_grad.astype(BF16).astype(F32)
                gate_grad = swiglu_grad * up * (sigmoid * (1.0 + gate * (1.0 - sigmoid)))
                up_grad = swiglu_grad * silu
                drift[which, 0:1, f] += jnp.sum(gate_grad * gate_before, axis=0, keepdims=True)
                drift[which, 1:2, f] += jnp.sum(up_grad * up_before, axis=0, keepdims=True)
                sw[which, :, f] = swiglu
                bg[which, 0, :, f] = (gate_grad * scale[0:1, f]).astype(BF16)
                bg[which, 1, :, f] = (up_grad * scale[1:2, f]).astype(BF16)
            d_low = d_low + nt(sw[which], da_low[which])
            d_low_t = d_low_t + nt(da_low[which], sw[which])
            for part in range(2):
                u_low = u_low + nt(bg[which, part], second[which, part])
                u_low_t = u_low_t + nt(second[which, part], bg[which, part])
                g_second[which, part] += 2.0 * nn(
                    lowrank_t[part * rank : (part + 1) * rank], bg[which, part]
                )
            g_down_first[which] += nn(d_low_grad_t, sw[which])
        d_low = d_low.astype(BF16)
        d_low_t = d_low_t.astype(BF16)
        u_low = u_low.astype(BF16)
        u_low_t = u_low_t.astype(BF16)

        for begin in range(0, features, TILE):
            d = pl.ds(begin, TILE)
            dx = nn(u_low, first_t[:, begin : begin + TILE])
            for which in range(2):
                for part in range(2):
                    dx = dx + nn(bg[which, part], wgu[which, part, :, d])
            parts[slot, :, d] = dx.astype(BF16)
        for at in range(1, slots):

            @pl.when(slot == at)
            def _():
                if count == 8 and at == 3:
                    relay(parts.at[3], landed, sums)
                else:
                    start(sums[at])

        for begin in range(0, features, TILE):
            d = pl.ds(begin, TILE)
            g_first[:, d] += nn(u_low_t, u[slot, :, d])
            total = nn(sw[0], wd[0, :, d]) + nn(sw[1], wd[1, :, d]) + nn(d_low, d_second[:, d])
            down[room, :, d] = total.astype(BF16)
            g_down_second[:, d] += 2.0 * nn(d_low_t, grad_low[:, d])
        store(slot).start()
        return carry

    lax.fori_loop(0, slots, one_slot, 0)

    gives = [
        sender.copy(source, target, (pair_sems.at[0, at], pair_sems.at[1, at]), 1)
        for at, source, target in (
            (3, g_second.at[1], second_landed),
            (4, g_down_first.at[1], first_landed),
            (5, drift.at[1], drift_landed),
        )
    ]
    start(gives)
    arrive(gives)
    total_drift = drift[0] + drift_landed[...]
    side[...] = jnp.zeros_like(side)
    side[2 * rank : 3 * rank] = g_down_first[0] + first_landed[...]
    for part in range(2):
        norm = g_stat[part, 0:1]
        one = total_drift[part : part + 1]
        factor = -one * gmag[part : part + 1] / (norm * norm * norm)
        at = pl.ds(part * rank, rank)
        side[at] = g_second[0, part] + second_landed[part] + 2.0 * g_stat[part, 8 : 8 + rank] * factor
        side[3 * rank + part : 3 * rank + part + 1] = one / norm
        factored = gb[part] * factor
        wide = nn(jnp.concatenate(split(factored), axis=0), wgu[0, part])
        gram = nt(factored, gb[part], EXACT)
        g_first[at] += 2.0 * (wide[:rank] + wide[rank:] + 2.0 * nn(gram, ga[part], EXACT))

    def out(d, value, carry):
        dx_sum[:, d] = value.astype(BF16)
        return carry

    lax.fori_loop(0, features // TILE, finish_reduce(count, parts.at[0], landed, sums, out), 0)
    for slot in range(max(0, slots - rooms), slots):
        store(slot).wait()
    leave(pairs + gives)
    for copies in (sums, stages, c_stages):
        leave_stages(copies)


def ffn(own, c_own, c_some, gu_own, gu_par, d_own, d_par, small):
    rows, features = own.shape
    count = lax.axis_size("tensor")
    slots = count // 2
    units = d_own.shape[0]
    rank = small[3].shape[0]
    many = pltpu.VMEM((slots, rows, features), BF16)
    return call(
        functools.partial(ffn_body, count),
        "ffn",
        (
            shape((slots, rows, features), BF16),
            shape((rows, features), BF16),
            shape((2 * rank, features), F32),
            shape((4 * rank, units), F32),
            shape((rank, features), F32),
        ),
        [ANY] * 7 + [VMEM] * len(small),
        (ANY,) + (VMEM,) * 4,
        [
            many,
            many,
            pltpu.VMEM((2, 2, units, features), BF16),
            pltpu.VMEM((2, units, features), BF16),
            pltpu.VMEM((rows, features), BF16),
            pltpu.VMEM((2, rows, units), BF16),
            pltpu.VMEM((2, 2, rows, units), BF16),
            pltpu.VMEM((min(slots, 4), rows, features), BF16),
            many,
            many,
            pltpu.VMEM((2, 2, 2 * rank, units), BF16),
            pltpu.VMEM((2, rank, units), F32),
            pltpu.VMEM((rank, units), F32),
            pltpu.VMEM((2, units), F32),
            pltpu.VMEM((2, units), F32),
            pltpu.VMEM((rank, features), BF16),
            pltpu.VMEM((2, 2, rank, units), F32),
            pltpu.VMEM((2, rank, units), F32),
            pltpu.VMEM((2, 2, units), F32),
            pltpu.VMEM((2, rank, units), F32),
            pltpu.VMEM((rank, units), F32),
            pltpu.VMEM((2, units), F32),
            DMA((8,)),
            DMA((slots,)),
            DMA((2, slots, 2)),
            DMA((2, slots, 2)),
            DMA((2, slots, 2)),
            DMA((2, 6)),
        ],
        24 * slots * rows * features * units,
        12 * features * units,
        (own, c_own, c_some, gu_own, gu_par, d_own, d_par, *small),
        3,
    )


def attend_backward_body(
    count, depth, lengths, q_stat, cosine_in, sine_in, blocks, attended_in, logsum, joined_in, w_all, at_all, ob, o_mag,
    r_stat, hidden_in, before_in, lowrank, cot_in, dx_in, gain, d_mag, down_all, gu_first, d_second, side,
    out_all, drift, hidden_grad_out, result_out, d_drift, span_sum, side_total,
    xs, dos, q, k, v, dq, centre, wv, og, ag, parts, landed, side_line,
    cosine, sine, attended, joined, hidden, before, cot, dx_sum, out, hidden_grad, result, o_drift_row,
    pay, along_in, part, group_in, block, total_sems,
    move_sems, sems, w_sems, part_sems, swap_sems, reduce_sems, side_sems,
):
    sender = Sender()
    me = sender.me
    length = lengths[0]
    _, rows, width = blocks.shape
    heads = width // (3 * HDIM)
    total = rows * count
    features = ob.shape[1]
    rank = ob.shape[0]
    slots = count // 2
    others = list(range(1, count))
    flips = list(range(1, depth))
    order = others + [0]
    move = Mover(move_sems)
    early = [move(hidden_in, hidden), move(dx_in, dx_sum), move(cot_in, cot), move(before_in, before)]
    loads = dict(
        zip(order, start_all([(w_all.at[mask], wv.at[mask]) for mask in order], w_sems))
    )
    joined_load = move(joined_in, joined)
    late = [move(cosine_in, cosine), move(sine_in, sine), move(attended_in, attended)]
    sender.meet(others, flips)
    sums = reduce_stages(sender, count, down_all, landed, reduce_sems, end=3)
    if count == 8:
        sums.update(reduce_stages(sender, count, parts, landed, reduce_sems, 1, 3))
        start(sums[2])
    else:
        for slot in range(1, slots):
            start(sums[slot])
    copies = start_all(
        [
            (blocks.at[mask], xs.at[pl.ds(pl.multiple_of((me ^ mask) * rows, rows), rows)])
            for mask in range(count)
        ],
        sems,
    )
    kept_parts = (0, 3) if count == 8 else (0,)
    part_loads = start_all(
        [(down_all.at[slot], parts.at[at]) for at, slot in enumerate(kept_parts)], part_sems
    )

    for copy in early[:2]:
        copy.wait()
    scale, back = norm_statistics(
        lambda d: hidden[:, d], lambda d: dx_sum[:, d].astype(F32) * gain[:, d], features, rows
    )

    for copy in early[2:]:
        copy.wait()

    def rows_grad(step, carry):
        d = pl.ds(pl.multiple_of(step * TILE, TILE), TILE)
        grad = cot[:, d].astype(F32) + scale * (dx_sum[:, d].astype(F32) * gain[:, d]) - hidden[:, d] * back
        hidden_grad[:, d] = grad
        o_drift_row[:, d] = jnp.sum(grad * before[:, d].astype(F32), axis=0, keepdims=True)
        og[:, d] = (grad * (o_mag[:, d] / r_stat[0, 0:1, d])).astype(BF16)
        return carry

    lax.fori_loop(0, features // TILE, rows_grad, 0)
    outs = [move(hidden_grad, hidden_grad_out)]
    o_drift = o_drift_row[...]
    second = (2.0 * ob[...]).astype(BF16)
    low_grad = nt(og[...], second).astype(BF16)
    mine = pl.ds(pl.multiple_of(me * rows, rows), rows)

    def exchange(h, mask, at=None):
        lane = pl.ds(pl.multiple_of(h * HDIM, HDIM), HDIM)
        return sender.copy(
            ag.at[mask, :, lane],
            dos.at[mine if at is None else at, lane],
            (swap_sems.at[0, h, mask], swap_sems.at[1, h, mask]),
            mask,
        )

    def landing(h, mask):
        return exchange(h, mask, pl.ds(pl.multiple_of((me ^ mask) * rows, rows), rows))

    for mask in order:
        loads[mask].wait()
        grad = nt(og[...], wv[mask]) + nn(low_grad, at_all[mask].astype(BF16))
        if mask:
            ag[mask] = grad.astype(BF16)
            exchange(0, mask).start()
        else:
            dos[mine] = grad.astype(BF16)
    for h in range(1, heads):
        for mask in others:
            exchange(h, mask).start()

    low_grad_t = nt(second, og[...]).astype(BF16)
    norm = r_stat[0, 0:1]
    factor = -o_drift * o_mag[...] / (norm * norm * norm)
    factored = ob[...] * factor
    wide = jnp.zeros((2 * rank, features), F32)
    gram = jnp.zeros((rank, rank), F32)
    joined_load.wait()
    for mask in range(count):
        first = at_all[mask]
        span = pl.ds(pl.multiple_of((me ^ mask) * (width // 3), width // 3), width // 3)
        pay[6 * rank : 7 * rank, span] = (
            nn(low_grad_t, joined[mask]) + 2.0 * second_direction(factored, ob[...], wv[mask], first)
        ).astype(BF16)
        wide = wide + nn(jnp.concatenate(split(first), axis=0), wv[mask])
        gram = gram + nt(first, first, EXACT)
    product = wide[:rank] + wide[rank:] + 2.0 * nn(gram, ob[...], EXACT)
    pay[0 : 2 * rank] = gu_first[...].astype(BF16)
    pay[2 * rank : 3 * rank] = d_second[...].astype(BF16)
    pay[3 * rank : 4 * rank] = r_stat[1, 8 : 8 + rank].astype(BF16)
    pay[4 * rank : 5 * rank] = (
        2.0 * tn(lowrank[...], og[...]) + 2.0 * product * factor
    ).astype(BF16)
    pay[5 * rank : 6 * rank] = jnp.broadcast_to(o_drift, (rank, features)).astype(BF16)
    pay[7 * rank :] = jnp.zeros_like(pay[7 * rank :])
    totals = Totals(
        sender, count, depth, pay, along_in, part, group_in, block, span_sum, None, total_sems
    )
    totals.give()
    side_line[0] = side[...].astype(BF16)
    sides = [
        sender.copy(
            side_line.at[0], side_line.at[flip], (side_sems.at[0, flip], side_sems.at[1, flip]), 0, flip
        )
        for flip in flips
    ]
    start(sides)
    for load in part_loads:
        load.wait()
    if count == 8:
        relay(parts.at[1], landed, sums)
    for copy in copies + late:
        copy.wait()

    short = total <= 2048
    factor2 = SOFTMAX_SCALE * LOG2E
    kept = lax.broadcasted_iota(jnp.int32, (rows, rows), 0) <= lax.broadcasted_iota(
        jnp.int32, (rows, rows), 1
    )

    def one_head(h, carry):
        load_head(count, rows, h, xs, q_stat, cosine, sine, q, k, v)
        for mask in others:
            landing(h, mask).wait_recv()
        own = pl.ds(pl.multiple_of(h * HDIM, HDIM), HDIM)

        def lanes(part):
            return pl.ds(pl.multiple_of((part * heads + h) * HDIM, HDIM), HDIM)

        for a in range(count):
            at = pl.ds(a * rows, rows)
            values = dos[at, own].astype(F32) * attended[a ^ me, :, own].astype(F32)
            column = jnp.sum(values, axis=1, keepdims=True)
            centre[:, at] = jnp.transpose(jnp.broadcast_to(column, (rows, HDIM)))[:8]

        def finish(a, part, grad):
            at = pl.ds(a * rows if isinstance(a, int) else pl.multiple_of(a * rows, rows), rows)
            if part < 2:
                grad = turn(grad, cosine[at], -sine[at])
            out[a ^ me, :, lanes(part)] = (grad * q_stat[part, 1:2, own]).astype(BF16)
            return jnp.sum(grad * xs[at, lanes(part)].astype(F32), axis=0, keepdims=True)

        def pair_grads(at, after, bias, keep):
            key = k[at]
            weights = jnp.exp2(nt(key, q[after]) * factor2 + (bias - logsum[h, :, after]))
            weights = keep(weights)
            score_grad = weights * (nt(v[at], dos[after, own]) - centre[:1, after])
            score_grad = score_grad.astype(BF16)
            value_grad = nn(weights.astype(BF16), dos[after, own])
            return nn(score_grad, q[after]), value_grad, tn(score_grad, key)

        zero = jnp.zeros((1, HDIM), F32)
        iota = lax.broadcasted_iota(jnp.int32, (rows, 1), 0)
        if short:
            key_drift, value_drift = zero, zero
            for a in range(count):
                bias = jnp.where(a * rows + iota < length, 0.0, MASKED)

                def keep(weights):
                    first = jnp.where(kept, weights[:, :rows], 0.0)
                    if a == count - 1:
                        return first
                    return jnp.concatenate([first, weights[:, rows:]], axis=1)

                at, after = pl.ds(a * rows, rows), pl.ds(a * rows, total - a * rows)
                key_grad, value_grad, query_part = pair_grads(at, after, bias, keep)
                if a == 0:
                    dq[...] = query_part
                else:
                    dq[after] += query_part
                key_drift = key_drift + finish(a, 1, key_grad * SOFTMAX_SCALE)
                value_drift = value_drift + finish(a, 2, value_grad)
        else:
            dq[...] = jnp.zeros_like(dq)

            def one_block(a, drifts):
                start_at = pl.multiple_of(a * rows, rows)
                at = pl.ds(start_at, rows)
                bias = jnp.where(start_at + iota < length, 0.0, MASKED)

                def one_pair(i, grads):
                    after = pl.ds(pl.multiple_of(i * rows, rows), rows)
                    ahead = (i - a) * rows

                    def keep(weights):
                        return jnp.where(kept | (ahead > 0), weights, 0.0)

                    key_part, value_part, query_part = pair_grads(at, after, bias, keep)
                    dq[after] += query_part
                    return grads[0] + key_part, grads[1] + value_part

                none = jnp.zeros((rows, HDIM), F32)
                key_grad, value_grad = lax.fori_loop(a, count, one_pair, (none, none))
                return (
                    drifts[0] + finish(a, 1, key_grad * SOFTMAX_SCALE),
                    drifts[1] + finish(a, 2, value_grad),
                )

            key_drift, value_drift = lax.fori_loop(0, count, one_block, (zero, zero))
        query_drift = zero
        for a in range(count):
            query_drift = query_drift + finish(a, 0, dq[pl.ds(a * rows, rows)] * SOFTMAX_SCALE)
        drift[0, :, own] = query_drift
        drift[1, :, own] = key_drift
        drift[2, :, own] = value_drift

        @pl.when(h == 0)
        def _():
            totals.add_along()
            if count == 8:
                start(sums[1])

        return carry

    lax.fori_loop(0, heads, one_head, 0)
    outs.append(move(out, out_all))
    totals.add_group()
    arrive(sides)
    side_total[...] = along_total(sender, depth, side_line)

    def rows_out(d, value, carry):
        result[:, d] = (hidden[:, d] + value * (d_mag[:, d] / r_stat[1, 0:1, d])).astype(BF16)
        d_drift[:, d] = jnp.sum(cot[:, d].astype(F32) * value, axis=0, keepdims=True)
        return carry

    lax.fori_loop(0, features // TILE, finish_reduce(count, parts.at[0], landed, sums, rows_out), 0)
    outs.append(move(result, result_out))
    totals.group()
    totals.end()
    for copy in outs:
        copy.wait()
    leave(sides)
    leave_stages(sums)
    for h in range(heads):
        for mask in others:
            exchange(h, mask).wait_send()


def attend_backward(blocks, features, rank, units, operands):
    count, rows, width = blocks.shape
    depth = lax.axis_size("dp")
    head_width = width // 3
    heads = head_width // HDIM
    total = count * rows
    slots = count // 2
    many = pltpu.VMEM((slots, rows, features), BF16)
    early = totals_scratch(8 * rank, features, count, depth)
    return call(
        functools.partial(attend_backward_body, count, depth),
        "attend_backward",
        (
            shape((count, rows, width), BF16),
            shape((3, 1, head_width), F32),
            shape((rows, features), F32),
            shape((rows, features), BF16),
            shape((1, features), F32),
            shape(early[5].shape, BF16),
            shape((4 * rank, units), F32),
        ),
        [SMEM, VMEM, ANY, ANY, ANY, ANY, VMEM, ANY, ANY] + [VMEM] * 4
        + [ANY, ANY, VMEM, ANY, ANY, VMEM, VMEM, ANY] + [VMEM] * 3,
        (ANY, VMEM, ANY, ANY) + (VMEM,) * 3,
        [pltpu.VMEM((total, width), BF16), pltpu.VMEM((total, head_width), BF16)]
        + [pltpu.VMEM((total, HDIM), BF16)] * 3
        + [
            pltpu.VMEM((total, HDIM), F32),
            pltpu.VMEM((8, total), F32),
            pltpu.VMEM((count, head_width, features), BF16),
            pltpu.VMEM((rows, features), BF16),
            pltpu.VMEM((count, rows, head_width), BF16),
            pltpu.VMEM((2 if count == 8 else 1, rows, features), BF16),
            many,
            pltpu.VMEM((depth, 4 * rank, units), BF16),
            pltpu.VMEM((total, HDIM), F32),
            pltpu.VMEM((total, HDIM), F32),
            pltpu.VMEM((count, rows, head_width), BF16),
            pltpu.VMEM((count, rows, head_width), BF16),
            pltpu.VMEM((rows, features), F32),
            pltpu.VMEM((rows, features), BF16),
            pltpu.VMEM((rows, features), BF16),
            pltpu.VMEM((rows, features), BF16),
            pltpu.VMEM((count, rows, width), BF16),
            pltpu.VMEM((rows, features), F32),
            pltpu.VMEM((rows, features), BF16),
            pltpu.VMEM((1, features), F32),
        ]
        + early[:5]
        + [
            early[7],
            DMA((11,)),
            DMA((count,)),
            DMA((count,)),
            DMA((2,)),
            DMA((2, heads, count)),
            DMA((2, slots, 2)),
            DMA((2, depth)),
        ],
        10 * heads * total * total * HDIM + 2 * rows * features * features,
        2 * total * width * 4,
        operands,
        4,
    )


def qkv_backward_body(
    count, depth, grads, u_all, w_own, w_par, d_own, qa, qb, qmag, q_stat, drift, r_stat, da, db, d_mag,
    early_sum, d_drift, side_total, tokens_in, gain, hidden_grad_in,
    tokens_grad_out, first_grad, own_total, upper, lower, d_mag_grad, gu_total, o_upper, o_mag_grad, o_total,
    u, w, wd, b_own, b_par, parts, landed, second_own, second_par, qb_par, g_first, g_own, g_par, g_landed, own_line,
    lows, dx_sum, tokens, hidden_grad, tokens_grad,
    pay, along_in, part, group_in, block, span_sum, main, total_sems, early_main, early_sems,
    move_sems, sems, u_sems, own_sems, par_sems, reduce_sems, small_sems, line_sems,
):
    sender = Sender()
    slots = slots_of(count)
    order = [2, 1, 3, 0] if count == 8 else list(range(len(slots) - 1, -1, -1))
    maps, features, width = w_own.shape
    rank = qb.shape[1]
    rows = grads.shape[1]
    half = rows // 2
    others = list(range(1, count))
    flips = list(range(1, depth))
    move = Mover(move_sems)
    loads = {slot: pltpu.make_async_copy(u_all.at[slot], u.at[slot], u_sems.at[slot]) for slot in order}
    loads[order[0]].start()
    local = start_all([(w_own, w.at[pl.ds(0, maps)]), (w_par, w.at[pl.ds(maps, maps)]), (d_own, wd)], sems)
    for slot in order[1:]:
        loads[slot].start()
    late = [move(tokens_in, tokens), move(hidden_grad_in, hidden_grad)]
    sender.meet(others, flips)
    early_width = early_sum.shape[1]

    def early_span(place):
        return pl.ds(pl.multiple_of(place * early_width, early_width), early_width)

    def early(flip, place):
        pair = (early_sems.at[0, flip], early_sems.at[1, flip])
        return sender.copy(early_sum, early_main.at[:, early_span(place)], pair, 0, flip)

    for flip in flips:
        early(flip, sender.place).start()
    early_main[:, early_span(sender.place)] = early_sum[...]
    sums = reduce_stages(sender, count, parts, landed, reduce_sems)
    small = sender.copy(qb, qb_par, (small_sems.at[0, 0], small_sems.at[1, 0]), 1)
    small.start()
    keeps, sends = {}, {}
    for slot in order:
        for h, mask in enumerate(slots[slot]):
            at = pl.ds(h * half, half)
            send = sender.copy(
                grads.at[mask ^ 1, at],
                b_par.at[slot, at],
                (par_sems.at[0, slot, h], par_sems.at[1, slot, h]),
                1,
            )
            keep = pltpu.make_async_copy(
                grads.at[mask, at], b_own.at[slot, at], own_sems.at[slot, h]
            )
            send.start()
            keep.start()
            sends.setdefault(slot, []).append(send)
            keeps.setdefault(slot, []).append(keep)
    first_t = qa[...].reshape(maps * rank, features).astype(BF16)
    second_own[...] = jnp.zeros_like(second_own)
    second_par[...] = jnp.zeros_like(second_par)
    small.wait_recv()
    for s in range(maps):
        at, lanes = pl.ds(s * rank, rank), pl.ds(s * width, width)
        second_own[at, lanes] = (2.0 * qb[s]).astype(BF16)
        second_par[at, lanes] = (2.0 * qb_par[s]).astype(BF16)

    def low_rank(slot, first):
        for keep in keeps[slot]:
            keep.wait()
        arrive(sends[slot])
        loads[slot].wait()
        own, par = b_own.at[slot], b_par.at[slot]
        lows[slot] = (nt(own[...], second_own[...]) + nt(par[...], second_par[...])).astype(BF16)
        low_t = (nt(second_own[...], own[...]) + nt(second_par[...], par[...])).astype(BF16)
        lowrank_t = nt(first_t, u[slot]).astype(BF16)
        for s in range(maps):
            lanes = pl.ds(s * width, width)
            piece = lowrank_t[s * rank : (s + 1) * rank]
            own_part, par_part = 2.0 * nn(piece, own[:, lanes]), 2.0 * nn(piece, par[:, lanes])
            if first:
                g_own[s], g_par[s] = own_part, par_part
            else:
                g_own[s] += own_part
                g_par[s] += par_part
        part = nn(low_t, u[slot])
        if first:
            g_first[...] = part
        else:
            g_first[...] += part

    def input_grad(slot):
        own, par = b_own.at[slot], b_par.at[slot]
        for begin in range(0, features, TILE):
            d = pl.ds(begin, TILE)
            dx = nn(lows[slot], first_t[:, begin : begin + TILE])
            for s in range(maps):
                lanes = pl.ds(s * width, width)
                dx = dx + nt(own[:, lanes], w[s, d, :]) + nt(par[:, lanes], w[maps + s, d, :])
            parts[slot, :, d] = dx.astype(BF16)
        if slot and (count != 8 or slot == 2):
            start(sums[slot])

    low_rank(order[0], True)
    local[0].wait()
    local[1].wait()
    input_grad(order[0])
    for slot in order[1:]:
        low_rank(slot, False)

    give = sender.copy(g_par, g_landed, (small_sems.at[0, 1], small_sems.at[1, 1]), 1)
    give.start()
    factors = []
    for s in range(maps):
        norm = q_stat[s, 0:1]
        factor = -drift[s] * qmag[s : s + 1] / (norm * norm * norm)
        factors.append(factor)
        pay[s * rank : (s + 1) * rank] = (
            g_first[s * rank : (s + 1) * rank]
            + 2.0 * second_direction(qb[s] * factor, qb[s], w[s], qa[s])
        ).astype(BF16)
    at = maps * rank
    pay[at : at + rank] = jnp.broadcast_to(d_drift[...], (rank, features)).astype(BF16)
    if at + rank < pay.shape[0]:
        pay[at + rank :] = jnp.zeros_like(pay[at + rank :])
    totals = Totals(
        sender, count, depth, pay, along_in, part, group_in, block, span_sum, main, total_sems
    )
    totals.give()
    if len(order) > 2:
        input_grad(order[1])
    for slot in order[2:]:
        input_grad(slot)
    totals.add_along()
    if count == 8:
        relay(parts.at[3], landed, sums)
    give.wait_recv()
    for s in range(maps):
        own_line[0, s * rank : (s + 1) * rank] = (
            g_own[s] + g_landed[s] + 2.0 * q_stat[s, 8 : 8 + rank] * factors[s]
        ).astype(BF16)
    magnitudes = [drift[s] / q_stat[s, 0:1] for s in range(maps)]
    magnitudes = jnp.concatenate(magnitudes + [jnp.zeros((rank - maps, width), F32)], axis=0)
    own_line[0, maps * rank :] = magnitudes.astype(BF16)
    along = [
        sender.copy(
            own_line.at[0], own_line.at[flip], (line_sems.at[0, flip], line_sems.at[1, flip]), 0, flip
        )
        for flip in flips
    ]
    start(along)
    totals.add_group()
    if count == 8:
        start(sums[1])
    arrive(along)
    own_total[...] = along_total(sender, depth, own_line)
    totals.group()
    totals.share()
    for flip in flips:
        early(flip, sender.place ^ flip).wait_recv()
    gu_total[...] = early_main[0 : 2 * rank].astype(F32)
    d_sums = early_main[2 * rank : 4 * rank].astype(F32)
    o_upper[...] = early_main[4 * rank : 5 * rank].astype(F32)
    o_mag_grad[...] = early_main[5 * rank : 6 * rank].astype(F32)[:1] / r_stat[0, 0:1]
    o_total[...] = early_main[
        6 * rank : 7 * rank, pl.ds(pl.multiple_of(sender.me * width, width), width)
    ].astype(F32)
    totals.take()
    first_grad[...] = main[0 : maps * rank].astype(F32)
    total_drift = main[maps * rank : (maps + 1) * rank].astype(F32)[:1]
    norm = r_stat[1, 0:1]
    factor = -total_drift * d_mag[...] / (norm * norm * norm)
    d_mag_grad[...] = total_drift / norm
    upper[...] = d_sums[0:rank] + (2.0 / depth) * d_sums[rank:] * factor
    local[2].wait()
    lower[...] = side_total[2 * rank : 3 * rank] + 2.0 * second_direction(
        db[...] * factor, db[...], wd[...], da[...]
    )

    def out(d, value, carry):
        dx_sum[:, d] = value
        return carry

    lax.fori_loop(0, features // TILE, finish_reduce(count, parts.at[0], landed, sums, out), 0)
    for copy in late:
        copy.wait()
    scale, back = norm_statistics(
        lambda d: tokens[:, d].astype(F32), lambda d: dx_sum[:, d] * gain[:, d], features, rows
    )

    def rows_grad(step, carry):
        d = pl.ds(pl.multiple_of(step * TILE, TILE), TILE)
        tokens_grad[:, d] = (
            hidden_grad[:, d] + scale * (dx_sum[:, d] * gain[:, d]) - tokens[:, d].astype(F32) * back
        )
        return carry

    lax.fori_loop(0, features // TILE, rows_grad, 0)
    last = move(tokens_grad, tokens_grad_out)
    totals.end()
    totals.end_share()
    for flip in flips:
        early(flip, sender.place).wait_send()
    last.wait()
    leave(along + [small, give])
    leave_stages(sums)
    leave_stages(sends)


def qkv_backward(grads, u_all, w_own, w_par, d_own, small):
    count, rows, _ = grads.shape
    depth = lax.axis_size("dp")
    slots = count // 2
    maps, features, width = w_own.shape
    qb = small[1]
    rank = qb.shape[1]
    ranks = maps * rank
    units = d_own.shape[0]
    many = pltpu.VMEM((slots, rows, features), BF16)
    return call(
        functools.partial(qkv_backward_body, count, depth),
        "qkv_backward",
        (
            shape((rows, features), F32),
            shape((ranks, features), F32),
            shape((ranks + rank, width), F32),
            shape((rank, features), F32),
            shape((rank, units), F32),
            shape((1, features), F32),
            shape((2 * rank, features), F32),
            shape((rank, features), F32),
            shape((1, features), F32),
            shape((rank, width), F32),
        ),
        [ANY] * 5 + [VMEM] * (len(small) - 3) + [ANY, VMEM, ANY],
        (ANY,) + (VMEM,) * 9,
        [
            many,
            pltpu.VMEM((2 * maps, features, width), BF16),
            pltpu.VMEM((units, features), BF16),
            pltpu.VMEM((slots, rows, maps * width), BF16),
            pltpu.VMEM((slots, rows, maps * width), BF16),
            many,
            many,
            pltpu.VMEM((ranks, maps * width), BF16),
            pltpu.VMEM((ranks, maps * width), BF16),
            pltpu.VMEM(qb.shape, F32),
            pltpu.VMEM((ranks, features), F32),
            pltpu.VMEM(qb.shape, F32),
            pltpu.VMEM(qb.shape, F32),
            pltpu.VMEM(qb.shape, F32),
            pltpu.VMEM((depth, ranks + rank, width), BF16),
            pltpu.VMEM((slots, rows, ranks), BF16),
            pltpu.VMEM((rows, features), F32),
            pltpu.VMEM((rows, features), BF16),
            pltpu.VMEM((rows, features), F32),
            pltpu.VMEM((rows, features), F32),
        ]
        + totals_scratch(ranks + rank, features, count, depth)
        + [
            pltpu.VMEM((8 * rank, features), BF16),
            DMA((2, depth)),
            DMA((3,)),
            DMA((3,)),
            DMA((slots,)),
            DMA((slots, 2)),
            DMA((2, slots, 2)),
            DMA((2, slots, 2)),
            DMA((2, 2)),
            DMA((2, depth)),
        ],
        4 * slots * rows * features * maps * width,
        8 * features * maps * width,
        (grads, u_all, w_own, w_par, d_own, *small),
        5,
    )


def results_body(
    maps, first, own, upper, o_mag, gu, side, o_first, d_upper, d_lower, d_mag,
    first_out, second_out, mag_out, o_first_out, upper_out, o_mag_out, gu_first_out, gu_second_out, gu_mag_out,
    d_lower_out, d_upper_out, d_mag_out,
):
    rank = upper.shape[0]
    for s in range(maps):
        at = pl.ds(s * rank, rank)
        first_out[s] = first[at]
        second_out[s] = own[at]
    for s in range(2):
        at = pl.ds(s * rank, rank)
        gu_first_out[s] = gu[at]
        gu_second_out[s] = side[at]
    mag_out[...] = own[maps * rank : maps * rank + maps]
    gu_mag_out[...] = side[3 * rank : 3 * rank + 2]
    o_first_out[...] = o_first[...]
    upper_out[...] = upper[...]
    o_mag_out[...] = o_mag[...]
    d_lower_out[...] = d_lower[...]
    d_upper_out[...] = d_upper[...]
    d_mag_out[...] = d_mag[...]


def results(maps, values):
    first, own, upper, o_mag, gu, side, o_first, d_upper, d_lower, d_mag = values
    rank, features = upper.shape
    units, width = side.shape[1], own.shape[1]
    return pl.pallas_call(
        functools.partial(results_body, maps),
        name="results",
        out_shape=(
            shape((maps, rank, features), F32),
            shape((maps, rank, width), F32),
            shape((maps, width), F32),
            shape(o_first.shape, F32),
            shape(upper.shape, F32),
            shape(o_mag.shape, F32),
            shape((2, rank, features), F32),
            shape((2, rank, units), F32),
            shape((2, units), F32),
            shape(d_lower.shape, F32),
            shape(d_upper.shape, F32),
            shape(d_mag.shape, F32),
        ),
        in_specs=[VMEM] * len(values),
        out_specs=(VMEM,) * 12,
    )(*values)


def rope_tables(total):
    half = HDIM // 2
    frequency = np.exp(-np.log(ROPE_THETA) * np.arange(half) / half)
    angles = np.arange(total)[:, None] * frequency[None, :]
    cosine, sine = np.cos(angles), np.sin(angles)
    return (
        jnp.asarray(np.concatenate([cosine, cosine], axis=1), F32),
        jnp.asarray(np.concatenate([-sine, sine], axis=1), F32),
    )


def body(
    tokens,
    attn_gain,
    ffn_gain,
    qkv_base,
    qkv_first,
    qkv_second,
    qkv_magnitude,
    output_frozen_weight,
    output_first,
    output_upper_map,
    output_magnitude,
    gate_up_base,
    gate_up_first,
    gate_up_second,
    gate_up_magnitude,
    down_frozen_weight,
    down_first,
    down_upper_map,
    down_magnitude,
    lengths,
    cotangent,
):
    rows, features = tokens.shape
    total = rows * lax.axis_size("tensor")
    rank = qkv_first.shape[2]
    units = down_frozen_weight.shape[0]
    cosine, sine = rope_tables(total)
    qkv_first_t = jnp.swapaxes(qkv_first, 1, 2)
    gu_first_t = jnp.swapaxes(gate_up_first, 1, 2)
    gu_base_t = jnp.swapaxes(gate_up_base, 1, 2)
    out_first_t = output_first.T
    down_first_t = down_first.T
    out_mag, down_mag = output_magnitude[None], down_magnitude[None]

    blocks, normed_all, qkv_other, gu_other, down_other, out_parts, at_all, q_stat, g_stat, r_stat, upstream = project(
        lengths,
        tokens,
        attn_gain[None],
        cotangent,
        qkv_base,
        gu_base_t,
        down_frozen_weight,
        output_frozen_weight,
        (
            qkv_first_t,
            qkv_second,
            qkv_magnitude,
            gu_first_t,
            gate_up_second,
            gate_up_magnitude,
            out_first_t,
            output_upper_map,
            down_first_t,
            down_upper_map,
        ),
    )
    attended, logsum, joined, out_weight, hidden, out_before, ffn_normed, out_lowrank, cot_some = attend_forward(
        lengths, q_stat, cosine, sine, blocks, out_parts, at_all, output_upper_map, out_mag, r_stat, tokens,
        ffn_gain[None], upstream,
    )
    down_all, ffn_normed_grad, gu_first_part, side, down_second_part = ffn(
        ffn_normed, upstream, cot_some, gu_base_t, gu_other, down_frozen_weight, down_other,
        (
            gu_first_t, gate_up_second, gate_up_magnitude, down_first_t, down_upper_map, g_stat, r_stat,
            down_mag,
        ),
    )
    (
        head_grads, qkv_drift, hidden_grad, result, down_drift, early_sum, side_total,
    ) = attend_backward(
        blocks,
        features,
        rank,
        units,
        (
            lengths, q_stat, cosine, sine, blocks, attended, logsum, joined, out_weight, at_all,
            output_upper_map, out_mag, r_stat, hidden, out_before, out_lowrank, upstream,
            ffn_normed_grad, ffn_gain[None], down_mag, down_all, gu_first_part, down_second_part, side,
        ),
    )
    (
        tokens_grad, qkv_first_grad, own_total, down_upper_gradient, down_lower_gradient, down_magnitude_grad,
        gate_up_first_grad, output_upper_gradient, output_magnitude_grad, output_first_grad,
    ) = qkv_backward(
        head_grads, normed_all, qkv_base, qkv_other, down_frozen_weight,
        (
            qkv_first_t, qkv_second, qkv_magnitude, q_stat, qkv_drift, r_stat, down_first_t,
            down_upper_map, down_mag, early_sum, down_drift, side_total, tokens, attn_gain[None],
            hidden_grad,
        ),
    )
    (
        qkv_first_grad, qkv_second_grad, qkv_magnitude_grad, output_first_grad, output_upper_gradient,
        output_magnitude_grad, gate_up_first_grad, gate_up_second_grad, gate_up_magnitude_grad,
        down_lower_gradient, down_upper_gradient, down_magnitude_grad,
    ) = results(
        3,
        (
            qkv_first_grad, own_total, output_upper_gradient, output_magnitude_grad, gate_up_first_grad, side_total,
            output_first_grad, down_upper_gradient, down_lower_gradient, down_magnitude_grad,
        ),
    )
    return (
        result,
        tokens_grad,
        jnp.swapaxes(qkv_first_grad, 1, 2),
        qkv_second_grad,
        qkv_magnitude_grad,
        output_first_grad.T,
        output_upper_gradient,
        output_magnitude_grad[0],
        jnp.swapaxes(gate_up_first_grad, 1, 2),
        gate_up_second_grad,
        gate_up_magnitude_grad,
        down_lower_gradient.T,
        down_upper_gradient,
        down_magnitude_grad[0],
    )


def solution(mesh):
    placed = (
        P(("dp", "tensor"), None),
        P(),
        P(),
        P(None, None, "tensor"),
        P(),
        P(None, None, "tensor"),
        P(None, "tensor"),
        P("tensor", None),
        P("tensor", None),
        P(),
        P(),
        P(None, None, "tensor"),
        P(),
        P(None, None, "tensor"),
        P(None, "tensor"),
        P("tensor", None),
        P("tensor", None),
        P(),
        P(),
        P("dp"),
        P(("dp", "tensor"), None),
    )
    return jax.shard_map(
        body,
        mesh=mesh,
        in_specs=placed,
        out_specs=(
            P(("dp", "tensor"), None),
            P(("dp", "tensor"), None),
            P(),
            P(None, None, "tensor"),
            P(None, "tensor"),
            P("tensor", None),
            P(),
            P(),
            P(),
            P(None, None, "tensor"),
            P(None, "tensor"),
            P("tensor", None),
            P(),
            P(),
        ),
        check_vma=False,
    )
```

```python
import functools

import jax
import jax.numpy as jnp
import numpy as np
from jax import lax
from jax.experimental import pallas as pl
from jax.experimental.pallas import tpu as pltpu
from jax.sharding import PartitionSpec as P

HDIM = 128
F32 = jnp.float32
BF16 = jnp.bfloat16
EXACT = lax.Precision.HIGHEST
NORM_EPS = 1e-05
ROPE_THETA = 10000.0
MASKED = -1e30
SOFTMAX_SCALE = HDIM**-0.5
LOG2E = 1.4426950408889634
VMEM_LIMIT = 60 * 2**20
TILE = 256
ANY = pl.BlockSpec(memory_space=pl.ANY)
VMEM = pl.BlockSpec(memory_space=pltpu.VMEM)
SMEM = pl.BlockSpec(memory_space=pltpu.SMEM)
MESH = pl.DeviceIdType.MESH
DMA = pltpu.SemaphoreType.DMA


def nn(left, right, precision=None):
    return jnp.dot(left, right, preferred_element_type=F32, precision=precision)


def nt(left, right, precision=None):
    return lax.dot_general(
        left, right, (((1,), (1,)), ((), ())), preferred_element_type=F32, precision=precision
    )


def tn(left, right):
    return lax.dot_general(left, right, (((0,), (0,)), ((), ())), preferred_element_type=F32)


def both_ways(value):
    return value.astype(BF16), jnp.transpose(value).astype(BF16)


def shape(dims, dtype):
    return jax.ShapeDtypeStruct(dims, dtype)


def tiles(size):
    return [(begin, min(TILE, size - begin)) for begin in range(0, size, TILE)]


def slots_of(count):
    if count == 8:
        return [(0, 0), (2, 4), (6, 6), (4, 2)]
    return [(mask, mask) for mask in range(0, count, 2)]


class Sender:
    def __init__(self):
        self.place = lax.axis_index("dp")
        self.me = lax.axis_index("tensor")

    def meet(self, masks, places=()):
        barrier = pltpu.get_barrier_semaphore()
        for mask in masks:
            pl.semaphore_signal(
                barrier, inc=1, device_id=(self.place, self.me ^ mask), device_id_type=MESH
            )
        for place in places:
            pl.semaphore_signal(
                barrier, inc=1, device_id=(self.place ^ place, self.me), device_id_type=MESH
            )
        pl.semaphore_wait(barrier, len(masks) + len(places))

    def copy(self, source, target, sems, mask, flip=0, step=0):
        place = self.place ^ flip if flip else self.place + step if step else self.place
        return pltpu.make_async_remote_copy(
            src_ref=source,
            dst_ref=target,
            send_sem=sems[0],
            recv_sem=sems[1],
            device_id=(place, self.me ^ mask if mask else self.me),
            device_id_type=MESH,
        )


def gather_stages(sender, count, own, slots, sems, begin=1, end=None):
    half = own.shape[0] // 2

    def rows(ref, slot, h):
        return ref.at[slot, pl.ds(h * half, half)]

    def message(slot, h, source, mask):
        return sender.copy(
            source, rows(slots, slot, h), (sems.at[0, slot, h], sems.at[1, slot, h]), mask
        )

    mine = [own.at[pl.ds(h * half, half)] for h in range(2)]
    if count != 8:
        stages = range(begin, end or count // 2)
        return {s: [message(s, h, mine[h], 2 * s) for h in range(2)] for s in stages}
    routes = {
        1: [(mine[0], 2), (mine[1], 4)],
        2: [(rows(slots, 1, 0), 4), (rows(slots, 1, 1), 2)],
        3: [(mine[0], 4), (mine[1], 2)],
    }
    return {s: [message(s, h, *routes[s][h]) for h in range(2)] for s in range(begin, end or 4)}


def reduce_stages(sender, count, parts, landed, sems, last=3, begin=1, end=4):
    half = parts.shape[1] // 2

    def message(slot, h, mask):
        at = pl.ds(h * half, half)
        return sender.copy(
            parts.at[last if slot == 3 and count == 8 else slot, at], landed.at[slot, at], (sems.at[0, slot, h], sems.at[1, slot, h]), mask
        )

    if count != 8:
        return {s: [message(s, h, 2 * s) for h in range(2)] for s in range(1, count // 2)}
    routes = {1: (2, 4), 2: (2, 4), 3: (4, 2)}
    return {s: [message(s, h, routes[s][h]) for h in range(2)] for s in range(begin, end)}


def relay(part, landed, sums):
    arrive(sums[2])
    part[...] = (part[...].astype(F32) + landed[2].astype(F32)).astype(BF16)
    start(sums[3])


def finish_reduce(count, part, landed, sums, out):
    slots = count // 2
    added = (1, 3) if count == 8 else tuple(range(1, slots))
    for slot in added:
        arrive(sums[slot])

    def columns(step, carry):
        d = pl.ds(pl.multiple_of(step * TILE, TILE), TILE)
        total = part[:, d].astype(F32)
        for slot in added:
            total = total + landed[slot, :, d].astype(F32)
        return out(d, total, carry)

    return columns


def leave_stages(sums):
    for copies in sums.values():
        leave(copies)


def norm_statistics(values_of, grads_of, features, rows):
    def columns(step, carry):
        squares, products = carry
        d = pl.ds(pl.multiple_of(step * TILE, TILE), TILE)
        values = values_of(d)
        squares = squares + jnp.sum(values * values, axis=1, keepdims=True)
        products = products + jnp.sum(values * grads_of(d), axis=1, keepdims=True)
        return squares, products

    zero = jnp.zeros((rows, 1), F32)
    squares, products = lax.fori_loop(0, features // TILE, columns, (zero, zero))
    scale = lax.rsqrt(squares * (1.0 / features) + NORM_EPS)
    return scale, products * (1.0 / features) * scale * scale * scale


class Totals:
    def __init__(self, sender, count, depth, pay, along_in, part, group_in, block, span, main, sems):
        self.sender, self.count, self.depth = sender, count, depth
        self.pay, self.along_in, self.part, self.group_in = pay, along_in, part, group_in
        self.block, self.whole, self.main, self.sems = block, span, main, sems
        self.others, self.flips = range(1, count), range(1, depth)
        self.width = part.shape[1]
        self.height, self.length = block.shape
        self.high = part.shape[0] // self.height
        self.place = sender.place

    def columns(self, place):
        return pl.ds(pl.multiple_of(place * self.width, self.width), self.width)

    def block_of(self, ref, index):
        row = lax.rem(index, self.high) * self.height
        lane = lax.div(index, self.high) * self.length
        return ref.at[
            pl.ds(pl.multiple_of(row, self.height), self.height),
            pl.ds(pl.multiple_of(lane, self.length), self.length),
        ]

    def pair(self, step, which):
        return self.sems.at[0, step, which], self.sems.at[1, step, which]

    def to_place(self, flip):
        source = self.pay.at[:, self.columns(self.place ^ flip)]
        return self.sender.copy(source, self.along_in.at[flip], self.pair(0, flip), 0, flip)

    def to_owner(self, mask):
        source = self.block_of(self.part, self.sender.me ^ mask)
        return self.sender.copy(source, self.group_in.at[mask], self.pair(1, mask), mask)

    def to_group(self, mask, index):
        return self.sender.copy(self.block, self.block_of(self.whole, index), self.pair(2, mask), mask)

    def to_all(self, flip, place):
        return self.sender.copy(self.whole, self.main.at[:, self.columns(place)], self.pair(3, flip), 0, flip)

    def give(self):
        for flip in self.flips:
            self.to_place(flip).start()

    def add_along(self):
        total = self.pay[:, self.columns(self.place)].astype(F32)
        for flip in self.flips:
            self.to_place(flip).wait_recv()
            total = total + self.along_in[flip].astype(F32)
        self.part[...] = total.astype(BF16)
        for mask in self.others:
            self.to_owner(mask).start()

    def add_group(self):
        me = self.sender.me
        total = self.block_of(self.part, me)[...].astype(F32)
        for mask in self.others:
            self.to_owner(mask).wait_recv()
            total = total + self.group_in[mask].astype(F32)
        self.block[...] = total.astype(BF16)
        for mask in self.others:
            self.to_group(mask, me).start()
        self.block_of(self.whole, me)[...] = self.block[...]

    def group(self):
        for mask in self.others:
            self.to_group(mask, self.sender.me ^ mask).wait_recv()

    def share(self):
        for flip in self.flips:
            self.to_all(flip, self.place).start()
        self.main[:, self.columns(self.place)] = self.whole[...]

    def take(self):
        for flip in self.flips:
            self.to_all(flip, self.place ^ flip).wait_recv()

    def end(self):
        for flip in self.flips:
            self.to_place(flip).wait_send()
        for mask in self.others:
            self.to_owner(mask).wait_send()
            self.to_group(mask, self.sender.me).wait_send()

    def end_share(self):
        for flip in self.flips:
            self.to_all(flip, self.place).wait_send()


def along_total(sender, depth, ref):
    total = ref[sender.place].astype(F32)
    for index in range(1, depth):
        total = total + ref[sender.place ^ index].astype(F32)
    return total


def totals_scratch(rows, features, count, depth):
    height = 16
    width = features // depth
    if width * (rows // height) // count < HDIM:
        rows = 8 * height
    length = width * rows // height // count
    return [
        pltpu.VMEM((rows, features), BF16),
        pltpu.VMEM((depth, rows, width), BF16),
        pltpu.VMEM((rows, width), BF16),
        pltpu.VMEM((count, height, length), BF16),
        pltpu.VMEM((height, length), BF16),
        pltpu.VMEM((rows, width), BF16),
        pltpu.VMEM((rows, features), BF16),
        DMA((2, 4, max(count, depth))),
    ]


class Mover:
    def __init__(self, sems):
        self.sems, self.many = sems, 0

    def __call__(self, source, target):
        copy = pltpu.make_async_copy(source, target, self.sems.at[self.many])
        self.many += 1
        copy.start()
        return copy


def start(copies):
    for copy in copies:
        copy.start()


def arrive(copies):
    for copy in copies:
        copy.wait_recv()


def leave(copies):
    for copy in copies:
        copy.wait_send()


def start_all(pairs, sems):
    copies = []
    for at, (source, target) in enumerate(pairs):
        copy = pltpu.make_async_copy(source, target, sems.at[at])
        copy.start()
        copies.append(copy)
    return copies


def call(body, name, out_shape, in_specs, out_specs, scratch, flops, moved, operands, identity):
    return pl.pallas_call(
        body,
        name=name,
        out_shape=out_shape,
        in_specs=in_specs,
        out_specs=out_specs,
        scratch_shapes=scratch,
        compiler_params=pltpu.CompilerParams(
            vmem_limit_bytes=VMEM_LIMIT, collective_id=identity, has_side_effects=True
        ),
        cost_estimate=pl.CostEstimate(flops=flops, bytes_accessed=moved, transcendentals=0),
    )(*operands)


def split(value):
    high = value.astype(BF16)
    return high, (value - high.astype(F32)).astype(BF16)


def left_stack(value):
    high, low = split(value)
    return jnp.concatenate([high, high, low], axis=0)


def right_stack(value):
    high, low = split(value)
    return jnp.concatenate([high, low, high], axis=0)


def first_direction(wide, first_t, second):
    rank = second.shape[0]
    gram = nt(first_t, first_t, EXACT)
    return wide[:rank] + wide[rank:] + 2.0 * nn(gram, second, EXACT)


def second_direction(factored, second, base, first_t):
    rank = second.shape[0]
    wide = nt(jnp.concatenate(split(factored), axis=0), base)
    gram = nt(factored, second, EXACT)
    return wide[:rank] + wide[rank:] + 2.0 * nn(gram, first_t, EXACT)


def line_forward(sender, depth, source, target, part, back, sems):
    place, last = sender.place, depth - 1

    def rows(ref, at):
        return ref.at[pl.ds(1, 3), pl.ds(pl.multiple_of(at * part, part), part)]

    def sends(act):
        @pl.when((place >= back) & (place < last))
        def _():
            at = place - back
            act(sender.copy(rows(source, at), rows(target, at), (sems.at[0, 0], sems.at[1, 0]), 0, 0, 1))

        @pl.when((place <= last - back) & (place > 0))
        def _():
            at = place + back
            act(sender.copy(rows(source, at), rows(target, at), (sems.at[0, 1], sems.at[1, 1]), 0, 0, -1))

    def arrivals(act):
        @pl.when(place > back)
        def _():
            at = place - back - 1
            act(sender.copy(rows(target, at), rows(target, at), (sems.at[0, 0], sems.at[1, 0]), 0, 0, -1))

        @pl.when(place < last - back)
        def _():
            at = place + back + 1
            act(sender.copy(rows(target, at), rows(target, at), (sems.at[0, 1], sems.at[1, 1]), 0, 0, 1))

    return sends, arrivals


def project_body(
    count, depth, lengths, tokens, gain, cot_in, w_own, gu_own, d_own, o_own,
    qa, qb, qmag, ga, gb, gmag, oa, ob, da, db,
    heads, rows_all, w_par, gu_par, d_par, wq, at_all, q_stat, g_stat, r_stat, upstream_out,
    cot, upstream, u, w, wgu, wd, wo, to_par, to_own, second_own, second_par, b_par, sq_all,
    sems, gather_sems, par_sems, head_sems, own_sems, weight_sems, piece_sems, line_sems, small_sems,
):
    sender = Sender()
    slots = slots_of(count)
    maps, _, width = w_own.shape
    rows, features = tokens.shape
    half = rows // 2
    units = d_own.shape[0]
    rank = qb.shape[1]
    shared = count == 8 and depth == 4
    heights = o_own.shape[0]
    part = heights // depth if shared else heights
    others = list(range(1, count))
    sender.meet(others, range(1, depth) if shared else ())

    stages = gather_stages(sender, count, u.at[0], u, gather_sems)
    weights = [
        sender.copy(source, target, (weight_sems.at[0, at], weight_sems.at[1, at]), 1)
        for at, (source, target) in enumerate(
            ((w_own, w_par), (qb, b_par), (gu_own, gu_par), (d_own, d_par))
        )
    ]
    start(weights)
    pieces = []
    for slot in (1, 2) if shared else range(1, count // 2):
        at = pl.ds(pl.multiple_of(sender.place * part, part), part) if shared else pl.ds(0, heights)
        pieces.append(
            sender.copy(
                o_own.at[at], wq.at[slot, at], (piece_sems.at[0, slot], piece_sems.at[1, slot]), 2 * slot
            )
        )
    start(pieces)
    across = []
    if shared:
        for h, (slot, mask) in enumerate(((1, 4), (2, 2))):
            half_part = part // 2
            begin = pl.multiple_of(sender.place * part + h * half_part, half_part)
            at = pl.ds(begin, half_part)
            across.append(
                sender.copy(
                    wq.at[slot, at],
                    wq.at[3, at],
                    (piece_sems.at[0, 3 * h], piece_sems.at[1, 3 * h]),
                    mask,
                )
            )
    smalls = [
        sender.copy(
            oa, at_all.at[mask], (small_sems.at[0, 0, mask], small_sems.at[1, 0, mask]), mask
        )
        for mask in others
    ]
    start(smalls)
    at_all[0] = oa[...]
    local = start_all(
        [(w_own, w.at[pl.ds(0, maps)]), (d_own, wd), (o_own, wo), (gu_own, wgu), (o_own, wq.at[0])]
        + [(cot_in, cot)],
        sems,
    )
    squares = jnp.zeros((rows, 1), F32)
    for begin in range(0, features, TILE):
        values = tokens[:, pl.ds(begin, TILE)].astype(F32)
        squares = squares + jnp.sum(values * values, axis=1, keepdims=True)
    scale = lax.rsqrt(squares * (1.0 / features) + NORM_EPS)
    for begin in range(0, features, TILE):
        d = pl.ds(begin, TILE)
        u[0, :, d] = (tokens[:, d].astype(F32) * scale * gain[:, d]).astype(BF16)
    if shared:
        arrive(pieces)
        start(across)
    start(stages[1])
    if count != 8:
        for slot in range(2, len(slots)):
            start(stages[slot])
    second_own[...] = jnp.zeros_like(second_own)
    second_par[...] = jnp.zeros_like(second_par)
    for s in range(maps):
        second_own[pl.ds(s * rank, rank), pl.ds(s * width, width)] = (2.0 * qb[s]).astype(BF16)
    first_t = qa[...].reshape(maps * rank, features).astype(BF16)
    local[0].wait()
    pending, sent = [], []

    def one_slot(slot):
        masks = slots[slot]
        keep = pltpu.make_async_copy(u.at[slot], rows_all.at[slot], own_sems.at[slot])
        keep.start()
        pending.append(keep)
        lowrank = nt(u[slot], first_t).astype(BF16)
        for s in range(maps):
            lanes = pl.ds(s * width, width)
            to_own[slot, :, lanes] = (nn(u[slot], w[s]) + nn(lowrank, second_own[:, lanes])).astype(BF16)
        if slot == 0:
            arrive(weights[:2])
            load = pltpu.make_async_copy(w_par, w.at[pl.ds(maps, maps)], sems.at[6])
            load.start()
            for s in range(maps):
                second_par[pl.ds(s * rank, rank), pl.ds(s * width, width)] = (2.0 * b_par[s]).astype(BF16)
            load.wait()
        for s in range(maps):
            lanes = pl.ds(s * width, width)
            to_par[slot, :, lanes] = (
                nn(u[slot], w[maps + s]) + nn(lowrank, second_par[:, lanes])
            ).astype(BF16)
        for h, mask in enumerate(masks):
            at = pl.ds(h * half, half)
            keep = pltpu.make_async_copy(
                to_own.at[slot, at], heads.at[mask, at], head_sems.at[slot, h]
            )
            send = sender.copy(
                to_par.at[slot, at],
                heads.at[mask ^ 1, at],
                (par_sems.at[0, slot, h], par_sems.at[1, slot, h]),
                1,
            )
            send.start()
            keep.start()
            pending.append(keep)
            sent.append(send)

    def next_slot(slot):
        arrive(stages[slot])
        if count == 8 and slot == 1:
            start(stages[2])
            start(stages[3])
        one_slot(slot)

    one_slot(0)
    place = sender.me * rows + lax.broadcasted_iota(jnp.int32, (rows, 1), 0)
    local[5].wait()
    upstream[...] = jnp.where(place < lengths[0], cot[...].astype(F32), 0.0).astype(BF16)
    masked = pltpu.make_async_copy(upstream, upstream_out, sems.at[7])
    masked.start()
    pending.append(masked)

    local[1].wait()
    local[2].wait()
    down_left, down_right = left_stack(da[...]), right_stack(db[...])
    total = jnp.zeros((1, features), F32)
    for begin, span in tiles(units):
        direction = wd[pl.ds(begin, span), :].astype(F32) + 2.0 * tn(
            down_left[:, begin : begin + span], down_right
        )
        total = total + jnp.sum(direction * direction, axis=0, keepdims=True)
    sq_all[0, 1:2, :] = total
    direction = wo[...].astype(F32) + 2.0 * tn(left_stack(oa[...]), right_stack(ob[...]))
    sq_all[0, 0:1, :] = jnp.sum(direction * direction, axis=0, keepdims=True)
    squares = [
        sender.copy(
            sq_all.at[0], sq_all.at[mask], (small_sems.at[0, 1, mask], small_sems.at[1, 1, mask]), mask
        )
        for mask in others
    ]
    start(squares)
    r_stat[0, 8 : 8 + rank] = jnp.zeros((rank, features), F32)
    r_stat[1, 8 : 8 + rank] = first_direction(
        nn(jnp.concatenate(split(da[...]), axis=0), wd[...]), da[...], db[...]
    )
    arrive(across if shared else pieces)
    if shared:
        sends0, arrivals0 = line_forward(sender, depth, wq, wq, part, 0, line_sems.at[0])
        sends1, arrivals1 = line_forward(sender, depth, wq, wq, part, 1, line_sems.at[1])
        sends0(lambda copy: copy.start())

    for s in range(maps):
        left, right = left_stack(qa[s]), right_stack(qb[s])
        total = jnp.zeros((1, width), F32)
        for begin in range(0, features, 512):
            direction = w[s, pl.ds(begin, 512), :].astype(F32) + 2.0 * tn(
                left[:, begin : begin + 512], right
            )
            total = total + jnp.sum(direction * direction, axis=0, keepdims=True)
        norm = jnp.sqrt(total)
        q_stat[s, 0:1] = norm
        q_stat[s, 1:2] = qmag[s : s + 1] / norm
        q_stat[s, 8 : 8 + rank] = first_direction(
            nn(jnp.concatenate(split(qa[s]), axis=0), w[s]), qa[s], qb[s]
        )
    next_slot(1)
    if shared:
        arrivals0(lambda copy: copy.wait_recv())
        sends1(lambda copy: copy.start())

    local[3].wait()
    ones = jnp.ones((8, HDIM), BF16)
    for s in range(2):
        left, right = left_stack(gb[s]), right_stack(ga[s])
        for begin, span in tiles(units):
            direction = wgu[s, pl.ds(begin, span), :].astype(F32) + 2.0 * tn(
                left[:, begin : begin + span], right
            )
            direction = direction * direction
            folded = direction[:, :HDIM]
            for lane in range(HDIM, features, HDIM):
                folded = folded + direction[:, lane : lane + HDIM]
            high, low = split(folded)
            norm = jnp.sqrt((nt(ones, high) + nt(ones, low))[:1])
            f = pl.ds(begin, span)
            g_stat[s, 0:1, f] = norm
            g_stat[s, 1:2, f] = gmag[s : s + 1, f] / norm
        g_stat[s, 8 : 8 + rank] = first_direction(
            nt(jnp.concatenate(split(ga[s]), axis=0), wgu[s]), ga[s], gb[s]
        )
    for slot in range(2, len(slots)):
        next_slot(slot)
    arrive(squares)
    total = jnp.zeros((2, features), F32)
    for index in range(count):
        total = total + sq_all[sender.me ^ index]
    norm = jnp.sqrt(total)
    r_stat[0, 0:1] = norm[0:1]
    r_stat[1, 0:1] = norm[1:2]

    for copy in pending:
        copy.wait()
    local[4].wait()
    arrive(sent + weights[2:] + smalls)
    leave(sent + weights + smalls + squares + pieces + across)
    for slot in range(1, len(slots)):
        leave(stages[slot])
    if shared:
        arrivals1(lambda copy: copy.wait_recv())
        sends0(lambda copy: copy.wait_send())
        sends1(lambda copy: copy.wait_send())


def project(lengths, tokens, gain, cot, w_own, gu_own, d_own, o_own, small):
    rows, features = tokens.shape
    count, depth = lax.axis_size("tensor"), lax.axis_size("dp")
    slots = count // 2
    maps, _, width = w_own.shape
    units = d_own.shape[0]
    rank = small[1].shape[1]
    return call(
        functools.partial(project_body, count, depth),
        "project",
        (
            shape((count, rows, maps * width), BF16),
            shape((slots, rows, features), BF16),
            shape(w_own.shape, BF16),
            shape(gu_own.shape, BF16),
            shape(d_own.shape, BF16),
            shape((slots, width, features), BF16),
            shape((count, rank, width), F32),
            shape((maps, 8 + rank, width), F32),
            shape((2, 8 + rank, units), F32),
            shape((2, 8 + rank, features), F32),
            shape((rows, features), BF16),
        ),
        [SMEM, VMEM, VMEM] + [ANY] * 5 + [VMEM] * len(small),
        (ANY,) * 6 + (VMEM,) * 4 + (ANY,),
        [
            pltpu.VMEM((rows, features), BF16),
            pltpu.VMEM((rows, features), BF16),
            pltpu.VMEM((slots, rows, features), BF16),
            pltpu.VMEM((2 * maps, features, width), BF16),
            pltpu.VMEM(gu_own.shape, BF16),
            pltpu.VMEM(d_own.shape, BF16),
            pltpu.VMEM(o_own.shape, BF16),
            pltpu.VMEM((slots, rows, maps * width), BF16),
            pltpu.VMEM((slots, rows, maps * width), BF16),
            pltpu.VMEM((maps * rank, maps * width), BF16),
            pltpu.VMEM((maps * rank, maps * width), BF16),
            pltpu.VMEM((maps, rank, width), F32),
            pltpu.VMEM((count, 2, features), F32),
            DMA((8,)),
            DMA((2, slots, 2)),
            DMA((2, slots, 2)),
            DMA((slots, 2)),
            DMA((slots,)),
            DMA((2, 4)),
            DMA((2, slots)),
            DMA((2, 2, 2)),
            DMA((2, 2, count)),
        ],
        4 * slots * rows * features * maps * width,
        8 * features * maps * width,
        (lengths, tokens, gain, cot, w_own, gu_own, d_own, o_own, *small),
        1,
    )


def turn(values, cosine, sine):
    return values * cosine + pltpu.roll(values, HDIM // 2, 1) * sine


def rms_scale(values):
    return lax.rsqrt(jnp.mean(values * values, axis=1, keepdims=True) + NORM_EPS)


def load_head(count, rows, h, xs, q_stat, cosine, sine, q, k, v):
    lane = pl.ds(pl.multiple_of(h * HDIM, HDIM), HDIM)
    heads = xs.shape[1] // (3 * HDIM)
    for a in range(count):
        at = pl.ds(a * rows, rows)
        cos, sin = cosine[at], sine[at]
        for part, target in enumerate((q, k, v)):
            lanes = pl.ds(pl.multiple_of((part * heads + h) * HDIM, HDIM), HDIM)
            values = xs[at, lanes].astype(F32) * q_stat[part, 1:2, lane]
            if part < 2:
                values = turn(values, cos, sin)
            target[at] = values.astype(BF16)


def attend_forward_body(
    count, depth, lengths, q_stat, cosine_in, sine_in, blocks, wq, at_all, ob, o_mag, r_stat, tokens_in, gain, grads,
    attended_out, logsum, joined_out, w_all, hidden_out, before_out, normed_out, lowrank, c_some,
    xs, q, k, v, wv, cosine, sine, tokens, attended, joined, hidden, before, normed, move_sems, sems, part_sems, line_sems, pair_sems, swap_sems, own_sems, c_sems, w_sems,
):
    sender = Sender()
    me, place = sender.me, sender.place
    length = lengths[0]
    _, rows, width = blocks.shape
    heads = width // (3 * HDIM)
    total = rows * count
    half = rows // 2
    features = ob.shape[1]
    shared = count == 8 and depth == 4
    part = wq.shape[1] // depth
    others = list(range(1, count))
    move = Mover(move_sems)
    copies = start_all(
        [
            (blocks.at[mask], xs.at[pl.ds(pl.multiple_of((me ^ mask) * rows, rows), rows)])
            for mask in range(count)
        ],
        sems,
    )
    copies = copies + [move(cosine_in, cosine), move(sine_in, sine)]
    tokens_load = move(tokens_in, tokens)
    sender.meet(others, range(1, depth) if shared else ())

    stages = gather_stages(sender, count, grads, c_some, c_sems, 1, 3)

    def rows_of(ref, at):
        return ref.at[pl.ds(1, 3), pl.ds(pl.multiple_of(at * part, part), part)]

    if shared:
        whole = pltpu.make_async_copy(wq.at[0], wv.at[0, 0], part_sems.at[depth])
        whole_pair = sender.copy(
            wq.at[0], wv.at[1, 0], (pair_sems.at[0, depth], pair_sems.at[1, depth]), 1
        )
        whole.start()
        whole_pair.start()

        def near(act, act_pair):
            for at in range(depth):

                @pl.when((place - at <= 2) & (at - place <= 2))
                def _():
                    if act is not None:
                        act(pltpu.make_async_copy(rows_of(wq, at), rows_of(wv.at[0], at), part_sems.at[at]))
                    act_pair(
                        sender.copy(
                            rows_of(wq, at), rows_of(wv.at[1], at), (pair_sems.at[0, at], pair_sems.at[1, at]), 1
                        )
                    )

        def far(act):
            for at, other in ((0, depth - 1), (depth - 1, 0)):

                @pl.when(place == other)
                def _():
                    act(
                        sender.copy(
                            rows_of(wv.at[0], at), rows_of(wv.at[1], at),
                            (pair_sems.at[0, at], pair_sems.at[1, at]), 1,
                        )
                    )

        def line_sends(act):
            @pl.when(place == 2)
            def _():
                act(
                    sender.copy(
                        rows_of(wq, 0), rows_of(wv.at[0], 0), (line_sems.at[0, 0], line_sems.at[1, 0]), 0, 0, 1
                    )
                )

            @pl.when(place == 1)
            def _():
                act(
                    sender.copy(
                        rows_of(wq, 3), rows_of(wv.at[0], 3), (line_sems.at[0, 1], line_sems.at[1, 1]), 0, 0, -1
                    )
                )

        def line_arrivals(act):
            @pl.when(place == 3)
            def _():
                act(
                    sender.copy(
                        rows_of(wv.at[0], 0), rows_of(wv.at[0], 0), (line_sems.at[0, 0], line_sems.at[1, 0]), 0, 0, -1
                    )
                )

            @pl.when(place == 0)
            def _():
                act(
                    sender.copy(
                        rows_of(wv.at[0], 3), rows_of(wv.at[0], 3), (line_sems.at[0, 1], line_sems.at[1, 1]), 0, 0, 1
                    )
                )

        near(lambda copy: copy.start(), lambda copy: copy.start())
        line_sends(lambda copy: copy.start())
    else:
        whole = pltpu.make_async_copy(wq, wv.at[0], part_sems.at[0])
        whole_pair = sender.copy(wq, wv.at[1], (pair_sems.at[0, 0], pair_sems.at[1, 0]), 1)
        whole.start()
        whole_pair.start()
    start(stages[1])

    for copy in copies:
        copy.wait()
    factor = SOFTMAX_SCALE * LOG2E
    bias = jnp.where(lax.broadcasted_iota(jnp.int32, (1, total), 1) < length, 0.0, MASKED)
    kept = lax.broadcasted_iota(jnp.int32, (rows, rows), 1) <= lax.broadcasted_iota(
        jnp.int32, (rows, rows), 0
    )

    def exchange(h, mask):
        lane = pl.ds(pl.multiple_of(h * HDIM, HDIM), HDIM)
        return sender.copy(
            attended.at[mask, :, lane],
            joined.at[mask, :, lane],
            (swap_sems.at[0, h, mask], swap_sems.at[1, h, mask]),
            mask,
        )

    def one_head(h, carry):
        load_head(count, rows, h, xs, q_stat, cosine, sine, q, k, v)
        lane = pl.ds(pl.multiple_of(h * HDIM, HDIM), HDIM)
        for a in range(count):
            at = pl.ds(a * rows, rows)
            query = q[at]
            inner = nt(query, k[at]) * factor + bias[:, a * rows : (a + 1) * rows]
            inner = jnp.where(kept, inner, MASKED)
            highest = jnp.max(inner, axis=1, keepdims=True)
            if a:
                earlier = pl.ds(0, a * rows)
                outer = nt(query, k[earlier]) * factor + bias[:, : a * rows]
                highest = jnp.maximum(highest, jnp.max(outer, axis=1, keepdims=True))
            inner = jnp.exp2(inner - highest)
            sums = jnp.sum(inner, axis=1, keepdims=True)
            result = nn(inner.astype(BF16), v[at])
            if a:
                outer = jnp.exp2(outer - highest)
                sums = sums + jnp.sum(outer, axis=1, keepdims=True)
                result = result + nn(outer.astype(BF16), v[earlier])
            attended[a ^ me, :, lane] = (result * (1.0 / sums)).astype(BF16)
            column = jnp.broadcast_to(highest + jnp.log2(sums), (rows, HDIM))
            logsum[h, :, at] = jnp.transpose(column)[:1]
        for mask in others:
            exchange(h, mask).start()
        return carry

    lax.fori_loop(0, heads, one_head, 0)
    arrive(stages[1])
    start(stages[2])
    joined[0] = attended[0]
    outs = [move(attended, attended_out)]
    if shared:
        line_arrivals(lambda copy: copy.wait_recv())
        far(lambda copy: copy.start())
        whole.wait()
        near(lambda copy: copy.wait(), lambda copy: copy.wait_recv())
        far(lambda copy: copy.wait_recv())
    else:
        whole.wait()
    arrive([whole_pair])
    keeps = start_all(
        [(wv.at[mask % 2, mask // 2], w_all.at[mask]) for mask in range(count)], w_sems
    )
    for h in range(heads):
        arrive([exchange(h, mask) for mask in others])
    outs.append(move(joined, joined_out))
    tokens_load.wait()

    low = jnp.zeros((rows, ob.shape[0]), F32)
    for mask in range(count):
        low = low + nt(joined[mask], at_all[mask].astype(BF16))
    low = low.astype(BF16)
    lowrank[...] = low

    def columns(step, squares):
        d = pl.ds(pl.multiple_of(step * TILE, TILE), TILE)
        result = nn(low, (2.0 * ob[:, d]).astype(BF16))
        for mask in range(count):
            result = result + nn(joined[mask], wv[mask % 2, mask // 2, :, d])
        before[:, d] = result.astype(BF16)
        result = tokens[:, d].astype(F32) + result * (o_mag[:, d] / r_stat[0, 0:1, d])
        hidden[:, d] = result
        return squares + jnp.sum(result * result, axis=1, keepdims=True)

    squares = lax.fori_loop(0, features // TILE, columns, jnp.zeros((rows, 1), F32))
    scale = lax.rsqrt(squares * (1.0 / features) + NORM_EPS)
    outs += [move(hidden, hidden_out), move(before, before_out)]
    normed[...] = (hidden[...] * scale * gain[...]).astype(BF16)
    outs.append(move(normed, normed_out))
    for copy in keeps + outs:
        copy.wait()
    arrive(stages[2])
    leave(stages[1] + stages[2] + [whole_pair])
    for h in range(heads):
        leave([exchange(h, mask) for mask in others])
    if shared:
        line_sends(lambda copy: copy.wait_send())
        near(None, lambda copy: copy.wait_send())
        far(lambda copy: copy.wait_send())


def attend_forward(lengths, q_stat, cosine, sine, blocks, wq, at_all, ob, o_mag, r_stat, tokens, gain, grads):
    count, rows, width = blocks.shape
    depth = lax.axis_size("dp")
    head_width = width // 3
    heads = head_width // HDIM
    total = count * rows
    features = ob.shape[1]
    slots = count // 2
    return call(
        functools.partial(attend_forward_body, count, depth),
        "attend_forward",
        (
            shape((count, rows, head_width), BF16),
            shape((heads, 1, total), F32),
            shape((count, rows, head_width), BF16),
            shape((count, head_width, features), BF16),
            shape((rows, features), F32),
            shape((rows, features), BF16),
            shape((rows, features), BF16),
            shape((rows, ob.shape[0]), BF16),
            shape((3, rows, features), BF16),
        ),
        [SMEM, VMEM, ANY, ANY, ANY, ANY] + [VMEM] * 4 + [ANY, VMEM, ANY],
        (ANY, VMEM, ANY, ANY, ANY, ANY, ANY, VMEM, ANY),
        [pltpu.VMEM((total, width), BF16)]
        + [pltpu.VMEM((total, HDIM), BF16)] * 3
        + [
            pltpu.VMEM((2, slots, head_width, features), BF16),
            pltpu.VMEM((total, HDIM), F32),
            pltpu.VMEM((total, HDIM), F32),
            pltpu.VMEM((rows, features), BF16),
            pltpu.VMEM((count, rows, head_width), BF16),
            pltpu.VMEM((count, rows, head_width), BF16),
            pltpu.VMEM((rows, features), F32),
            pltpu.VMEM((rows, features), BF16),
            pltpu.VMEM((rows, features), BF16),
            DMA((8,)),
            DMA((count,)),
            DMA((depth + 1,)),
            DMA((2, 2)),
            DMA((2, depth + 1)),
            DMA((2, heads, count)),
            DMA((1,)),
            DMA((2, 3, 2)),
            DMA((count,)),
        ],
        4 * heads * total * total * HDIM + 2 * rows * features * features,
        2 * total * width * 2,
        (lengths, q_stat, cosine, sine, blocks, wq, at_all, ob, o_mag, r_stat, tokens, gain, grads),
        2,
    )


def ffn_body(
    count, own, c_own, c_some, gu_own, gu_par, d_own, d_par,
    ga, gb, gmag, da, db, g_stat, r_stat, d_mag,
    down_all, dx_sum, g_first, side, g_down_second,
    u, c, wgu, wd, grad_low, sw, bg, down, parts, landed, second, second_par, da_par, scale_par, scale_own, d_second,
    g_second, g_down_first, drift, second_landed, first_landed, drift_landed,
    sems, down_sems, gather_sems, c_sems, reduce_sems, pair_sems,
):
    sender = Sender()
    slots = count // 2
    rows, features = own.shape
    units = d_own.shape[0]
    rank = da.shape[0]
    sender.meet([1] + list(range(2, count, 2)))
    stages = gather_stages(sender, count, own, u, gather_sems)
    c_stages = gather_stages(sender, count, c_own, c, c_sems, 3)
    sums = reduce_stages(sender, count, parts, landed, reduce_sems)
    scale_own[...] = g_stat[:, 1]
    pairs = [
        sender.copy(source, target, (pair_sems.at[0, at], pair_sems.at[1, at]), 1)
        for at, (source, target) in enumerate(((gb, second_par), (da, da_par), (scale_own, scale_par)))
    ]
    start(pairs)
    start(stages[1])
    local = start_all(
        [(own, u.at[0]), (c_own, c.at[0])]
        + [(gu_own, wgu.at[0]), (d_own, wd.at[0]), (gu_par, wgu.at[1]), (d_par, wd.at[1])]
        + [(c_some.at[slot], c.at[slot]) for slot in (1, 2)],
        sems,
    )
    if count != 8:
        for slot in range(2, slots):
            start(stages[slot])
        for slot in range(3, slots):
            start(c_stages[slot])
    first_t = ga[...].reshape(2 * rank, features).astype(BF16)
    d_scale = d_mag[...] / r_stat[1, 0:1]
    d_second[...] = (2.0 * db[...]).astype(BF16)
    second[...] = jnp.zeros_like(second)
    for part in range(2):
        second[0, part, pl.ds(part * rank, rank), :] = (2.0 * gb[part]).astype(BF16)
    arrive(pairs)
    for part in range(2):
        second[1, part, pl.ds(part * rank, rank), :] = (2.0 * second_par[part]).astype(BF16)
    da_low = (da[...].astype(BF16), da_par[...].astype(BF16))
    for ref in (g_first, g_second, g_down_first, g_down_second, drift):
        ref[...] = jnp.zeros_like(ref)
    local[0].wait()
    local[1].wait()
    rooms = down.shape[0]

    def store(slot):
        return pltpu.make_async_copy(down.at[slot % rooms], down_all.at[slot], down_sems.at[slot])

    def one_slot(slot, carry):
        room = lax.rem(slot, rooms)
        if slots > rooms:

            @pl.when(slot >= rooms)
            def _():
                store(slot - rooms).wait()

        for at in range(1, slots):

            @pl.when(slot == at)
            def _():
                if at in (1, 2):
                    local[5 + at].wait()
                else:
                    arrive(c_stages[at])

        lowrank, lowrank_t = both_ways(nt(u[slot], first_t))
        grad_low[...] = (c[slot].astype(F32) * d_scale).astype(BF16)
        d_low_grad, d_low_grad_t = both_ways(nt(grad_low[...], d_second[...]))
        d_low = jnp.zeros((rows, rank), F32)
        u_low = jnp.zeros((rows, 2 * rank), F32)
        for which, scale in enumerate((scale_own, scale_par)):

            @pl.when(slot == 0)
            def _():
                local[2 + 2 * which].wait()
                local[3 + 2 * which].wait()

            for at in range(1, slots) if which else ():

                @pl.when(slot == at - 1)
                def _():
                    arrive(stages[at])
                    if count == 8 and at == 1:
                        start(stages[2])
                        start(stages[3])
                        start(c_stages[3])

            for begin, span in tiles(units):
                f = pl.ds(begin, span)
                gate_before = nt(u[slot], wgu[which, 0, f, :]) + nn(lowrank, second[which, 0, :, f])
                up_before = nt(u[slot], wgu[which, 1, f, :]) + nn(lowrank, second[which, 1, :, f])
                gate = gate_before * scale[0:1, f]
                up = up_before * scale[1:2, f]
                sigmoid = 1.0 / (1.0 + jnp.exp(-gate))
                silu = gate * sigmoid
                swiglu = (silu * up).astype(BF16)
                swiglu_grad = nt(grad_low[...], wd[which, f, :]) + nn(
                    d_low_grad, da_low[which][:, begin : begin + span]
                )
                swiglu_grad = swiglu_grad.astype(BF16).astype(F32)
                gate_grad = swiglu_grad * up * (sigmoid * (1.0 + gate * (1.0 - sigmoid)))
                up_grad = swiglu_grad * silu
                drift[which, 0:1, f] += jnp.sum(gate_grad * gate_before, axis=0, keepdims=True)
                drift[which, 1:2, f] += jnp.sum(up_grad * up_before, axis=0, keepdims=True)
                sw[which, :, f] = swiglu
                bg[which, 0, :, f] = (gate_grad * scale[0:1, f]).astype(BF16)
                bg[which, 1, :, f] = (up_grad * scale[1:2, f]).astype(BF16)
            d_low = d_low + nt(sw[which], da_low[which])
            for part in range(2):
                u_low = u_low + nt(bg[which, part], second[which, part])
                g_second[which, part] += 2.0 * nn(
                    lowrank_t[part * rank : (part + 1) * rank], bg[which, part]
                )
            g_down_first[which] += nn(d_low_grad_t, sw[which])
        d_low, d_low_t = both_ways(d_low)
        u_low, u_low_t = both_ways(u_low)

        for begin in range(0, features, TILE):
            d = pl.ds(begin, TILE)
            dx = nn(u_low, first_t[:, begin : begin + TILE])
            for which in range(2):
                for part in range(2):
                    dx = dx + nn(bg[which, part], wgu[which, part, :, d])
            parts[slot, :, d] = dx.astype(BF16)
        for at in range(1, slots):

            @pl.when(slot == at)
            def _():
                if count == 8 and at == 3:
                    relay(parts.at[3], landed, sums)
                else:
                    start(sums[at])

        for begin in range(0, features, TILE):
            d = pl.ds(begin, TILE)
            g_first[:, d] += nn(u_low_t, u[slot, :, d])
            total = nn(sw[0], wd[0, :, d]) + nn(sw[1], wd[1, :, d]) + nn(d_low, d_second[:, d])
            down[room, :, d] = total.astype(BF16)
            g_down_second[:, d] += 2.0 * nn(d_low_t, grad_low[:, d])
        store(slot).start()
        return carry

    lax.fori_loop(0, slots, one_slot, 0)

    gives = [
        sender.copy(source, target, (pair_sems.at[0, at], pair_sems.at[1, at]), 1)
        for at, source, target in (
            (3, g_second.at[1], second_landed),
            (4, g_down_first.at[1], first_landed),
            (5, drift.at[1], drift_landed),
        )
    ]
    start(gives)
    arrive(gives)
    total_drift = drift[0] + drift_landed[...]
    side[...] = jnp.zeros_like(side)
    side[2 * rank : 3 * rank] = g_down_first[0] + first_landed[...]
    for part in range(2):
        norm = g_stat[part, 0:1]
        one = total_drift[part : part + 1]
        factor = -one * gmag[part : part + 1] / (norm * norm * norm)
        at = pl.ds(part * rank, rank)
        side[at] = g_second[0, part] + second_landed[part] + 2.0 * g_stat[part, 8 : 8 + rank] * factor
        side[3 * rank + part : 3 * rank + part + 1] = one / norm
        factored = gb[part] * factor
        wide = nn(jnp.concatenate(split(factored), axis=0), wgu[0, part])
        gram = nt(factored, gb[part], EXACT)
        g_first[at] += 2.0 * (wide[:rank] + wide[rank:] + 2.0 * nn(gram, ga[part], EXACT))

    def out(d, value, carry):
        dx_sum[:, d] = value.astype(BF16)
        return carry

    lax.fori_loop(0, features // TILE, finish_reduce(count, parts.at[0], landed, sums, out), 0)
    for slot in range(max(0, slots - rooms), slots):
        store(slot).wait()
    leave(pairs + gives)
    for copies in (sums, stages, c_stages):
        leave_stages(copies)


def ffn(own, c_own, c_some, gu_own, gu_par, d_own, d_par, small):
    rows, features = own.shape
    count = lax.axis_size("tensor")
    slots = count // 2
    units = d_own.shape[0]
    rank = small[3].shape[0]
    many = pltpu.VMEM((slots, rows, features), BF16)
    return call(
        functools.partial(ffn_body, count),
        "ffn",
        (
            shape((slots, rows, features), BF16),
            shape((rows, features), BF16),
            shape((2 * rank, features), F32),
            shape((4 * rank, units), F32),
            shape((rank, features), F32),
        ),
        [ANY] * 7 + [VMEM] * len(small),
        (ANY,) + (VMEM,) * 4,
        [
            many,
            many,
            pltpu.VMEM((2, 2, units, features), BF16),
            pltpu.VMEM((2, units, features), BF16),
            pltpu.VMEM((rows, features), BF16),
            pltpu.VMEM((2, rows, units), BF16),
            pltpu.VMEM((2, 2, rows, units), BF16),
            pltpu.VMEM((min(slots, 4), rows, features), BF16),
            many,
            many,
            pltpu.VMEM((2, 2, 2 * rank, units), BF16),
            pltpu.VMEM((2, rank, units), F32),
            pltpu.VMEM((rank, units), F32),
            pltpu.VMEM((2, units), F32),
            pltpu.VMEM((2, units), F32),
            pltpu.VMEM((rank, features), BF16),
            pltpu.VMEM((2, 2, rank, units), F32),
            pltpu.VMEM((2, rank, units), F32),
            pltpu.VMEM((2, 2, units), F32),
            pltpu.VMEM((2, rank, units), F32),
            pltpu.VMEM((rank, units), F32),
            pltpu.VMEM((2, units), F32),
            DMA((8,)),
            DMA((slots,)),
            DMA((2, slots, 2)),
            DMA((2, slots, 2)),
            DMA((2, slots, 2)),
            DMA((2, 6)),
        ],
        24 * slots * rows * features * units,
        12 * features * units,
        (own, c_own, c_some, gu_own, gu_par, d_own, d_par, *small),
        3,
    )


def attend_backward_body(
    count, depth, lengths, q_stat, cosine_in, sine_in, blocks, attended_in, logsum, joined_in, w_all, at_all, ob, o_mag,
    r_stat, hidden_in, before_in, lowrank, cot_in, dx_in, gain, d_mag, down_all, gu_first, d_second, side,
    out_all, drift, hidden_grad_out, result_out, d_drift, span_sum, side_total,
    xs, dos, q, k, v, dq, centre, wv, og, ag, parts, landed, side_line,
    cosine, sine, attended, joined, hidden, before, cot, dx_sum, out, hidden_grad, result, o_drift_row,
    pay, along_in, part, group_in, block, total_sems,
    move_sems, sems, w_sems, part_sems, swap_sems, reduce_sems, side_sems,
):
    sender = Sender()
    me = sender.me
    length = lengths[0]
    _, rows, width = blocks.shape
    heads = width // (3 * HDIM)
    total = rows * count
    features = ob.shape[1]
    rank = ob.shape[0]
    slots = count // 2
    others = list(range(1, count))
    flips = list(range(1, depth))
    order = others + [0]
    move = Mover(move_sems)
    early = [move(hidden_in, hidden), move(dx_in, dx_sum), move(cot_in, cot), move(before_in, before)]
    loads = dict(
        zip(order, start_all([(w_all.at[mask], wv.at[mask]) for mask in order], w_sems))
    )
    joined_load = move(joined_in, joined)
    late = [move(cosine_in, cosine), move(sine_in, sine), move(attended_in, attended)]
    sender.meet(others, flips)
    sums = reduce_stages(sender, count, down_all, landed, reduce_sems, end=3)
    if count == 8:
        sums.update(reduce_stages(sender, count, parts, landed, reduce_sems, 1, 3))
        start(sums[2])
    else:
        for slot in range(1, slots):
            start(sums[slot])
    copies = start_all(
        [
            (blocks.at[mask], xs.at[pl.ds(pl.multiple_of((me ^ mask) * rows, rows), rows)])
            for mask in range(count)
        ],
        sems,
    )
    kept_parts = (0, 3) if count == 8 else (0,)
    part_loads = start_all(
        [(down_all.at[slot], parts.at[at]) for at, slot in enumerate(kept_parts)], part_sems
    )

    for copy in early[:2]:
        copy.wait()
    scale, back = norm_statistics(
        lambda d: hidden[:, d], lambda d: dx_sum[:, d].astype(F32) * gain[:, d], features, rows
    )

    for copy in early[2:]:
        copy.wait()

    def rows_grad(step, carry):
        d = pl.ds(pl.multiple_of(step * TILE, TILE), TILE)
        grad = cot[:, d].astype(F32) + scale * (dx_sum[:, d].astype(F32) * gain[:, d]) - hidden[:, d] * back
        hidden_grad[:, d] = grad
        o_drift_row[:, d] = jnp.sum(grad * before[:, d].astype(F32), axis=0, keepdims=True)
        og[:, d] = (grad * (o_mag[:, d] / r_stat[0, 0:1, d])).astype(BF16)
        return carry

    lax.fori_loop(0, features // TILE, rows_grad, 0)
    outs = [move(hidden_grad, hidden_grad_out)]
    o_drift = o_drift_row[...]
    second = (2.0 * ob[...]).astype(BF16)
    low_grad = nt(og[...], second).astype(BF16)
    mine = pl.ds(pl.multiple_of(me * rows, rows), rows)

    def exchange(h, mask, at=None):
        lane = pl.ds(pl.multiple_of(h * HDIM, HDIM), HDIM)
        return sender.copy(
            ag.at[mask, :, lane],
            dos.at[mine if at is None else at, lane],
            (swap_sems.at[0, h, mask], swap_sems.at[1, h, mask]),
            mask,
        )

    def landing(h, mask):
        return exchange(h, mask, pl.ds(pl.multiple_of((me ^ mask) * rows, rows), rows))

    for mask in order:
        loads[mask].wait()
        grad = nt(og[...], wv[mask]) + nn(low_grad, at_all[mask].astype(BF16))
        if mask:
            ag[mask] = grad.astype(BF16)
            exchange(0, mask).start()
        else:
            dos[mine] = grad.astype(BF16)
    for h in range(1, heads):
        for mask in others:
            exchange(h, mask).start()

    low_grad_t = nt(second, og[...]).astype(BF16)
    norm = r_stat[0, 0:1]
    factor = -o_drift * o_mag[...] / (norm * norm * norm)
    factored = ob[...] * factor
    wide = jnp.zeros((2 * rank, features), F32)
    gram = jnp.zeros((rank, rank), F32)
    joined_load.wait()
    for mask in range(count):
        first = at_all[mask]
        span = pl.ds(pl.multiple_of((me ^ mask) * (width // 3), width // 3), width // 3)
        pay[6 * rank : 7 * rank, span] = (
            nn(low_grad_t, joined[mask]) + 2.0 * second_direction(factored, ob[...], wv[mask], first)
        ).astype(BF16)
        wide = wide + nn(jnp.concatenate(split(first), axis=0), wv[mask])
        gram = gram + nt(first, first, EXACT)
    product = wide[:rank] + wide[rank:] + 2.0 * nn(gram, ob[...], EXACT)
    pay[0 : 2 * rank] = gu_first[...].astype(BF16)
    pay[2 * rank : 3 * rank] = d_second[...].astype(BF16)
    pay[3 * rank : 4 * rank] = r_stat[1, 8 : 8 + rank].astype(BF16)
    pay[4 * rank : 5 * rank] = (
        2.0 * tn(lowrank[...], og[...]) + 2.0 * product * factor
    ).astype(BF16)
    pay[5 * rank : 6 * rank] = jnp.broadcast_to(o_drift, (rank, features)).astype(BF16)
    pay[7 * rank :] = jnp.zeros_like(pay[7 * rank :])
    totals = Totals(
        sender, count, depth, pay, along_in, part, group_in, block, span_sum, None, total_sems
    )
    totals.give()
    side_line[0] = side[...].astype(BF16)
    sides = [
        sender.copy(
            side_line.at[0], side_line.at[flip], (side_sems.at[0, flip], side_sems.at[1, flip]), 0, flip
        )
        for flip in flips
    ]
    start(sides)
    for load in part_loads:
        load.wait()
    if count == 8:
        relay(parts.at[1], landed, sums)
    for copy in copies + late:
        copy.wait()

    short = total <= 2048
    factor2 = SOFTMAX_SCALE * LOG2E
    kept = lax.broadcasted_iota(jnp.int32, (rows, rows), 0) <= lax.broadcasted_iota(
        jnp.int32, (rows, rows), 1
    )

    def one_head(h, carry):
        load_head(count, rows, h, xs, q_stat, cosine, sine, q, k, v)
        for mask in others:
            landing(h, mask).wait_recv()
        own = pl.ds(pl.multiple_of(h * HDIM, HDIM), HDIM)

        def lanes(part):
            return pl.ds(pl.multiple_of((part * heads + h) * HDIM, HDIM), HDIM)

        for a in range(count):
            at = pl.ds(a * rows, rows)
            values = dos[at, own].astype(F32) * attended[a ^ me, :, own].astype(F32)
            column = jnp.sum(values, axis=1, keepdims=True)
            centre[:, at] = jnp.transpose(jnp.broadcast_to(column, (rows, HDIM)))[:8]

        def finish(a, part, grad):
            at = pl.ds(a * rows if isinstance(a, int) else pl.multiple_of(a * rows, rows), rows)
            if part < 2:
                grad = turn(grad, cosine[at], -sine[at])
            out[a ^ me, :, lanes(part)] = (grad * q_stat[part, 1:2, own]).astype(BF16)
            return jnp.sum(grad * xs[at, lanes(part)].astype(F32), axis=0, keepdims=True)

        def pair_grads(at, after, bias, keep):
            key = k[at]
            weights = jnp.exp2(nt(key, q[after]) * factor2 + (bias - logsum[h, :, after]))
            weights = keep(weights)
            score_grad = weights * (nt(v[at], dos[after, own]) - centre[:1, after])
            score_grad = score_grad.astype(BF16)
            value_grad = nn(weights.astype(BF16), dos[after, own])
            return nn(score_grad, q[after]), value_grad, tn(score_grad, key)

        zero = jnp.zeros((1, HDIM), F32)
        iota = lax.broadcasted_iota(jnp.int32, (rows, 1), 0)
        if short:
            key_drift, value_drift = zero, zero
            for a in range(count):
                bias = jnp.where(a * rows + iota < length, 0.0, MASKED)

                def keep(weights):
                    first = jnp.where(kept, weights[:, :rows], 0.0)
                    if a == count - 1:
                        return first
                    return jnp.concatenate([first, weights[:, rows:]], axis=1)

                at, after = pl.ds(a * rows, rows), pl.ds(a * rows, total - a * rows)
                key_grad, value_grad, query_part = pair_grads(at, after, bias, keep)
                if a == 0:
                    dq[...] = query_part
                else:
                    dq[after] += query_part
                key_drift = key_drift + finish(a, 1, key_grad * SOFTMAX_SCALE)
                value_drift = value_drift + finish(a, 2, value_grad)
        else:
            dq[...] = jnp.zeros_like(dq)

            def one_block(a, drifts):
                start_at = pl.multiple_of(a * rows, rows)
                at = pl.ds(start_at, rows)
                bias = jnp.where(start_at + iota < length, 0.0, MASKED)

                def one_pair(i, grads):
                    after = pl.ds(pl.multiple_of(i * rows, rows), rows)
                    ahead = (i - a) * rows

                    def keep(weights):
                        return jnp.where(kept | (ahead > 0), weights, 0.0)

                    key_part, value_part, query_part = pair_grads(at, after, bias, keep)
                    dq[after] += query_part
                    return grads[0] + key_part, grads[1] + value_part

                none = jnp.zeros((rows, HDIM), F32)
                key_grad, value_grad = lax.fori_loop(a, count, one_pair, (none, none))
                return (
                    drifts[0] + finish(a, 1, key_grad * SOFTMAX_SCALE),
                    drifts[1] + finish(a, 2, value_grad),
                )

            key_drift, value_drift = lax.fori_loop(0, count, one_block, (zero, zero))
        query_drift = zero
        for a in range(count):
            query_drift = query_drift + finish(a, 0, dq[pl.ds(a * rows, rows)] * SOFTMAX_SCALE)
        drift[0, :, own] = query_drift
        drift[1, :, own] = key_drift
        drift[2, :, own] = value_drift

        @pl.when(h == 0)
        def _():
            totals.add_along()
            if count == 8:
                start(sums[1])

        return carry

    lax.fori_loop(0, heads, one_head, 0)
    outs.append(move(out, out_all))
    totals.add_group()
    arrive(sides)
    side_total[...] = along_total(sender, depth, side_line)

    def rows_out(d, value, carry):
        result[:, d] = (hidden[:, d] + value * (d_mag[:, d] / r_stat[1, 0:1, d])).astype(BF16)
        d_drift[:, d] = jnp.sum(cot[:, d].astype(F32) * value, axis=0, keepdims=True)
        return carry

    lax.fori_loop(0, features // TILE, finish_reduce(count, parts.at[0], landed, sums, rows_out), 0)
    outs.append(move(result, result_out))
    totals.group()
    totals.end()
    for copy in outs:
        copy.wait()
    leave(sides)
    leave_stages(sums)
    for h in range(heads):
        for mask in others:
            exchange(h, mask).wait_send()


def attend_backward(blocks, features, rank, units, operands):
    count, rows, width = blocks.shape
    depth = lax.axis_size("dp")
    head_width = width // 3
    heads = head_width // HDIM
    total = count * rows
    slots = count // 2
    many = pltpu.VMEM((slots, rows, features), BF16)
    early = totals_scratch(8 * rank, features, count, depth)
    return call(
        functools.partial(attend_backward_body, count, depth),
        "attend_backward",
        (
            shape((count, rows, width), BF16),
            shape((3, 1, head_width), F32),
            shape((rows, features), F32),
            shape((rows, features), BF16),
            shape((1, features), F32),
            shape(early[5].shape, BF16),
            shape((4 * rank, units), F32),
        ),
        [SMEM, VMEM, ANY, ANY, ANY, ANY, VMEM, ANY, ANY] + [VMEM] * 4
        + [ANY, ANY, VMEM, ANY, ANY, VMEM, VMEM, ANY] + [VMEM] * 3,
        (ANY, VMEM, ANY, ANY) + (VMEM,) * 3,
        [pltpu.VMEM((total, width), BF16), pltpu.VMEM((total, head_width), BF16)]
        + [pltpu.VMEM((total, HDIM), BF16)] * 3
        + [
            pltpu.VMEM((total, HDIM), F32),
            pltpu.VMEM((8, total), F32),
            pltpu.VMEM((count, head_width, features), BF16),
            pltpu.VMEM((rows, features), BF16),
            pltpu.VMEM((count, rows, head_width), BF16),
            pltpu.VMEM((2 if count == 8 else 1, rows, features), BF16),
            many,
            pltpu.VMEM((depth, 4 * rank, units), BF16),
            pltpu.VMEM((total, HDIM), F32),
            pltpu.VMEM((total, HDIM), F32),
            pltpu.VMEM((count, rows, head_width), BF16),
            pltpu.VMEM((count, rows, head_width), BF16),
            pltpu.VMEM((rows, features), F32),
            pltpu.VMEM((rows, features), BF16),
            pltpu.VMEM((rows, features), BF16),
            pltpu.VMEM((rows, features), BF16),
            pltpu.VMEM((count, rows, width), BF16),
            pltpu.VMEM((rows, features), F32),
            pltpu.VMEM((rows, features), BF16),
            pltpu.VMEM((1, features), F32),
        ]
        + early[:5]
        + [
            early[7],
            DMA((11,)),
            DMA((count,)),
            DMA((count,)),
            DMA((2,)),
            DMA((2, heads, count)),
            DMA((2, slots, 2)),
            DMA((2, depth)),
        ],
        10 * heads * total * total * HDIM + 2 * rows * features * features,
        2 * total * width * 4,
        operands,
        4,
    )


def qkv_backward_body(
    count, depth, grads, u_all, w_own, w_par, d_own, qa, qb, qmag, q_stat, drift, r_stat, da, db, d_mag,
    early_sum, d_drift, side_total, tokens_in, gain, hidden_grad_in,
    tokens_grad_out, first_grad, own_total, upper, lower, d_mag_grad, gu_total, o_upper, o_mag_grad, o_total,
    u, w, wd, b_own, b_par, parts, landed, second_own, second_par, qb_par, g_first, g_own, g_par, g_landed, own_line,
    lows, dx_sum, tokens, hidden_grad, tokens_grad,
    pay, along_in, part, group_in, block, span_sum, main, total_sems, early_main, early_sems,
    move_sems, sems, u_sems, own_sems, par_sems, reduce_sems, small_sems, line_sems,
):
    sender = Sender()
    slots = slots_of(count)
    order = [2, 1, 3, 0] if count == 8 else list(range(len(slots) - 1, -1, -1))
    maps, features, width = w_own.shape
    rank = qb.shape[1]
    rows = grads.shape[1]
    half = rows // 2
    others = list(range(1, count))
    flips = list(range(1, depth))
    move = Mover(move_sems)
    loads = {slot: pltpu.make_async_copy(u_all.at[slot], u.at[slot], u_sems.at[slot]) for slot in order}
    loads[order[0]].start()
    local = start_all([(w_own, w.at[pl.ds(0, maps)]), (w_par, w.at[pl.ds(maps, maps)]), (d_own, wd)], sems)
    for slot in order[1:]:
        loads[slot].start()
    late = [move(tokens_in, tokens), move(hidden_grad_in, hidden_grad)]
    sender.meet(others, flips)
    early_width = early_sum.shape[1]

    def early_span(place):
        return pl.ds(pl.multiple_of(place * early_width, early_width), early_width)

    def early(flip, place):
        pair = (early_sems.at[0, flip], early_sems.at[1, flip])
        return sender.copy(early_sum, early_main.at[:, early_span(place)], pair, 0, flip)

    sums = reduce_stages(sender, count, parts, landed, reduce_sems)
    small = sender.copy(qb, qb_par, (small_sems.at[0, 0], small_sems.at[1, 0]), 1)
    small.start()
    keeps, sends = {}, {}
    for slot in order:
        for h, mask in enumerate(slots[slot]):
            at = pl.ds(h * half, half)
            send = sender.copy(
                grads.at[mask ^ 1, at],
                b_par.at[slot, at],
                (par_sems.at[0, slot, h], par_sems.at[1, slot, h]),
                1,
            )
            keep = pltpu.make_async_copy(
                grads.at[mask, at], b_own.at[slot, at], own_sems.at[slot, h]
            )
            send.start()
            keep.start()
            sends.setdefault(slot, []).append(send)
            keeps.setdefault(slot, []).append(keep)
    for flip in flips:
        early(flip, sender.place).start()
    early_main[:, early_span(sender.place)] = early_sum[...]
    first_t = qa[...].reshape(maps * rank, features).astype(BF16)
    second_own[...] = jnp.zeros_like(second_own)
    second_par[...] = jnp.zeros_like(second_par)
    small.wait_recv()
    for s in range(maps):
        at, lanes = pl.ds(s * rank, rank), pl.ds(s * width, width)
        second_own[at, lanes] = (2.0 * qb[s]).astype(BF16)
        second_par[at, lanes] = (2.0 * qb_par[s]).astype(BF16)

    def low_rank(slot, first):
        for keep in keeps[slot]:
            keep.wait()
        arrive(sends[slot])
        loads[slot].wait()
        own, par = b_own.at[slot], b_par.at[slot]
        lows[slot], low_t = both_ways(nt(own[...], second_own[...]) + nt(par[...], second_par[...]))
        _, lowrank_t = both_ways(nt(u[slot], first_t))
        for s in range(maps):
            lanes = pl.ds(s * width, width)
            piece = lowrank_t[s * rank : (s + 1) * rank]
            own_part, par_part = 2.0 * nn(piece, own[:, lanes]), 2.0 * nn(piece, par[:, lanes])
            if first:
                g_own[s], g_par[s] = own_part, par_part
            else:
                g_own[s] += own_part
                g_par[s] += par_part
        part = nn(low_t, u[slot])
        if first:
            g_first[...] = part
        else:
            g_first[...] += part

    def input_grad(slot):
        own, par = b_own.at[slot], b_par.at[slot]
        for begin in range(0, features, TILE):
            d = pl.ds(begin, TILE)
            dx = nn(lows[slot], first_t[:, begin : begin + TILE])
            for s in range(maps):
                lanes = pl.ds(s * width, width)
                dx = dx + nt(own[:, lanes], w[s, d, :]) + nt(par[:, lanes], w[maps + s, d, :])
            parts[slot, :, d] = dx.astype(BF16)
        if slot and (count != 8 or slot == 2):
            start(sums[slot])

    low_rank(order[0], True)
    local[0].wait()
    local[1].wait()
    input_grad(order[0])
    for slot in order[1:]:
        low_rank(slot, False)

    give = sender.copy(g_par, g_landed, (small_sems.at[0, 1], small_sems.at[1, 1]), 1)
    give.start()
    factors = []
    for s in range(maps):
        norm = q_stat[s, 0:1]
        factor = -drift[s] * qmag[s : s + 1] / (norm * norm * norm)
        factors.append(factor)
        pay[s * rank : (s + 1) * rank] = (
            g_first[s * rank : (s + 1) * rank]
            + 2.0 * second_direction(qb[s] * factor, qb[s], w[s], qa[s])
        ).astype(BF16)
    at = maps * rank
    pay[at : at + rank] = jnp.broadcast_to(d_drift[...], (rank, features)).astype(BF16)
    if at + rank < pay.shape[0]:
        pay[at + rank :] = jnp.zeros_like(pay[at + rank :])
    totals = Totals(
        sender, count, depth, pay, along_in, part, group_in, block, span_sum, main, total_sems
    )
    totals.give()
    if len(order) > 2:
        input_grad(order[1])
    for slot in order[2:]:
        input_grad(slot)
    totals.add_along()
    if count == 8:
        relay(parts.at[3], landed, sums)
    give.wait_recv()
    for s in range(maps):
        own_line[0, s * rank : (s + 1) * rank] = (
            g_own[s] + g_landed[s] + 2.0 * q_stat[s, 8 : 8 + rank] * factors[s]
        ).astype(BF16)
    magnitudes = [drift[s] / q_stat[s, 0:1] for s in range(maps)]
    magnitudes = jnp.concatenate(magnitudes + [jnp.zeros((rank - maps, width), F32)], axis=0)
    own_line[0, maps * rank :] = magnitudes.astype(BF16)
    along = [
        sender.copy(
            own_line.at[0], own_line.at[flip], (line_sems.at[0, flip], line_sems.at[1, flip]), 0, flip
        )
        for flip in flips
    ]
    start(along)
    totals.add_group()
    if count == 8:
        start(sums[1])
    arrive(along)
    own_total[...] = along_total(sender, depth, own_line)
    totals.group()
    totals.share()
    for flip in flips:
        early(flip, sender.place ^ flip).wait_recv()
    gu_total[...] = early_main[0 : 2 * rank].astype(F32)
    d_sums = early_main[2 * rank : 4 * rank].astype(F32)
    o_upper[...] = early_main[4 * rank : 5 * rank].astype(F32)
    o_mag_grad[...] = early_main[5 * rank : 6 * rank].astype(F32)[:1] / r_stat[0, 0:1]
    o_total[...] = early_main[
        6 * rank : 7 * rank, pl.ds(pl.multiple_of(sender.me * width, width), width)
    ].astype(F32)
    totals.take()
    first_grad[...] = main[0 : maps * rank].astype(F32)
    total_drift = main[maps * rank : (maps + 1) * rank].astype(F32)[:1]
    norm = r_stat[1, 0:1]
    factor = -total_drift * d_mag[...] / (norm * norm * norm)
    d_mag_grad[...] = total_drift / norm
    upper[...] = d_sums[0:rank] + (2.0 / depth) * d_sums[rank:] * factor
    local[2].wait()
    lower[...] = side_total[2 * rank : 3 * rank] + 2.0 * second_direction(
        db[...] * factor, db[...], wd[...], da[...]
    )

    def out(d, value, carry):
        dx_sum[:, d] = value
        return carry

    lax.fori_loop(0, features // TILE, finish_reduce(count, parts.at[0], landed, sums, out), 0)
    for copy in late:
        copy.wait()
    scale, back = norm_statistics(
        lambda d: tokens[:, d].astype(F32), lambda d: dx_sum[:, d] * gain[:, d], features, rows
    )

    def rows_grad(step, carry):
        d = pl.ds(pl.multiple_of(step * TILE, TILE), TILE)
        tokens_grad[:, d] = (
            hidden_grad[:, d] + scale * (dx_sum[:, d] * gain[:, d]) - tokens[:, d].astype(F32) * back
        )
        return carry

    lax.fori_loop(0, features // TILE, rows_grad, 0)
    last = move(tokens_grad, tokens_grad_out)
    totals.end()
    totals.end_share()
    for flip in flips:
        early(flip, sender.place).wait_send()
    last.wait()
    leave(along + [small, give])
    leave_stages(sums)
    leave_stages(sends)


def qkv_backward(grads, u_all, w_own, w_par, d_own, small):
    count, rows, _ = grads.shape
    depth = lax.axis_size("dp")
    slots = count // 2
    maps, features, width = w_own.shape
    qb = small[1]
    rank = qb.shape[1]
    ranks = maps * rank
    units = d_own.shape[0]
    many = pltpu.VMEM((slots, rows, features), BF16)
    return call(
        functools.partial(qkv_backward_body, count, depth),
        "qkv_backward",
        (
            shape((rows, features), F32),
            shape((ranks, features), F32),
            shape((ranks + rank, width), F32),
            shape((rank, features), F32),
            shape((rank, units), F32),
            shape((1, features), F32),
            shape((2 * rank, features), F32),
            shape((rank, features), F32),
            shape((1, features), F32),
            shape((rank, width), F32),
        ),
        [ANY] * 5 + [VMEM] * (len(small) - 3) + [ANY, VMEM, ANY],
        (ANY,) + (VMEM,) * 9,
        [
            many,
            pltpu.VMEM((2 * maps, features, width), BF16),
            pltpu.VMEM((units, features), BF16),
            pltpu.VMEM((slots, rows, maps * width), BF16),
            pltpu.VMEM((slots, rows, maps * width), BF16),
            many,
            many,
            pltpu.VMEM((ranks, maps * width), BF16),
            pltpu.VMEM((ranks, maps * width), BF16),
            pltpu.VMEM(qb.shape, F32),
            pltpu.VMEM((ranks, features), F32),
            pltpu.VMEM(qb.shape, F32),
            pltpu.VMEM(qb.shape, F32),
            pltpu.VMEM(qb.shape, F32),
            pltpu.VMEM((depth, ranks + rank, width), BF16),
            pltpu.VMEM((slots, rows, ranks), BF16),
            pltpu.VMEM((rows, features), F32),
            pltpu.VMEM((rows, features), BF16),
            pltpu.VMEM((rows, features), F32),
            pltpu.VMEM((rows, features), F32),
        ]
        + totals_scratch(ranks + rank, features, count, depth)
        + [
            pltpu.VMEM((8 * rank, features), BF16),
            DMA((2, depth)),
            DMA((3,)),
            DMA((3,)),
            DMA((slots,)),
            DMA((slots, 2)),
            DMA((2, slots, 2)),
            DMA((2, slots, 2)),
            DMA((2, 2)),
            DMA((2, depth)),
        ],
        4 * slots * rows * features * maps * width,
        8 * features * maps * width,
        (grads, u_all, w_own, w_par, d_own, *small),
        5,
    )


def results_body(
    maps, first, own, upper, o_mag, gu, side, o_first, d_upper, d_lower, d_mag,
    first_out, second_out, mag_out, o_first_out, upper_out, o_mag_out, gu_first_out, gu_second_out, gu_mag_out,
    d_lower_out, d_upper_out, d_mag_out,
):
    rank = upper.shape[0]
    for s in range(maps):
        at = pl.ds(s * rank, rank)
        first_out[s] = first[at]
        second_out[s] = own[at]
    for s in range(2):
        at = pl.ds(s * rank, rank)
        gu_first_out[s] = gu[at]
        gu_second_out[s] = side[at]
    mag_out[...] = own[maps * rank : maps * rank + maps]
    gu_mag_out[...] = side[3 * rank : 3 * rank + 2]
    o_first_out[...] = o_first[...]
    upper_out[...] = upper[...]
    o_mag_out[...] = o_mag[...]
    d_lower_out[...] = d_lower[...]
    d_upper_out[...] = d_upper[...]
    d_mag_out[...] = d_mag[...]


def results(maps, values):
    first, own, upper, o_mag, gu, side, o_first, d_upper, d_lower, d_mag = values
    rank, features = upper.shape
    units, width = side.shape[1], own.shape[1]
    return pl.pallas_call(
        functools.partial(results_body, maps),
        name="results",
        out_shape=(
            shape((maps, rank, features), F32),
            shape((maps, rank, width), F32),
            shape((maps, width), F32),
            shape(o_first.shape, F32),
            shape(upper.shape, F32),
            shape(o_mag.shape, F32),
            shape((2, rank, features), F32),
            shape((2, rank, units), F32),
            shape((2, units), F32),
            shape(d_lower.shape, F32),
            shape(d_upper.shape, F32),
            shape(d_mag.shape, F32),
        ),
        in_specs=[VMEM] * len(values),
        out_specs=(VMEM,) * 12,
    )(*values)


def rope_tables(total):
    half = HDIM // 2
    frequency = np.exp(-np.log(ROPE_THETA) * np.arange(half) / half)
    angles = np.arange(total)[:, None] * frequency[None, :]
    cosine, sine = np.cos(angles), np.sin(angles)
    return (
        jnp.asarray(np.concatenate([cosine, cosine], axis=1), F32),
        jnp.asarray(np.concatenate([-sine, sine], axis=1), F32),
    )


def body(
    tokens,
    attn_gain,
    ffn_gain,
    qkv_base,
    qkv_first,
    qkv_second,
    qkv_magnitude,
    output_frozen_weight,
    output_first,
    output_upper_map,
    output_magnitude,
    gate_up_base,
    gate_up_first,
    gate_up_second,
    gate_up_magnitude,
    down_frozen_weight,
    down_first,
    down_upper_map,
    down_magnitude,
    lengths,
    cotangent,
):
    rows, features = tokens.shape
    total = rows * lax.axis_size("tensor")
    rank = qkv_first.shape[2]
    units = down_frozen_weight.shape[0]
    cosine, sine = rope_tables(total)
    qkv_first_t = jnp.swapaxes(qkv_first, 1, 2)
    gu_first_t = jnp.swapaxes(gate_up_first, 1, 2)
    gu_base_t = jnp.swapaxes(gate_up_base, 1, 2)
    out_first_t = output_first.T
    down_first_t = down_first.T
    out_mag, down_mag = output_magnitude[None], down_magnitude[None]

    blocks, normed_all, qkv_other, gu_other, down_other, out_parts, at_all, q_stat, g_stat, r_stat, upstream = project(
        lengths,
        tokens,
        attn_gain[None],
        cotangent,
        qkv_base,
        gu_base_t,
        down_frozen_weight,
        output_frozen_weight,
        (
            qkv_first_t,
            qkv_second,
            qkv_magnitude,
            gu_first_t,
            gate_up_second,
            gate_up_magnitude,
            out_first_t,
            output_upper_map,
            down_first_t,
            down_upper_map,
        ),
    )
    attended, logsum, joined, out_weight, hidden, out_before, ffn_normed, out_lowrank, cot_some = attend_forward(
        lengths, q_stat, cosine, sine, blocks, out_parts, at_all, output_upper_map, out_mag, r_stat, tokens,
        ffn_gain[None], upstream,
    )
    down_all, ffn_normed_grad, gu_first_part, side, down_second_part = ffn(
        ffn_normed, upstream, cot_some, gu_base_t, gu_other, down_frozen_weight, down_other,
        (
            gu_first_t, gate_up_second, gate_up_magnitude, down_first_t, down_upper_map, g_stat, r_stat,
            down_mag,
        ),
    )
    (
        head_grads, qkv_drift, hidden_grad, result, down_drift, early_sum, side_total,
    ) = attend_backward(
        blocks,
        features,
        rank,
        units,
        (
            lengths, q_stat, cosine, sine, blocks, attended, logsum, joined, out_weight, at_all,
            output_upper_map, out_mag, r_stat, hidden, out_before, out_lowrank, upstream,
            ffn_normed_grad, ffn_gain[None], down_mag, down_all, gu_first_part, down_second_part, side,
        ),
    )
    (
        tokens_grad, qkv_first_grad, own_total, down_upper_gradient, down_lower_gradient, down_magnitude_grad,
        gate_up_first_grad, output_upper_gradient, output_magnitude_grad, output_first_grad,
    ) = qkv_backward(
        head_grads, normed_all, qkv_base, qkv_other, down_frozen_weight,
        (
            qkv_first_t, qkv_second, qkv_magnitude, q_stat, qkv_drift, r_stat, down_first_t,
            down_upper_map, down_mag, early_sum, down_drift, side_total, tokens, attn_gain[None],
            hidden_grad,
        ),
    )
    (
        qkv_first_grad, qkv_second_grad, qkv_magnitude_grad, output_first_grad, output_upper_gradient,
        output_magnitude_grad, gate_up_first_grad, gate_up_second_grad, gate_up_magnitude_grad,
        down_lower_gradient, down_upper_gradient, down_magnitude_grad,
    ) = results(
        3,
        (
            qkv_first_grad, own_total, output_upper_gradient, output_magnitude_grad, gate_up_first_grad, side_total,
            output_first_grad, down_upper_gradient, down_lower_gradient, down_magnitude_grad,
        ),
    )
    return (
        result,
        tokens_grad,
        jnp.swapaxes(qkv_first_grad, 1, 2),
        qkv_second_grad,
        qkv_magnitude_grad,
        output_first_grad.T,
        output_upper_gradient,
        output_magnitude_grad[0],
        jnp.swapaxes(gate_up_first_grad, 1, 2),
        gate_up_second_grad,
        gate_up_magnitude_grad,
        down_lower_gradient.T,
        down_upper_gradient,
        down_magnitude_grad[0],
    )


def solution(mesh):
    placed = (
        P(("dp", "tensor"), None),
        P(),
        P(),
        P(None, None, "tensor"),
        P(),
        P(None, None, "tensor"),
        P(None, "tensor"),
        P("tensor", None),
        P("tensor", None),
        P(),
        P(),
        P(None, None, "tensor"),
        P(),
        P(None, None, "tensor"),
        P(None, "tensor"),
        P("tensor", None),
        P("tensor", None),
        P(),
        P(),
        P("dp"),
        P(("dp", "tensor"), None),
    )
    return jax.shard_map(
        body,
        mesh=mesh,
        in_specs=placed,
        out_specs=(
            P(("dp", "tensor"), None),
            P(("dp", "tensor"), None),
            P(),
            P(None, None, "tensor"),
            P(None, "tensor"),
            P("tensor", None),
            P(),
            P(),
            P(),
            P(None, None, "tensor"),
            P(None, "tensor"),
            P("tensor", None),
            P(),
            P(),
        ),
        check_vma=False,
    )
```

```python
import functools

import jax
import jax.numpy as jnp
import numpy as np
from jax import lax
from jax.experimental import pallas as pl
from jax.experimental.pallas import tpu as pltpu
from jax.sharding import PartitionSpec as P

HDIM = 128
F32 = jnp.float32
BF16 = jnp.bfloat16
EXACT = lax.Precision.HIGHEST
NORM_EPS = 1e-05
ROPE_THETA = 10000.0
MASKED = -1e30
SOFTMAX_SCALE = HDIM**-0.5
LOG2E = 1.4426950408889634
VMEM_LIMIT = 60 * 2**20
TILE = 256
ANY = pl.BlockSpec(memory_space=pl.ANY)
VMEM = pl.BlockSpec(memory_space=pltpu.VMEM)
SMEM = pl.BlockSpec(memory_space=pltpu.SMEM)
MESH = pl.DeviceIdType.MESH
DMA = pltpu.SemaphoreType.DMA


def nn(left, right, precision=None):
    return jnp.dot(left, right, preferred_element_type=F32, precision=precision)


def nt(left, right, precision=None):
    return lax.dot_general(
        left, right, (((1,), (1,)), ((), ())), preferred_element_type=F32, precision=precision
    )


def tn(left, right):
    return lax.dot_general(left, right, (((0,), (0,)), ((), ())), preferred_element_type=F32)


def both_ways(value):
    return value.astype(BF16), jnp.transpose(value).astype(BF16)


def shape(dims, dtype):
    return jax.ShapeDtypeStruct(dims, dtype)


def tiles(size):
    return [(begin, min(TILE, size - begin)) for begin in range(0, size, TILE)]


def slots_of(count):
    if count == 8:
        return [(0, 0), (2, 4), (6, 6), (4, 2)]
    return [(mask, mask) for mask in range(0, count, 2)]


class Sender:
    def __init__(self):
        self.place = lax.axis_index("dp")
        self.me = lax.axis_index("tensor")

    def meet(self, masks, places=()):
        barrier = pltpu.get_barrier_semaphore()
        for mask in masks:
            pl.semaphore_signal(
                barrier, inc=1, device_id=(self.place, self.me ^ mask), device_id_type=MESH
            )
        for place in places:
            pl.semaphore_signal(
                barrier, inc=1, device_id=(self.place ^ place, self.me), device_id_type=MESH
            )
        pl.semaphore_wait(barrier, len(masks) + len(places))

    def copy(self, source, target, sems, mask, flip=0, step=0):
        place = self.place ^ flip if flip else self.place + step if step else self.place
        return pltpu.make_async_remote_copy(
            src_ref=source,
            dst_ref=target,
            send_sem=sems[0],
            recv_sem=sems[1],
            device_id=(place, self.me ^ mask if mask else self.me),
            device_id_type=MESH,
        )


def gather_stages(sender, count, own, slots, sems, begin=1, end=None):
    half = own.shape[0] // 2

    def rows(ref, slot, h):
        return ref.at[slot, pl.ds(h * half, half)]

    def message(slot, h, source, mask):
        return sender.copy(
            source, rows(slots, slot, h), (sems.at[0, slot, h], sems.at[1, slot, h]), mask
        )

    mine = [own.at[pl.ds(h * half, half)] for h in range(2)]
    if count != 8:
        stages = range(begin, end or count // 2)
        return {s: [message(s, h, mine[h], 2 * s) for h in range(2)] for s in stages}
    routes = {
        1: [(mine[0], 2), (mine[1], 4)],
        2: [(rows(slots, 1, 0), 4), (rows(slots, 1, 1), 2)],
        3: [(mine[0], 4), (mine[1], 2)],
    }
    return {s: [message(s, h, *routes[s][h]) for h in range(2)] for s in range(begin, end or 4)}


def reduce_stages(sender, count, parts, landed, sems, last=3, begin=1, end=4):
    half = parts.shape[1] // 2

    def message(slot, h, mask):
        at = pl.ds(h * half, half)
        return sender.copy(
            parts.at[last if slot == 3 and count == 8 else slot, at], landed.at[slot, at], (sems.at[0, slot, h], sems.at[1, slot, h]), mask
        )

    if count != 8:
        return {s: [message(s, h, 2 * s) for h in range(2)] for s in range(1, count // 2)}
    routes = {1: (2, 4), 2: (2, 4), 3: (4, 2)}
    return {s: [message(s, h, routes[s][h]) for h in range(2)] for s in range(begin, end)}


def relay(part, landed, sums):
    arrive(sums[2])
    part[...] = (part[...].astype(F32) + landed[2].astype(F32)).astype(BF16)
    start(sums[3])


def finish_reduce(count, part, landed, sums, out):
    slots = count // 2
    added = (1, 3) if count == 8 else tuple(range(1, slots))
    for slot in added:
        arrive(sums[slot])

    def columns(step, carry):
        d = pl.ds(pl.multiple_of(step * TILE, TILE), TILE)
        total = part[:, d].astype(F32)
        for slot in added:
            total = total + landed[slot, :, d].astype(F32)
        return out(d, total, carry)

    return columns


def leave_stages(sums):
    for copies in sums.values():
        leave(copies)


def norm_statistics(values_of, grads_of, features, rows):
    def columns(step, carry):
        squares, products = carry
        d = pl.ds(pl.multiple_of(step * TILE, TILE), TILE)
        values = values_of(d)
        squares = squares + jnp.sum(values * values, axis=1, keepdims=True)
        products = products + jnp.sum(values * grads_of(d), axis=1, keepdims=True)
        return squares, products

    zero = jnp.zeros((rows, 1), F32)
    squares, products = lax.fori_loop(0, features // TILE, columns, (zero, zero))
    scale = lax.rsqrt(squares * (1.0 / features) + NORM_EPS)
    return scale, products * (1.0 / features) * scale * scale * scale


class Totals:
    def __init__(self, sender, count, depth, pay, along_in, part, group_in, block, span, main, sems):
        self.sender, self.count, self.depth = sender, count, depth
        self.pay, self.along_in, self.part, self.group_in = pay, along_in, part, group_in
        self.block, self.whole, self.main, self.sems = block, span, main, sems
        self.others, self.flips = range(1, count), range(1, depth)
        self.width = part.shape[1]
        self.height, self.length = block.shape
        self.high = part.shape[0] // self.height
        self.place = sender.place

    def columns(self, place):
        return pl.ds(pl.multiple_of(place * self.width, self.width), self.width)

    def block_of(self, ref, index):
        row = lax.rem(index, self.high) * self.height
        lane = lax.div(index, self.high) * self.length
        return ref.at[
            pl.ds(pl.multiple_of(row, self.height), self.height),
            pl.ds(pl.multiple_of(lane, self.length), self.length),
        ]

    def pair(self, step, which):
        return self.sems.at[0, step, which], self.sems.at[1, step, which]

    def to_place(self, flip):
        source = self.pay.at[:, self.columns(self.place ^ flip)]
        return self.sender.copy(source, self.along_in.at[flip], self.pair(0, flip), 0, flip)

    def to_owner(self, mask):
        source = self.block_of(self.part, self.sender.me ^ mask)
        return self.sender.copy(source, self.group_in.at[mask], self.pair(1, mask), mask)

    def to_group(self, mask, index):
        return self.sender.copy(self.block, self.block_of(self.whole, index), self.pair(2, mask), mask)

    def to_all(self, flip, place):
        return self.sender.copy(self.whole, self.main.at[:, self.columns(place)], self.pair(3, flip), 0, flip)

    def give(self):
        for flip in self.flips:
            self.to_place(flip).start()

    def add_along(self):
        total = self.pay[:, self.columns(self.place)].astype(F32)
        for flip in self.flips:
            self.to_place(flip).wait_recv()
            total = total + self.along_in[flip].astype(F32)
        self.part[...] = total.astype(BF16)
        for mask in self.others:
            self.to_owner(mask).start()

    def add_group(self):
        me = self.sender.me
        total = self.block_of(self.part, me)[...].astype(F32)
        for mask in self.others:
            self.to_owner(mask).wait_recv()
            total = total + self.group_in[mask].astype(F32)
        self.block[...] = total.astype(BF16)
        for mask in self.others:
            self.to_group(mask, me).start()
        self.block_of(self.whole, me)[...] = self.block[...]

    def group(self):
        for mask in self.others:
            self.to_group(mask, self.sender.me ^ mask).wait_recv()

    def share(self):
        for flip in self.flips:
            self.to_all(flip, self.place).start()
        self.main[:, self.columns(self.place)] = self.whole[...]

    def take(self):
        for flip in self.flips:
            self.to_all(flip, self.place ^ flip).wait_recv()

    def end(self):
        for flip in self.flips:
            self.to_place(flip).wait_send()
        for mask in self.others:
            self.to_owner(mask).wait_send()
            self.to_group(mask, self.sender.me).wait_send()

    def end_share(self):
        for flip in self.flips:
            self.to_all(flip, self.place).wait_send()


def along_total(sender, depth, ref):
    total = ref[sender.place].astype(F32)
    for index in range(1, depth):
        total = total + ref[sender.place ^ index].astype(F32)
    return total


def totals_scratch(rows, features, count, depth):
    height = 16
    width = features // depth
    if width * (rows // height) // count < HDIM:
        rows = 8 * height
    length = width * rows // height // count
    return [
        pltpu.VMEM((rows, features), BF16),
        pltpu.VMEM((depth, rows, width), BF16),
        pltpu.VMEM((rows, width), BF16),
        pltpu.VMEM((count, height, length), BF16),
        pltpu.VMEM((height, length), BF16),
        pltpu.VMEM((rows, width), BF16),
        pltpu.VMEM((rows, features), BF16),
        DMA((2, 4, max(count, depth))),
    ]


class Mover:
    def __init__(self, sems):
        self.sems, self.many = sems, 0

    def __call__(self, source, target):
        copy = pltpu.make_async_copy(source, target, self.sems.at[self.many])
        self.many += 1
        copy.start()
        return copy


def start(copies):
    for copy in copies:
        copy.start()


def arrive(copies):
    for copy in copies:
        copy.wait_recv()


def leave(copies):
    for copy in copies:
        copy.wait_send()


def start_all(pairs, sems):
    copies = []
    for at, (source, target) in enumerate(pairs):
        copy = pltpu.make_async_copy(source, target, sems.at[at])
        copy.start()
        copies.append(copy)
    return copies


def call(body, name, out_shape, in_specs, out_specs, scratch, flops, moved, operands, identity):
    return pl.pallas_call(
        body,
        name=name,
        out_shape=out_shape,
        in_specs=in_specs,
        out_specs=out_specs,
        scratch_shapes=scratch,
        compiler_params=pltpu.CompilerParams(
            vmem_limit_bytes=VMEM_LIMIT, collective_id=identity, has_side_effects=True
        ),
        cost_estimate=pl.CostEstimate(flops=flops, bytes_accessed=moved, transcendentals=0),
    )(*operands)


def split(value):
    high = value.astype(BF16)
    return high, (value - high.astype(F32)).astype(BF16)


def left_stack(value):
    high, low = split(value)
    return jnp.concatenate([high, high, low], axis=0)


def right_stack(value):
    high, low = split(value)
    return jnp.concatenate([high, low, high], axis=0)


def first_direction(wide, first_t, second):
    rank = second.shape[0]
    gram = nt(first_t, first_t, EXACT)
    return wide[:rank] + wide[rank:] + 2.0 * nn(gram, second, EXACT)


def second_direction(factored, second, base, first_t):
    rank = second.shape[0]
    wide = nt(jnp.concatenate(split(factored), axis=0), base)
    gram = nt(factored, second, EXACT)
    return wide[:rank] + wide[rank:] + 2.0 * nn(gram, first_t, EXACT)


def line_forward(sender, depth, source, target, part, back, sems):
    place, last = sender.place, depth - 1

    def rows(ref, at):
        return ref.at[pl.ds(1, 3), pl.ds(pl.multiple_of(at * part, part), part)]

    def sends(act):
        @pl.when((place >= back) & (place < last))
        def _():
            at = place - back
            act(sender.copy(rows(source, at), rows(target, at), (sems.at[0, 0], sems.at[1, 0]), 0, 0, 1))

        @pl.when((place <= last - back) & (place > 0))
        def _():
            at = place + back
            act(sender.copy(rows(source, at), rows(target, at), (sems.at[0, 1], sems.at[1, 1]), 0, 0, -1))

    def arrivals(act):
        @pl.when(place > back)
        def _():
            at = place - back - 1
            act(sender.copy(rows(target, at), rows(target, at), (sems.at[0, 0], sems.at[1, 0]), 0, 0, -1))

        @pl.when(place < last - back)
        def _():
            at = place + back + 1
            act(sender.copy(rows(target, at), rows(target, at), (sems.at[0, 1], sems.at[1, 1]), 0, 0, 1))

    return sends, arrivals


def project_body(
    count, depth, lengths, tokens, gain, cot_in, w_own, gu_own, d_own, o_own,
    qa, qb, qmag, ga, gb, gmag, oa, ob, da, db,
    heads, rows_all, w_par, gu_par, d_par, wq, at_all, q_stat, g_stat, r_stat, upstream_out,
    cot, upstream, u, w, wgu, wd, wo, to_par, to_own, second_own, second_par, b_par, sq_all,
    sems, gather_sems, par_sems, head_sems, own_sems, weight_sems, piece_sems, line_sems, small_sems,
):
    sender = Sender()
    slots = slots_of(count)
    maps, _, width = w_own.shape
    rows, features = tokens.shape
    half = rows // 2
    units = d_own.shape[0]
    rank = qb.shape[1]
    shared = count == 8 and depth == 4
    heights = o_own.shape[0]
    part = heights // depth if shared else heights
    others = list(range(1, count))
    sender.meet(others, range(1, depth) if shared else ())

    stages = gather_stages(sender, count, u.at[0], u, gather_sems)
    weights = [
        sender.copy(source, target, (weight_sems.at[0, at], weight_sems.at[1, at]), 1)
        for at, (source, target) in enumerate(
            ((w_own, w_par), (qb, b_par), (gu_own, gu_par), (d_own, d_par))
        )
    ]
    start(weights)
    pieces = []
    for slot in (1, 2) if shared else range(1, count // 2):
        at = pl.ds(pl.multiple_of(sender.place * part, part), part) if shared else pl.ds(0, heights)
        pieces.append(
            sender.copy(
                o_own.at[at], wq.at[slot, at], (piece_sems.at[0, slot], piece_sems.at[1, slot]), 2 * slot
            )
        )
    start(pieces)
    across = []
    if shared:
        for h, (slot, mask) in enumerate(((1, 4), (2, 2))):
            half_part = part // 2
            begin = pl.multiple_of(sender.place * part + h * half_part, half_part)
            at = pl.ds(begin, half_part)
            across.append(
                sender.copy(
                    wq.at[slot, at],
                    wq.at[3, at],
                    (piece_sems.at[0, 3 * h], piece_sems.at[1, 3 * h]),
                    mask,
                )
            )
    smalls = [
        sender.copy(
            oa, at_all.at[mask], (small_sems.at[0, 0, mask], small_sems.at[1, 0, mask]), mask
        )
        for mask in others
    ]
    start(smalls)
    at_all[0] = oa[...]
    local = start_all(
        [(w_own, w.at[pl.ds(0, maps)]), (d_own, wd), (o_own, wo), (gu_own, wgu), (o_own, wq.at[0])]
        + [(cot_in, cot)],
        sems,
    )
    squares = jnp.zeros((rows, 1), F32)
    for begin in range(0, features, TILE):
        values = tokens[:, pl.ds(begin, TILE)].astype(F32)
        squares = squares + jnp.sum(values * values, axis=1, keepdims=True)
    scale = lax.rsqrt(squares * (1.0 / features) + NORM_EPS)
    for begin in range(0, features, TILE):
        d = pl.ds(begin, TILE)
        u[0, :, d] = (tokens[:, d].astype(F32) * scale * gain[:, d]).astype(BF16)
    if shared:
        arrive(pieces)
        start(across)
    start(stages[1])
    for slot in (3,) if count == 8 else range(2, len(slots)):
        start(stages[slot])
    second_own[...] = jnp.zeros_like(second_own)
    second_par[...] = jnp.zeros_like(second_par)
    for s in range(maps):
        second_own[pl.ds(s * rank, rank), pl.ds(s * width, width)] = (2.0 * qb[s]).astype(BF16)
    first_t = qa[...].reshape(maps * rank, features).astype(BF16)
    local[0].wait()
    pending, sent = [], []

    def one_slot(slot):
        masks = slots[slot]
        keep = pltpu.make_async_copy(u.at[slot], rows_all.at[slot], own_sems.at[slot])
        keep.start()
        pending.append(keep)
        lowrank = nt(u[slot], first_t).astype(BF16)
        for s in range(maps):
            lanes = pl.ds(s * width, width)
            to_own[slot, :, lanes] = (nn(u[slot], w[s]) + nn(lowrank, second_own[:, lanes])).astype(BF16)
        if slot == 0:
            arrive(weights[:2])
            load = pltpu.make_async_copy(w_par, w.at[pl.ds(maps, maps)], sems.at[6])
            load.start()
            for s in range(maps):
                second_par[pl.ds(s * rank, rank), pl.ds(s * width, width)] = (2.0 * b_par[s]).astype(BF16)
            load.wait()
        for s in range(maps):
            lanes = pl.ds(s * width, width)
            to_par[slot, :, lanes] = (
                nn(u[slot], w[maps + s]) + nn(lowrank, second_par[:, lanes])
            ).astype(BF16)
        for h, mask in enumerate(masks):
            at = pl.ds(h * half, half)
            keep = pltpu.make_async_copy(
                to_own.at[slot, at], heads.at[mask, at], head_sems.at[slot, h]
            )
            send = sender.copy(
                to_par.at[slot, at],
                heads.at[mask ^ 1, at],
                (par_sems.at[0, slot, h], par_sems.at[1, slot, h]),
                1,
            )
            send.start()
            keep.start()
            pending.append(keep)
            sent.append(send)

    def next_slot(slot):
        arrive(stages[slot])
        if count == 8 and slot == 1:
            start(stages[2])
        one_slot(slot)

    one_slot(0)
    place = sender.me * rows + lax.broadcasted_iota(jnp.int32, (rows, 1), 0)
    local[5].wait()
    upstream[...] = jnp.where(place < lengths[0], cot[...].astype(F32), 0.0).astype(BF16)
    masked = pltpu.make_async_copy(upstream, upstream_out, sems.at[7])
    masked.start()
    pending.append(masked)

    local[1].wait()
    local[2].wait()
    down_left, down_right = left_stack(da[...]), right_stack(db[...])
    total = jnp.zeros((1, features), F32)
    for begin, span in tiles(units):
        direction = wd[pl.ds(begin, span), :].astype(F32) + 2.0 * tn(
            down_left[:, begin : begin + span], down_right
        )
        total = total + jnp.sum(direction * direction, axis=0, keepdims=True)
    sq_all[0, 1:2, :] = total
    direction = wo[...].astype(F32) + 2.0 * tn(left_stack(oa[...]), right_stack(ob[...]))
    sq_all[0, 0:1, :] = jnp.sum(direction * direction, axis=0, keepdims=True)
    squares = [
        sender.copy(
            sq_all.at[0], sq_all.at[mask], (small_sems.at[0, 1, mask], small_sems.at[1, 1, mask]), mask
        )
        for mask in others
    ]
    start(squares)
    r_stat[0, 8 : 8 + rank] = jnp.zeros((rank, features), F32)
    r_stat[1, 8 : 8 + rank] = first_direction(
        nn(jnp.concatenate(split(da[...]), axis=0), wd[...]), da[...], db[...]
    )
    arrive(across if shared else pieces)
    if shared:
        sends0, arrivals0 = line_forward(sender, depth, wq, wq, part, 0, line_sems.at[0])
        sends1, arrivals1 = line_forward(sender, depth, wq, wq, part, 1, line_sems.at[1])
        sends0(lambda copy: copy.start())

    for s in range(maps):
        left, right = left_stack(qa[s]), right_stack(qb[s])
        total = jnp.zeros((1, width), F32)
        for begin in range(0, features, 512):
            direction = w[s, pl.ds(begin, 512), :].astype(F32) + 2.0 * tn(
                left[:, begin : begin + 512], right
            )
            total = total + jnp.sum(direction * direction, axis=0, keepdims=True)
        norm = jnp.sqrt(total)
        q_stat[s, 0:1] = norm
        q_stat[s, 1:2] = qmag[s : s + 1] / norm
        q_stat[s, 8 : 8 + rank] = first_direction(
            nn(jnp.concatenate(split(qa[s]), axis=0), w[s]), qa[s], qb[s]
        )
    next_slot(1)
    if shared:
        arrivals0(lambda copy: copy.wait_recv())
        sends1(lambda copy: copy.start())

    local[3].wait()
    ones = jnp.ones((8, HDIM), BF16)
    for s in range(2):
        left, right = left_stack(gb[s]), right_stack(ga[s])
        for begin, span in tiles(units):
            direction = wgu[s, pl.ds(begin, span), :].astype(F32) + 2.0 * tn(
                left[:, begin : begin + span], right
            )
            direction = direction * direction
            folded = direction[:, :HDIM]
            for lane in range(HDIM, features, HDIM):
                folded = folded + direction[:, lane : lane + HDIM]
            high, low = split(folded)
            norm = jnp.sqrt((nt(ones, high) + nt(ones, low))[:1])
            f = pl.ds(begin, span)
            g_stat[s, 0:1, f] = norm
            g_stat[s, 1:2, f] = gmag[s : s + 1, f] / norm
        g_stat[s, 8 : 8 + rank] = first_direction(
            nt(jnp.concatenate(split(ga[s]), axis=0), wgu[s]), ga[s], gb[s]
        )
    for slot in (3, 2) if count == 8 else range(2, len(slots)):
        next_slot(slot)
    arrive(squares)
    total = jnp.zeros((2, features), F32)
    for index in range(count):
        total = total + sq_all[sender.me ^ index]
    norm = jnp.sqrt(total)
    r_stat[0, 0:1] = norm[0:1]
    r_stat[1, 0:1] = norm[1:2]

    for copy in pending:
        copy.wait()
    local[4].wait()
    arrive(sent + weights[2:] + smalls)
    leave(sent + weights + smalls + squares + pieces + across)
    for slot in range(1, len(slots)):
        leave(stages[slot])
    if shared:
        arrivals1(lambda copy: copy.wait_recv())
        sends0(lambda copy: copy.wait_send())
        sends1(lambda copy: copy.wait_send())


def project(lengths, tokens, gain, cot, w_own, gu_own, d_own, o_own, small):
    rows, features = tokens.shape
    count, depth = lax.axis_size("tensor"), lax.axis_size("dp")
    slots = count // 2
    maps, _, width = w_own.shape
    units = d_own.shape[0]
    rank = small[1].shape[1]
    return call(
        functools.partial(project_body, count, depth),
        "project",
        (
            shape((count, rows, maps * width), BF16),
            shape((slots, rows, features), BF16),
            shape(w_own.shape, BF16),
            shape(gu_own.shape, BF16),
            shape(d_own.shape, BF16),
            shape((slots, width, features), BF16),
            shape((count, rank, width), F32),
            shape((maps, 8 + rank, width), F32),
            shape((2, 8 + rank, units), F32),
            shape((2, 8 + rank, features), F32),
            shape((rows, features), BF16),
        ),
        [SMEM, VMEM, VMEM] + [ANY] * 5 + [VMEM] * len(small),
        (ANY,) * 6 + (VMEM,) * 4 + (ANY,),
        [
            pltpu.VMEM((rows, features), BF16),
            pltpu.VMEM((rows, features), BF16),
            pltpu.VMEM((slots, rows, features), BF16),
            pltpu.VMEM((2 * maps, features, width), BF16),
            pltpu.VMEM(gu_own.shape, BF16),
            pltpu.VMEM(d_own.shape, BF16),
            pltpu.VMEM(o_own.shape, BF16),
            pltpu.VMEM((slots, rows, maps * width), BF16),
            pltpu.VMEM((slots, rows, maps * width), BF16),
            pltpu.VMEM((maps * rank, maps * width), BF16),
            pltpu.VMEM((maps * rank, maps * width), BF16),
            pltpu.VMEM((maps, rank, width), F32),
            pltpu.VMEM((count, 2, features), F32),
            DMA((8,)),
            DMA((2, slots, 2)),
            DMA((2, slots, 2)),
            DMA((slots, 2)),
            DMA((slots,)),
            DMA((2, 4)),
            DMA((2, slots)),
            DMA((2, 2, 2)),
            DMA((2, 2, count)),
        ],
        4 * slots * rows * features * maps * width,
        8 * features * maps * width,
        (lengths, tokens, gain, cot, w_own, gu_own, d_own, o_own, *small),
        1,
    )


def turn(values, cosine, sine):
    return values * cosine + pltpu.roll(values, HDIM // 2, 1) * sine


def rms_scale(values):
    return lax.rsqrt(jnp.mean(values * values, axis=1, keepdims=True) + NORM_EPS)


def load_head(count, rows, h, xs, q_stat, cosine, sine, q, k, v):
    lane = pl.ds(pl.multiple_of(h * HDIM, HDIM), HDIM)
    heads = xs.shape[1] // (3 * HDIM)
    for a in range(count):
        at = pl.ds(a * rows, rows)
        cos, sin = cosine[at], sine[at]
        for part, target in enumerate((q, k, v)):
            lanes = pl.ds(pl.multiple_of((part * heads + h) * HDIM, HDIM), HDIM)
            values = xs[at, lanes].astype(F32) * q_stat[part, 1:2, lane]
            if part < 2:
                values = turn(values, cos, sin)
            target[at] = values.astype(BF16)


def attend_forward_body(
    count, depth, lengths, q_stat, cosine_in, sine_in, blocks, wq, at_all, ob, o_mag, r_stat, tokens_in, gain, grads,
    attended_out, logsum, joined_out, w_all, hidden_out, before_out, normed_out, lowrank, c_some,
    xs, q, k, v, wv, cosine, sine, tokens, attended, joined, hidden, before, normed, move_sems, sems, part_sems, line_sems, pair_sems, swap_sems, own_sems, c_sems, w_sems,
):
    sender = Sender()
    me, place = sender.me, sender.place
    length = lengths[0]
    _, rows, width = blocks.shape
    heads = width // (3 * HDIM)
    total = rows * count
    half = rows // 2
    features = ob.shape[1]
    shared = count == 8 and depth == 4
    part = wq.shape[1] // depth
    others = list(range(1, count))
    move = Mover(move_sems)
    copies = start_all(
        [
            (blocks.at[mask], xs.at[pl.ds(pl.multiple_of((me ^ mask) * rows, rows), rows)])
            for mask in range(count)
        ],
        sems,
    )
    copies = copies + [move(cosine_in, cosine), move(sine_in, sine)]
    tokens_load = move(tokens_in, tokens)
    sender.meet(others, range(1, depth) if shared else ())

    stages = gather_stages(sender, count, grads, c_some, c_sems, 1, 3)

    def rows_of(ref, at):
        return ref.at[pl.ds(1, 3), pl.ds(pl.multiple_of(at * part, part), part)]

    if shared:
        whole = pltpu.make_async_copy(wq.at[0], wv.at[0, 0], part_sems.at[depth])
        whole_pair = sender.copy(
            wq.at[0], wv.at[1, 0], (pair_sems.at[0, depth], pair_sems.at[1, depth]), 1
        )
        whole.start()
        whole_pair.start()

        def near(act, act_pair):
            for at in range(depth):

                @pl.when((place - at <= 2) & (at - place <= 2))
                def _():
                    if act is not None:
                        act(pltpu.make_async_copy(rows_of(wq, at), rows_of(wv.at[0], at), part_sems.at[at]))
                    act_pair(
                        sender.copy(
                            rows_of(wq, at), rows_of(wv.at[1], at), (pair_sems.at[0, at], pair_sems.at[1, at]), 1
                        )
                    )

        def far(act):
            for at, other in ((0, depth - 1), (depth - 1, 0)):

                @pl.when(place == other)
                def _():
                    act(
                        sender.copy(
                            rows_of(wv.at[0], at), rows_of(wv.at[1], at),
                            (pair_sems.at[0, at], pair_sems.at[1, at]), 1,
                        )
                    )

        def line_sends(act):
            @pl.when(place == 2)
            def _():
                act(
                    sender.copy(
                        rows_of(wq, 0), rows_of(wv.at[0], 0), (line_sems.at[0, 0], line_sems.at[1, 0]), 0, 0, 1
                    )
                )

            @pl.when(place == 1)
            def _():
                act(
                    sender.copy(
                        rows_of(wq, 3), rows_of(wv.at[0], 3), (line_sems.at[0, 1], line_sems.at[1, 1]), 0, 0, -1
                    )
                )

        def line_arrivals(act):
            @pl.when(place == 3)
            def _():
                act(
                    sender.copy(
                        rows_of(wv.at[0], 0), rows_of(wv.at[0], 0), (line_sems.at[0, 0], line_sems.at[1, 0]), 0, 0, -1
                    )
                )

            @pl.when(place == 0)
            def _():
                act(
                    sender.copy(
                        rows_of(wv.at[0], 3), rows_of(wv.at[0], 3), (line_sems.at[0, 1], line_sems.at[1, 1]), 0, 0, 1
                    )
                )

        near(lambda copy: copy.start(), lambda copy: copy.start())
        line_sends(lambda copy: copy.start())
    else:
        whole = pltpu.make_async_copy(wq, wv.at[0], part_sems.at[0])
        whole_pair = sender.copy(wq, wv.at[1], (pair_sems.at[0, 0], pair_sems.at[1, 0]), 1)
        whole.start()
        whole_pair.start()
    start(stages[1])

    for copy in copies:
        copy.wait()
    factor = SOFTMAX_SCALE * LOG2E
    bias = jnp.where(lax.broadcasted_iota(jnp.int32, (1, total), 1) < length, 0.0, MASKED)
    kept = lax.broadcasted_iota(jnp.int32, (rows, rows), 1) <= lax.broadcasted_iota(
        jnp.int32, (rows, rows), 0
    )

    def exchange(h, mask):
        lane = pl.ds(pl.multiple_of(h * HDIM, HDIM), HDIM)
        return sender.copy(
            attended.at[mask, :, lane],
            joined.at[mask, :, lane],
            (swap_sems.at[0, h, mask], swap_sems.at[1, h, mask]),
            mask,
        )

    def one_head(h, carry):
        load_head(count, rows, h, xs, q_stat, cosine, sine, q, k, v)
        lane = pl.ds(pl.multiple_of(h * HDIM, HDIM), HDIM)
        for a in range(count):
            at = pl.ds(a * rows, rows)
            query = q[at]
            inner = nt(query, k[at]) * factor + bias[:, a * rows : (a + 1) * rows]
            inner = jnp.where(kept, inner, MASKED)
            highest = jnp.max(inner, axis=1, keepdims=True)
            if a:
                earlier = pl.ds(0, a * rows)
                outer = nt(query, k[earlier]) * factor + bias[:, : a * rows]
                highest = jnp.maximum(highest, jnp.max(outer, axis=1, keepdims=True))
            inner = jnp.exp2(inner - highest)
            sums = jnp.sum(inner, axis=1, keepdims=True)
            result = nn(inner.astype(BF16), v[at])
            if a:
                outer = jnp.exp2(outer - highest)
                sums = sums + jnp.sum(outer, axis=1, keepdims=True)
                result = result + nn(outer.astype(BF16), v[earlier])
            attended[a ^ me, :, lane] = (result * (1.0 / sums)).astype(BF16)
            column = jnp.broadcast_to(highest + jnp.log2(sums), (rows, HDIM))
            logsum[h, :, at] = jnp.transpose(column)[:1]
        for mask in others:
            exchange(h, mask).start()
        return carry

    lax.fori_loop(0, heads, one_head, 0)
    arrive(stages[1])
    start(stages[2])
    joined[0] = attended[0]
    outs = [move(attended, attended_out)]
    if shared:
        line_arrivals(lambda copy: copy.wait_recv())
        far(lambda copy: copy.start())
        whole.wait()
        near(lambda copy: copy.wait(), lambda copy: copy.wait_recv())
        far(lambda copy: copy.wait_recv())
    else:
        whole.wait()
    arrive([whole_pair])
    keeps = start_all(
        [(wv.at[mask % 2, mask // 2], w_all.at[mask]) for mask in range(count)], w_sems
    )
    for h in range(heads):
        arrive([exchange(h, mask) for mask in others])
    outs.append(move(joined, joined_out))
    tokens_load.wait()

    low = jnp.zeros((rows, ob.shape[0]), F32)
    for mask in range(count):
        low = low + nt(joined[mask], at_all[mask].astype(BF16))
    low = low.astype(BF16)
    lowrank[...] = low

    def columns(step, squares):
        d = pl.ds(pl.multiple_of(step * TILE, TILE), TILE)
        result = nn(low, (2.0 * ob[:, d]).astype(BF16))
        for mask in range(count):
            result = result + nn(joined[mask], wv[mask % 2, mask // 2, :, d])
        before[:, d] = result.astype(BF16)
        result = tokens[:, d].astype(F32) + result * (o_mag[:, d] / r_stat[0, 0:1, d])
        hidden[:, d] = result
        return squares + jnp.sum(result * result, axis=1, keepdims=True)

    squares = lax.fori_loop(0, features // TILE, columns, jnp.zeros((rows, 1), F32))
    scale = lax.rsqrt(squares * (1.0 / features) + NORM_EPS)
    outs += [move(hidden, hidden_out), move(before, before_out)]
    normed[...] = (hidden[...] * scale * gain[...]).astype(BF16)
    outs.append(move(normed, normed_out))
    for copy in keeps + outs:
        copy.wait()
    arrive(stages[2])
    leave(stages[1] + stages[2] + [whole_pair])
    for h in range(heads):
        leave([exchange(h, mask) for mask in others])
    if shared:
        line_sends(lambda copy: copy.wait_send())
        near(None, lambda copy: copy.wait_send())
        far(lambda copy: copy.wait_send())


def attend_forward(lengths, q_stat, cosine, sine, blocks, wq, at_all, ob, o_mag, r_stat, tokens, gain, grads):
    count, rows, width = blocks.shape
    depth = lax.axis_size("dp")
    head_width = width // 3
    heads = head_width // HDIM
    total = count * rows
    features = ob.shape[1]
    slots = count // 2
    return call(
        functools.partial(attend_forward_body, count, depth),
        "attend_forward",
        (
            shape((count, rows, head_width), BF16),
            shape((heads, 1, total), F32),
            shape((count, rows, head_width), BF16),
            shape((count, head_width, features), BF16),
            shape((rows, features), F32),
            shape((rows, features), BF16),
            shape((rows, features), BF16),
            shape((rows, ob.shape[0]), BF16),
            shape((3, rows, features), BF16),
        ),
        [SMEM, VMEM, ANY, ANY, ANY, ANY] + [VMEM] * 4 + [ANY, VMEM, ANY],
        (ANY, VMEM, ANY, ANY, ANY, ANY, ANY, VMEM, ANY),
        [pltpu.VMEM((total, width), BF16)]
        + [pltpu.VMEM((total, HDIM), BF16)] * 3
        + [
            pltpu.VMEM((2, slots, head_width, features), BF16),
            pltpu.VMEM((total, HDIM), F32),
            pltpu.VMEM((total, HDIM), F32),
            pltpu.VMEM((rows, features), BF16),
            pltpu.VMEM((count, rows, head_width), BF16),
            pltpu.VMEM((count, rows, head_width), BF16),
            pltpu.VMEM((rows, features), F32),
            pltpu.VMEM((rows, features), BF16),
            pltpu.VMEM((rows, features), BF16),
            DMA((8,)),
            DMA((count,)),
            DMA((depth + 1,)),
            DMA((2, 2)),
            DMA((2, depth + 1)),
            DMA((2, heads, count)),
            DMA((1,)),
            DMA((2, 3, 2)),
            DMA((count,)),
        ],
        4 * heads * total * total * HDIM + 2 * rows * features * features,
        2 * total * width * 2,
        (lengths, q_stat, cosine, sine, blocks, wq, at_all, ob, o_mag, r_stat, tokens, gain, grads),
        2,
    )


def ffn_body(
    count, own, c_own, c_some, gu_own, gu_par, d_own, d_par,
    ga, gb, gmag, da, db, g_stat, r_stat, d_mag,
    down_all, dx_sum, g_first, side, g_down_second,
    u, c, wgu, wd, grad_low, sw, bg, down, parts, landed, second, second_par, da_par, scale_par, scale_own, d_second,
    g_second, g_down_first, drift, second_landed, first_landed, drift_landed,
    sems, down_sems, gather_sems, c_sems, reduce_sems, pair_sems,
):
    sender = Sender()
    slots = count // 2
    rows, features = own.shape
    units = d_own.shape[0]
    rank = da.shape[0]
    sender.meet([1] + list(range(2, count, 2)))
    stages = gather_stages(sender, count, own, u, gather_sems)
    c_stages = gather_stages(sender, count, c_own, c, c_sems, 3)
    sums = reduce_stages(sender, count, parts, landed, reduce_sems)
    scale_own[...] = g_stat[:, 1]
    pairs = [
        sender.copy(source, target, (pair_sems.at[0, at], pair_sems.at[1, at]), 1)
        for at, (source, target) in enumerate(((gb, second_par), (da, da_par), (scale_own, scale_par)))
    ]
    start(pairs)
    start(stages[1])
    local = start_all(
        [(own, u.at[0]), (c_own, c.at[0])]
        + [(gu_own, wgu.at[0]), (d_own, wd.at[0]), (gu_par, wgu.at[1]), (d_par, wd.at[1])]
        + [(c_some.at[slot], c.at[slot]) for slot in (1, 2)],
        sems,
    )
    if count == 8:
        start(stages[3])
    else:
        for slot in range(2, slots):
            start(stages[slot])
        for slot in range(3, slots):
            start(c_stages[slot])
    first_t = ga[...].reshape(2 * rank, features).astype(BF16)
    d_scale = d_mag[...] / r_stat[1, 0:1]
    d_second[...] = (2.0 * db[...]).astype(BF16)
    second[...] = jnp.zeros_like(second)
    for part in range(2):
        second[0, part, pl.ds(part * rank, rank), :] = (2.0 * gb[part]).astype(BF16)
    arrive(pairs)
    for part in range(2):
        second[1, part, pl.ds(part * rank, rank), :] = (2.0 * second_par[part]).astype(BF16)
    da_low = (da[...].astype(BF16), da_par[...].astype(BF16))
    for ref in (g_first, g_second, g_down_first, g_down_second, drift):
        ref[...] = jnp.zeros_like(ref)
    local[0].wait()
    local[1].wait()
    rooms = down.shape[0]

    def store(slot):
        return pltpu.make_async_copy(down.at[slot % rooms], down_all.at[slot], down_sems.at[slot])

    def one_slot(slot, carry):
        room = lax.rem(slot, rooms)
        if slots > rooms:

            @pl.when(slot >= rooms)
            def _():
                store(slot - rooms).wait()

        for at in range(1, slots):

            @pl.when(slot == at)
            def _():
                if at in (1, 2):
                    local[5 + at].wait()
                else:
                    arrive(c_stages[at])

        lowrank, lowrank_t = both_ways(nt(u[slot], first_t))
        grad_low[...] = (c[slot].astype(F32) * d_scale).astype(BF16)
        d_low_grad, d_low_grad_t = both_ways(nt(grad_low[...], d_second[...]))
        d_low = jnp.zeros((rows, rank), F32)
        u_low = jnp.zeros((rows, 2 * rank), F32)
        for which, scale in enumerate((scale_own, scale_par)):

            @pl.when(slot == 0)
            def _():
                local[2 + 2 * which].wait()
                local[3 + 2 * which].wait()

            for at in range(1, slots) if which else ():

                @pl.when(slot == at - 1)
                def _():
                    arrive(stages[at])
                    if count == 8 and at == 1:
                        start(stages[2])
                        start(c_stages[3])

            for begin, span in tiles(units):
                f = pl.ds(begin, span)
                gate_before = nt(u[slot], wgu[which, 0, f, :]) + nn(lowrank, second[which, 0, :, f])
                up_before = nt(u[slot], wgu[which, 1, f, :]) + nn(lowrank, second[which, 1, :, f])
                gate = gate_before * scale[0:1, f]
                up = up_before * scale[1:2, f]
                sigmoid = 1.0 / (1.0 + jnp.exp(-gate))
                silu = gate * sigmoid
                swiglu = (silu * up).astype(BF16)
                swiglu_grad = nt(grad_low[...], wd[which, f, :]) + nn(
                    d_low_grad, da_low[which][:, begin : begin + span]
                )
                swiglu_grad = swiglu_grad.astype(BF16).astype(F32)
                gate_grad = swiglu_grad * up * (sigmoid * (1.0 + gate * (1.0 - sigmoid)))
                up_grad = swiglu_grad * silu
                drift[which, 0:1, f] += jnp.sum(gate_grad * gate_before, axis=0, keepdims=True)
                drift[which, 1:2, f] += jnp.sum(up_grad * up_before, axis=0, keepdims=True)
                sw[which, :, f] = swiglu
                bg[which, 0, :, f] = (gate_grad * scale[0:1, f]).astype(BF16)
                bg[which, 1, :, f] = (up_grad * scale[1:2, f]).astype(BF16)
            d_low = d_low + nt(sw[which], da_low[which])
            for part in range(2):
                u_low = u_low + nt(bg[which, part], second[which, part])
                g_second[which, part] += 2.0 * nn(
                    lowrank_t[part * rank : (part + 1) * rank], bg[which, part]
                )
            g_down_first[which] += nn(d_low_grad_t, sw[which])
        d_low, d_low_t = both_ways(d_low)
        u_low, u_low_t = both_ways(u_low)

        for begin in range(0, features, TILE):
            d = pl.ds(begin, TILE)
            dx = nn(u_low, first_t[:, begin : begin + TILE])
            for which in range(2):
                for part in range(2):
                    dx = dx + nn(bg[which, part], wgu[which, part, :, d])
            parts[slot, :, d] = dx.astype(BF16)
        for at in range(1, slots):

            @pl.when(slot == at)
            def _():
                if count == 8 and at == 3:
                    relay(parts.at[3], landed, sums)
                else:
                    start(sums[at])

        for begin in range(0, features, TILE):
            d = pl.ds(begin, TILE)
            g_first[:, d] += nn(u_low_t, u[slot, :, d])
            total = nn(sw[0], wd[0, :, d]) + nn(sw[1], wd[1, :, d]) + nn(d_low, d_second[:, d])
            down[room, :, d] = total.astype(BF16)
            g_down_second[:, d] += 2.0 * nn(d_low_t, grad_low[:, d])
        store(slot).start()
        return carry

    lax.fori_loop(0, slots, one_slot, 0)

    gives = [
        sender.copy(source, target, (pair_sems.at[0, at], pair_sems.at[1, at]), 1)
        for at, source, target in (
            (3, g_second.at[1], second_landed),
            (4, g_down_first.at[1], first_landed),
            (5, drift.at[1], drift_landed),
        )
    ]
    start(gives)
    arrive(gives)
    total_drift = drift[0] + drift_landed[...]
    side[...] = jnp.zeros_like(side)
    side[2 * rank : 3 * rank] = g_down_first[0] + first_landed[...]
    for part in range(2):
        norm = g_stat[part, 0:1]
        one = total_drift[part : part + 1]
        factor = -one * gmag[part : part + 1] / (norm * norm * norm)
        at = pl.ds(part * rank, rank)
        side[at] = g_second[0, part] + second_landed[part] + 2.0 * g_stat[part, 8 : 8 + rank] * factor
        side[3 * rank + part : 3 * rank + part + 1] = one / norm
        factored = gb[part] * factor
        wide = nn(jnp.concatenate(split(factored), axis=0), wgu[0, part])
        gram = nt(factored, gb[part], EXACT)
        g_first[at] += 2.0 * (wide[:rank] + wide[rank:] + 2.0 * nn(gram, ga[part], EXACT))

    def out(d, value, carry):
        dx_sum[:, d] = value.astype(BF16)
        return carry

    lax.fori_loop(0, features // TILE, finish_reduce(count, parts.at[0], landed, sums, out), 0)
    for slot in range(max(0, slots - rooms), slots):
        store(slot).wait()
    leave(pairs + gives)
    for copies in (sums, stages, c_stages):
        leave_stages(copies)


def ffn(own, c_own, c_some, gu_own, gu_par, d_own, d_par, small):
    rows, features = own.shape
    count = lax.axis_size("tensor")
    slots = count // 2
    units = d_own.shape[0]
    rank = small[3].shape[0]
    many = pltpu.VMEM((slots, rows, features), BF16)
    return call(
        functools.partial(ffn_body, count),
        "ffn",
        (
            shape((slots, rows, features), BF16),
            shape((rows, features), BF16),
            shape((2 * rank, features), F32),
            shape((4 * rank, units), F32),
            shape((rank, features), F32),
        ),
        [ANY] * 7 + [VMEM] * len(small),
        (ANY,) + (VMEM,) * 4,
        [
            many,
            many,
            pltpu.VMEM((2, 2, units, features), BF16),
            pltpu.VMEM((2, units, features), BF16),
            pltpu.VMEM((rows, features), BF16),
            pltpu.VMEM((2, rows, units), BF16),
            pltpu.VMEM((2, 2, rows, units), BF16),
            pltpu.VMEM((min(slots, 4), rows, features), BF16),
            many,
            many,
            pltpu.VMEM((2, 2, 2 * rank, units), BF16),
            pltpu.VMEM((2, rank, units), F32),
            pltpu.VMEM((rank, units), F32),
            pltpu.VMEM((2, units), F32),
            pltpu.VMEM((2, units), F32),
            pltpu.VMEM((rank, features), BF16),
            pltpu.VMEM((2, 2, rank, units), F32),
            pltpu.VMEM((2, rank, units), F32),
            pltpu.VMEM((2, 2, units), F32),
            pltpu.VMEM((2, rank, units), F32),
            pltpu.VMEM((rank, units), F32),
            pltpu.VMEM((2, units), F32),
            DMA((8,)),
            DMA((slots,)),
            DMA((2, slots, 2)),
            DMA((2, slots, 2)),
            DMA((2, slots, 2)),
            DMA((2, 6)),
        ],
        24 * slots * rows * features * units,
        12 * features * units,
        (own, c_own, c_some, gu_own, gu_par, d_own, d_par, *small),
        3,
    )


def attend_backward_body(
    count, depth, lengths, q_stat, cosine_in, sine_in, blocks, attended_in, logsum, joined_in, w_all, at_all, ob, o_mag,
    r_stat, hidden_in, before_in, lowrank, cot_in, dx_in, gain, d_mag, down_all, gu_first, d_second, side,
    out_all, drift, hidden_grad_out, result_out, d_drift, span_sum, side_total,
    xs, dos, q, k, v, dq, centre, wv, og, ag, parts, landed, side_line,
    cosine, sine, attended, joined, hidden, before, cot, dx_sum, out, hidden_grad, result, o_drift_row,
    pay, along_in, part, group_in, block, total_sems,
    move_sems, sems, w_sems, part_sems, swap_sems, reduce_sems, side_sems,
):
    sender = Sender()
    me = sender.me
    length = lengths[0]
    _, rows, width = blocks.shape
    heads = width // (3 * HDIM)
    total = rows * count
    features = ob.shape[1]
    rank = ob.shape[0]
    slots = count // 2
    others = list(range(1, count))
    flips = list(range(1, depth))
    order = others + [0]
    move = Mover(move_sems)
    early = [move(hidden_in, hidden), move(dx_in, dx_sum), move(cot_in, cot), move(before_in, before)]
    loads = dict(
        zip(order, start_all([(w_all.at[mask], wv.at[mask]) for mask in order], w_sems))
    )
    joined_load = move(joined_in, joined)
    late = [move(cosine_in, cosine), move(sine_in, sine), move(attended_in, attended)]
    sender.meet(others, flips)
    sums = reduce_stages(sender, count, down_all, landed, reduce_sems, end=3)
    if count == 8:
        sums.update(reduce_stages(sender, count, parts, landed, reduce_sems, 1, 3))
        start(sums[2])
    else:
        for slot in range(1, slots):
            start(sums[slot])
    copies = start_all(
        [
            (blocks.at[mask], xs.at[pl.ds(pl.multiple_of((me ^ mask) * rows, rows), rows)])
            for mask in range(count)
        ],
        sems,
    )
    kept_parts = (0, 3) if count == 8 else (0,)
    part_loads = start_all(
        [(down_all.at[slot], parts.at[at]) for at, slot in enumerate(kept_parts)], part_sems
    )

    for copy in early[:2]:
        copy.wait()
    scale, back = norm_statistics(
        lambda d: hidden[:, d], lambda d: dx_sum[:, d].astype(F32) * gain[:, d], features, rows
    )

    for copy in early[2:]:
        copy.wait()

    def rows_grad(step, carry):
        d = pl.ds(pl.multiple_of(step * TILE, TILE), TILE)
        grad = cot[:, d].astype(F32) + scale * (dx_sum[:, d].astype(F32) * gain[:, d]) - hidden[:, d] * back
        hidden_grad[:, d] = grad
        o_drift_row[:, d] = jnp.sum(grad * before[:, d].astype(F32), axis=0, keepdims=True)
        og[:, d] = (grad * (o_mag[:, d] / r_stat[0, 0:1, d])).astype(BF16)
        return carry

    lax.fori_loop(0, features // TILE, rows_grad, 0)
    outs = [move(hidden_grad, hidden_grad_out)]
    o_drift = o_drift_row[...]
    second = (2.0 * ob[...]).astype(BF16)
    low_grad = nt(og[...], second).astype(BF16)
    mine = pl.ds(pl.multiple_of(me * rows, rows), rows)

    def exchange(h, mask, at=None):
        lane = pl.ds(pl.multiple_of(h * HDIM, HDIM), HDIM)
        return sender.copy(
            ag.at[mask, :, lane],
            dos.at[mine if at is None else at, lane],
            (swap_sems.at[0, h, mask], swap_sems.at[1, h, mask]),
            mask,
        )

    def landing(h, mask):
        return exchange(h, mask, pl.ds(pl.multiple_of((me ^ mask) * rows, rows), rows))

    for mask in order:
        loads[mask].wait()
        grad = nt(og[...], wv[mask]) + nn(low_grad, at_all[mask].astype(BF16))
        if mask:
            ag[mask] = grad.astype(BF16)
            exchange(0, mask).start()
        else:
            dos[mine] = grad.astype(BF16)
    for h in range(1, heads):
        for mask in others:
            exchange(h, mask).start()

    low_grad_t = nt(second, og[...]).astype(BF16)
    norm = r_stat[0, 0:1]
    factor = -o_drift * o_mag[...] / (norm * norm * norm)
    factored = ob[...] * factor
    wide = jnp.zeros((2 * rank, features), F32)
    gram = jnp.zeros((rank, rank), F32)
    joined_load.wait()
    for mask in range(count):
        first = at_all[mask]
        span = pl.ds(pl.multiple_of((me ^ mask) * (width // 3), width // 3), width // 3)
        pay[6 * rank : 7 * rank, span] = (
            nn(low_grad_t, joined[mask]) + 2.0 * second_direction(factored, ob[...], wv[mask], first)
        ).astype(BF16)
        wide = wide + nn(jnp.concatenate(split(first), axis=0), wv[mask])
        gram = gram + nt(first, first, EXACT)
    product = wide[:rank] + wide[rank:] + 2.0 * nn(gram, ob[...], EXACT)
    pay[0 : 2 * rank] = gu_first[...].astype(BF16)
    pay[2 * rank : 3 * rank] = d_second[...].astype(BF16)
    pay[3 * rank : 4 * rank] = r_stat[1, 8 : 8 + rank].astype(BF16)
    pay[4 * rank : 5 * rank] = (
        2.0 * tn(lowrank[...], og[...]) + 2.0 * product * factor
    ).astype(BF16)
    pay[5 * rank : 6 * rank] = jnp.broadcast_to(o_drift, (rank, features)).astype(BF16)
    pay[7 * rank :] = jnp.zeros_like(pay[7 * rank :])
    totals = Totals(
        sender, count, depth, pay, along_in, part, group_in, block, span_sum, None, total_sems
    )
    totals.give()
    side_line[0] = side[...].astype(BF16)
    sides = [
        sender.copy(
            side_line.at[0], side_line.at[flip], (side_sems.at[0, flip], side_sems.at[1, flip]), 0, flip
        )
        for flip in flips
    ]
    start(sides)
    for load in part_loads:
        load.wait()
    if count == 8:
        relay(parts.at[1], landed, sums)
    for copy in copies + late:
        copy.wait()

    short = total <= 2048
    factor2 = SOFTMAX_SCALE * LOG2E
    kept = lax.broadcasted_iota(jnp.int32, (rows, rows), 0) <= lax.broadcasted_iota(
        jnp.int32, (rows, rows), 1
    )

    def one_head(h, carry):
        load_head(count, rows, h, xs, q_stat, cosine, sine, q, k, v)
        for mask in others:
            landing(h, mask).wait_recv()
        own = pl.ds(pl.multiple_of(h * HDIM, HDIM), HDIM)

        def lanes(part):
            return pl.ds(pl.multiple_of((part * heads + h) * HDIM, HDIM), HDIM)

        for a in range(count):
            at = pl.ds(a * rows, rows)
            values = dos[at, own].astype(F32) * attended[a ^ me, :, own].astype(F32)
            column = jnp.sum(values, axis=1, keepdims=True)
            centre[:, at] = jnp.transpose(jnp.broadcast_to(column, (rows, HDIM)))[:8]

        def finish(a, part, grad):
            at = pl.ds(a * rows if isinstance(a, int) else pl.multiple_of(a * rows, rows), rows)
            if part < 2:
                grad = turn(grad, cosine[at], -sine[at])
            out[a ^ me, :, lanes(part)] = (grad * q_stat[part, 1:2, own]).astype(BF16)
            return jnp.sum(grad * xs[at, lanes(part)].astype(F32), axis=0, keepdims=True)

        def pair_grads(at, after, bias, keep):
            key = k[at]
            weights = jnp.exp2(nt(key, q[after]) * factor2 + (bias - logsum[h, :, after]))
            weights = keep(weights)
            score_grad = weights * (nt(v[at], dos[after, own]) - centre[:1, after])
            score_grad = score_grad.astype(BF16)
            value_grad = nn(weights.astype(BF16), dos[after, own])
            return nn(score_grad, q[after]), value_grad, tn(score_grad, key)

        zero = jnp.zeros((1, HDIM), F32)
        iota = lax.broadcasted_iota(jnp.int32, (rows, 1), 0)
        if short:
            key_drift, value_drift = zero, zero
            for a in range(count):
                bias = jnp.where(a * rows + iota < length, 0.0, MASKED)

                def keep(weights):
                    first = jnp.where(kept, weights[:, :rows], 0.0)
                    if a == count - 1:
                        return first
                    return jnp.concatenate([first, weights[:, rows:]], axis=1)

                at, after = pl.ds(a * rows, rows), pl.ds(a * rows, total - a * rows)
                key_grad, value_grad, query_part = pair_grads(at, after, bias, keep)
                if a == 0:
                    dq[...] = query_part
                else:
                    dq[after] += query_part
                key_drift = key_drift + finish(a, 1, key_grad * SOFTMAX_SCALE)
                value_drift = value_drift + finish(a, 2, value_grad)
        else:
            dq[...] = jnp.zeros_like(dq)

            def one_block(a, drifts):
                start_at = pl.multiple_of(a * rows, rows)
                at = pl.ds(start_at, rows)
                bias = jnp.where(start_at + iota < length, 0.0, MASKED)

                def one_pair(i, grads):
                    after = pl.ds(pl.multiple_of(i * rows, rows), rows)
                    ahead = (i - a) * rows

                    def keep(weights):
                        return jnp.where(kept | (ahead > 0), weights, 0.0)

                    key_part, value_part, query_part = pair_grads(at, after, bias, keep)
                    dq[after] += query_part
                    return grads[0] + key_part, grads[1] + value_part

                none = jnp.zeros((rows, HDIM), F32)
                key_grad, value_grad = lax.fori_loop(a, count, one_pair, (none, none))
                return (
                    drifts[0] + finish(a, 1, key_grad * SOFTMAX_SCALE),
                    drifts[1] + finish(a, 2, value_grad),
                )

            key_drift, value_drift = lax.fori_loop(0, count, one_block, (zero, zero))
        query_drift = zero
        for a in range(count):
            query_drift = query_drift + finish(a, 0, dq[pl.ds(a * rows, rows)] * SOFTMAX_SCALE)
        drift[0, :, own] = query_drift
        drift[1, :, own] = key_drift
        drift[2, :, own] = value_drift

        @pl.when(h == 0)
        def _():
            totals.add_along()
            if count == 8:
                start(sums[1])

        return carry

    lax.fori_loop(0, heads, one_head, 0)
    outs.append(move(out, out_all))
    totals.add_group()
    arrive(sides)
    side_total[...] = along_total(sender, depth, side_line)

    def rows_out(d, value, carry):
        result[:, d] = (hidden[:, d] + value * (d_mag[:, d] / r_stat[1, 0:1, d])).astype(BF16)
        d_drift[:, d] = jnp.sum(cot[:, d].astype(F32) * value, axis=0, keepdims=True)
        return carry

    lax.fori_loop(0, features // TILE, finish_reduce(count, parts.at[0], landed, sums, rows_out), 0)
    outs.append(move(result, result_out))
    totals.group()
    totals.end()
    for copy in outs:
        copy.wait()
    leave(sides)
    leave_stages(sums)
    for h in range(heads):
        for mask in others:
            exchange(h, mask).wait_send()


def attend_backward(blocks, features, rank, units, operands):
    count, rows, width = blocks.shape
    depth = lax.axis_size("dp")
    head_width = width // 3
    heads = head_width // HDIM
    total = count * rows
    slots = count // 2
    many = pltpu.VMEM((slots, rows, features), BF16)
    early = totals_scratch(8 * rank, features, count, depth)
    return call(
        functools.partial(attend_backward_body, count, depth),
        "attend_backward",
        (
            shape((count, rows, width), BF16),
            shape((3, 1, head_width), F32),
            shape((rows, features), F32),
            shape((rows, features), BF16),
            shape((1, features), F32),
            shape(early[5].shape, BF16),
            shape((4 * rank, units), F32),
        ),
        [SMEM, VMEM, ANY, ANY, ANY, ANY, VMEM, ANY, ANY] + [VMEM] * 4
        + [ANY, ANY, VMEM, ANY, ANY, VMEM, VMEM, ANY] + [VMEM] * 3,
        (ANY, VMEM, ANY, ANY) + (VMEM,) * 3,
        [pltpu.VMEM((total, width), BF16), pltpu.VMEM((total, head_width), BF16)]
        + [pltpu.VMEM((total, HDIM), BF16)] * 3
        + [
            pltpu.VMEM((total, HDIM), F32),
            pltpu.VMEM((8, total), F32),
            pltpu.VMEM((count, head_width, features), BF16),
            pltpu.VMEM((rows, features), BF16),
            pltpu.VMEM((count, rows, head_width), BF16),
            pltpu.VMEM((2 if count == 8 else 1, rows, features), BF16),
            many,
            pltpu.VMEM((depth, 4 * rank, units), BF16),
            pltpu.VMEM((total, HDIM), F32),
            pltpu.VMEM((total, HDIM), F32),
            pltpu.VMEM((count, rows, head_width), BF16),
            pltpu.VMEM((count, rows, head_width), BF16),
            pltpu.VMEM((rows, features), F32),
            pltpu.VMEM((rows, features), BF16),
            pltpu.VMEM((rows, features), BF16),
            pltpu.VMEM((rows, features), BF16),
            pltpu.VMEM((count, rows, width), BF16),
            pltpu.VMEM((rows, features), F32),
            pltpu.VMEM((rows, features), BF16),
            pltpu.VMEM((1, features), F32),
        ]
        + early[:5]
        + [
            early[7],
            DMA((11,)),
            DMA((count,)),
            DMA((count,)),
            DMA((2,)),
            DMA((2, heads, count)),
            DMA((2, slots, 2)),
            DMA((2, depth)),
        ],
        10 * heads * total * total * HDIM + 2 * rows * features * features,
        2 * total * width * 4,
        operands,
        4,
    )


def qkv_backward_body(
    count, depth, grads, u_all, w_own, w_par, d_own, qa, qb, qmag, q_stat, drift, r_stat, da, db, d_mag,
    early_sum, d_drift, side_total, tokens_in, gain, hidden_grad_in,
    tokens_grad_out, first_grad, own_total, upper, lower, d_mag_grad, gu_total, o_upper, o_mag_grad, o_total,
    u, w, wd, b_own, b_par, parts, landed, second_own, second_par, qb_par, g_first, g_own, g_par, g_landed, own_line,
    lows, dx_sum, tokens, hidden_grad, tokens_grad,
    pay, along_in, part, group_in, block, span_sum, main, total_sems, early_main, early_sems,
    move_sems, sems, u_sems, own_sems, par_sems, reduce_sems, small_sems, line_sems,
):
    sender = Sender()
    slots = slots_of(count)
    order = [2, 1, 3, 0] if count == 8 else list(range(len(slots) - 1, -1, -1))
    maps, features, width = w_own.shape
    rank = qb.shape[1]
    rows = grads.shape[1]
    half = rows // 2
    others = list(range(1, count))
    flips = list(range(1, depth))
    move = Mover(move_sems)
    loads = {slot: pltpu.make_async_copy(u_all.at[slot], u.at[slot], u_sems.at[slot]) for slot in order}
    loads[order[0]].start()
    local = start_all([(w_own, w.at[pl.ds(0, maps)]), (w_par, w.at[pl.ds(maps, maps)]), (d_own, wd)], sems)
    for slot in order[1:]:
        loads[slot].start()
    late = [move(tokens_in, tokens), move(hidden_grad_in, hidden_grad)]
    sender.meet(others, flips)
    early_width = early_sum.shape[1]

    def early_span(place):
        return pl.ds(pl.multiple_of(place * early_width, early_width), early_width)

    def early(flip, place):
        pair = (early_sems.at[0, flip], early_sems.at[1, flip])
        return sender.copy(early_sum, early_main.at[:, early_span(place)], pair, 0, flip)

    sums = reduce_stages(sender, count, parts, landed, reduce_sems)
    small = sender.copy(qb, qb_par, (small_sems.at[0, 0], small_sems.at[1, 0]), 1)
    small.start()
    keeps, sends = {}, {}
    for slot in order:
        for h, mask in enumerate(slots[slot]):
            at = pl.ds(h * half, half)
            send = sender.copy(
                grads.at[mask ^ 1, at],
                b_par.at[slot, at],
                (par_sems.at[0, slot, h], par_sems.at[1, slot, h]),
                1,
            )
            keep = pltpu.make_async_copy(
                grads.at[mask, at], b_own.at[slot, at], own_sems.at[slot, h]
            )
            send.start()
            keep.start()
            sends.setdefault(slot, []).append(send)
            keeps.setdefault(slot, []).append(keep)
    for flip in flips:
        early(flip, sender.place).start()
    early_main[:, early_span(sender.place)] = early_sum[...]
    first_t = qa[...].reshape(maps * rank, features).astype(BF16)
    second_own[...] = jnp.zeros_like(second_own)
    second_par[...] = jnp.zeros_like(second_par)
    small.wait_recv()
    for s in range(maps):
        at, lanes = pl.ds(s * rank, rank), pl.ds(s * width, width)
        second_own[at, lanes] = (2.0 * qb[s]).astype(BF16)
        second_par[at, lanes] = (2.0 * qb_par[s]).astype(BF16)

    def low_rank(slot, first):
        for keep in keeps[slot]:
            keep.wait()
        arrive(sends[slot])
        loads[slot].wait()
        own, par = b_own.at[slot], b_par.at[slot]
        lows[slot], low_t = both_ways(nt(own[...], second_own[...]) + nt(par[...], second_par[...]))
        _, lowrank_t = both_ways(nt(u[slot], first_t))
        for s in range(maps):
            lanes = pl.ds(s * width, width)
            piece = lowrank_t[s * rank : (s + 1) * rank]
            own_part, par_part = 2.0 * nn(piece, own[:, lanes]), 2.0 * nn(piece, par[:, lanes])
            if first:
                g_own[s], g_par[s] = own_part, par_part
            else:
                g_own[s] += own_part
                g_par[s] += par_part
        part = nn(low_t, u[slot])
        if first:
            g_first[...] = part
        else:
            g_first[...] += part

    def input_grad(slot):
        own, par = b_own.at[slot], b_par.at[slot]
        for begin in range(0, features, TILE):
            d = pl.ds(begin, TILE)
            dx = nn(lows[slot], first_t[:, begin : begin + TILE])
            for s in range(maps):
                lanes = pl.ds(s * width, width)
                dx = dx + nt(own[:, lanes], w[s, d, :]) + nt(par[:, lanes], w[maps + s, d, :])
            parts[slot, :, d] = dx.astype(BF16)
        if slot and (count != 8 or slot == 2):
            start(sums[slot])

    low_rank(order[0], True)
    local[0].wait()
    local[1].wait()
    input_grad(order[0])
    for slot in order[1:]:
        low_rank(slot, False)

    give = sender.copy(g_par, g_landed, (small_sems.at[0, 1], small_sems.at[1, 1]), 1)
    give.start()
    factors = []
    for s in range(maps):
        norm = q_stat[s, 0:1]
        factor = -drift[s] * qmag[s : s + 1] / (norm * norm * norm)
        factors.append(factor)
        pay[s * rank : (s + 1) * rank] = (
            g_first[s * rank : (s + 1) * rank]
            + 2.0 * second_direction(qb[s] * factor, qb[s], w[s], qa[s])
        ).astype(BF16)
    at = maps * rank
    pay[at : at + rank] = jnp.broadcast_to(d_drift[...], (rank, features)).astype(BF16)
    if at + rank < pay.shape[0]:
        pay[at + rank :] = jnp.zeros_like(pay[at + rank :])
    totals = Totals(
        sender, count, depth, pay, along_in, part, group_in, block, span_sum, main, total_sems
    )
    totals.give()
    if len(order) > 2:
        input_grad(order[1])
    for slot in order[2:]:
        input_grad(slot)
    totals.add_along()
    if count == 8:
        relay(parts.at[3], landed, sums)
    give.wait_recv()
    for s in range(maps):
        own_line[0, s * rank : (s + 1) * rank] = (
            g_own[s] + g_landed[s] + 2.0 * q_stat[s, 8 : 8 + rank] * factors[s]
        ).astype(BF16)
    magnitudes = [drift[s] / q_stat[s, 0:1] for s in range(maps)]
    magnitudes = jnp.concatenate(magnitudes + [jnp.zeros((rank - maps, width), F32)], axis=0)
    own_line[0, maps * rank :] = magnitudes.astype(BF16)
    along = [
        sender.copy(
            own_line.at[0], own_line.at[flip], (line_sems.at[0, flip], line_sems.at[1, flip]), 0, flip
        )
        for flip in flips
    ]
    start(along)
    totals.add_group()
    if count == 8:
        start(sums[1])
    arrive(along)
    own_total[...] = along_total(sender, depth, own_line)
    totals.group()
    totals.share()
    for flip in flips:
        early(flip, sender.place ^ flip).wait_recv()
    gu_total[...] = early_main[0 : 2 * rank].astype(F32)
    d_sums = early_main[2 * rank : 4 * rank].astype(F32)
    o_upper[...] = early_main[4 * rank : 5 * rank].astype(F32)
    o_mag_grad[...] = early_main[5 * rank : 6 * rank].astype(F32)[:1] / r_stat[0, 0:1]
    o_total[...] = early_main[
        6 * rank : 7 * rank, pl.ds(pl.multiple_of(sender.me * width, width), width)
    ].astype(F32)
    totals.take()
    first_grad[...] = main[0 : maps * rank].astype(F32)
    total_drift = main[maps * rank : (maps + 1) * rank].astype(F32)[:1]
    norm = r_stat[1, 0:1]
    factor = -total_drift * d_mag[...] / (norm * norm * norm)
    d_mag_grad[...] = total_drift / norm
    upper[...] = d_sums[0:rank] + (2.0 / depth) * d_sums[rank:] * factor
    local[2].wait()
    lower[...] = side_total[2 * rank : 3 * rank] + 2.0 * second_direction(
        db[...] * factor, db[...], wd[...], da[...]
    )

    def out(d, value, carry):
        dx_sum[:, d] = value
        return carry

    lax.fori_loop(0, features // TILE, finish_reduce(count, parts.at[0], landed, sums, out), 0)
    for copy in late:
        copy.wait()
    scale, back = norm_statistics(
        lambda d: tokens[:, d].astype(F32), lambda d: dx_sum[:, d] * gain[:, d], features, rows
    )

    def rows_grad(step, carry):
        d = pl.ds(pl.multiple_of(step * TILE, TILE), TILE)
        tokens_grad[:, d] = (
            hidden_grad[:, d] + scale * (dx_sum[:, d] * gain[:, d]) - tokens[:, d].astype(F32) * back
        )
        return carry

    lax.fori_loop(0, features // TILE, rows_grad, 0)
    last = move(tokens_grad, tokens_grad_out)
    totals.end()
    totals.end_share()
    for flip in flips:
        early(flip, sender.place).wait_send()
    last.wait()
    leave(along + [small, give])
    leave_stages(sums)
    leave_stages(sends)


def qkv_backward(grads, u_all, w_own, w_par, d_own, small):
    count, rows, _ = grads.shape
    depth = lax.axis_size("dp")
    slots = count // 2
    maps, features, width = w_own.shape
    qb = small[1]
    rank = qb.shape[1]
    ranks = maps * rank
    units = d_own.shape[0]
    many = pltpu.VMEM((slots, rows, features), BF16)
    return call(
        functools.partial(qkv_backward_body, count, depth),
        "qkv_backward",
        (
            shape((rows, features), F32),
            shape((ranks, features), F32),
            shape((ranks + rank, width), F32),
            shape((rank, features), F32),
            shape((rank, units), F32),
            shape((1, features), F32),
            shape((2 * rank, features), F32),
            shape((rank, features), F32),
            shape((1, features), F32),
            shape((rank, width), F32),
        ),
        [ANY] * 5 + [VMEM] * (len(small) - 3) + [ANY, VMEM, ANY],
        (ANY,) + (VMEM,) * 9,
        [
            many,
            pltpu.VMEM((2 * maps, features, width), BF16),
            pltpu.VMEM((units, features), BF16),
            pltpu.VMEM((slots, rows, maps * width), BF16),
            pltpu.VMEM((slots, rows, maps * width), BF16),
            many,
            many,
            pltpu.VMEM((ranks, maps * width), BF16),
            pltpu.VMEM((ranks, maps * width), BF16),
            pltpu.VMEM(qb.shape, F32),
            pltpu.VMEM((ranks, features), F32),
            pltpu.VMEM(qb.shape, F32),
            pltpu.VMEM(qb.shape, F32),
            pltpu.VMEM(qb.shape, F32),
            pltpu.VMEM((depth, ranks + rank, width), BF16),
            pltpu.VMEM((slots, rows, ranks), BF16),
            pltpu.VMEM((rows, features), F32),
            pltpu.VMEM((rows, features), BF16),
            pltpu.VMEM((rows, features), F32),
            pltpu.VMEM((rows, features), F32),
        ]
        + totals_scratch(ranks + rank, features, count, depth)
        + [
            pltpu.VMEM((8 * rank, features), BF16),
            DMA((2, depth)),
            DMA((3,)),
            DMA((3,)),
            DMA((slots,)),
            DMA((slots, 2)),
            DMA((2, slots, 2)),
            DMA((2, slots, 2)),
            DMA((2, 2)),
            DMA((2, depth)),
        ],
        4 * slots * rows * features * maps * width,
        8 * features * maps * width,
        (grads, u_all, w_own, w_par, d_own, *small),
        5,
    )


def results_body(
    maps, first, own, upper, o_mag, gu, side, o_first, d_upper, d_lower, d_mag,
    first_out, second_out, mag_out, o_first_out, upper_out, o_mag_out, gu_first_out, gu_second_out, gu_mag_out,
    d_lower_out, d_upper_out, d_mag_out,
):
    rank = upper.shape[0]
    for s in range(maps):
        at = pl.ds(s * rank, rank)
        first_out[s] = first[at]
        second_out[s] = own[at]
    for s in range(2):
        at = pl.ds(s * rank, rank)
        gu_first_out[s] = gu[at]
        gu_second_out[s] = side[at]
    mag_out[...] = own[maps * rank : maps * rank + maps]
    gu_mag_out[...] = side[3 * rank : 3 * rank + 2]
    o_first_out[...] = o_first[...]
    upper_out[...] = upper[...]
    o_mag_out[...] = o_mag[...]
    d_lower_out[...] = d_lower[...]
    d_upper_out[...] = d_upper[...]
    d_mag_out[...] = d_mag[...]


def results(maps, values):
    first, own, upper, o_mag, gu, side, o_first, d_upper, d_lower, d_mag = values
    rank, features = upper.shape
    units, width = side.shape[1], own.shape[1]
    return pl.pallas_call(
        functools.partial(results_body, maps),
        name="results",
        out_shape=(
            shape((maps, rank, features), F32),
            shape((maps, rank, width), F32),
            shape((maps, width), F32),
            shape(o_first.shape, F32),
            shape(upper.shape, F32),
            shape(o_mag.shape, F32),
            shape((2, rank, features), F32),
            shape((2, rank, units), F32),
            shape((2, units), F32),
            shape(d_lower.shape, F32),
            shape(d_upper.shape, F32),
            shape(d_mag.shape, F32),
        ),
        in_specs=[VMEM] * len(values),
        out_specs=(VMEM,) * 12,
    )(*values)


def rope_tables(total):
    half = HDIM // 2
    frequency = np.exp(-np.log(ROPE_THETA) * np.arange(half) / half)
    angles = np.arange(total)[:, None] * frequency[None, :]
    cosine, sine = np.cos(angles), np.sin(angles)
    return (
        jnp.asarray(np.concatenate([cosine, cosine], axis=1), F32),
        jnp.asarray(np.concatenate([-sine, sine], axis=1), F32),
    )


def body(
    tokens,
    attn_gain,
    ffn_gain,
    qkv_base,
    qkv_first,
    qkv_second,
    qkv_magnitude,
    output_frozen_weight,
    output_first,
    output_upper_map,
    output_magnitude,
    gate_up_base,
    gate_up_first,
    gate_up_second,
    gate_up_magnitude,
    down_frozen_weight,
    down_first,
    down_upper_map,
    down_magnitude,
    lengths,
    cotangent,
):
    rows, features = tokens.shape
    total = rows * lax.axis_size("tensor")
    rank = qkv_first.shape[2]
    units = down_frozen_weight.shape[0]
    cosine, sine = rope_tables(total)
    qkv_first_t = jnp.swapaxes(qkv_first, 1, 2)
    gu_first_t = jnp.swapaxes(gate_up_first, 1, 2)
    gu_base_t = jnp.swapaxes(gate_up_base, 1, 2)
    out_first_t = output_first.T
    down_first_t = down_first.T
    out_mag, down_mag = output_magnitude[None], down_magnitude[None]

    blocks, normed_all, qkv_other, gu_other, down_other, out_parts, at_all, q_stat, g_stat, r_stat, upstream = project(
        lengths,
        tokens,
        attn_gain[None],
        cotangent,
        qkv_base,
        gu_base_t,
        down_frozen_weight,
        output_frozen_weight,
        (
            qkv_first_t,
            qkv_second,
            qkv_magnitude,
            gu_first_t,
            gate_up_second,
            gate_up_magnitude,
            out_first_t,
            output_upper_map,
            down_first_t,
            down_upper_map,
        ),
    )
    attended, logsum, joined, out_weight, hidden, out_before, ffn_normed, out_lowrank, cot_some = attend_forward(
        lengths, q_stat, cosine, sine, blocks, out_parts, at_all, output_upper_map, out_mag, r_stat, tokens,
        ffn_gain[None], upstream,
    )
    down_all, ffn_normed_grad, gu_first_part, side, down_second_part = ffn(
        ffn_normed, upstream, cot_some, gu_base_t, gu_other, down_frozen_weight, down_other,
        (
            gu_first_t, gate_up_second, gate_up_magnitude, down_first_t, down_upper_map, g_stat, r_stat,
            down_mag,
        ),
    )
    (
        head_grads, qkv_drift, hidden_grad, result, down_drift, early_sum, side_total,
    ) = attend_backward(
        blocks,
        features,
        rank,
        units,
        (
            lengths, q_stat, cosine, sine, blocks, attended, logsum, joined, out_weight, at_all,
            output_upper_map, out_mag, r_stat, hidden, out_before, out_lowrank, upstream,
            ffn_normed_grad, ffn_gain[None], down_mag, down_all, gu_first_part, down_second_part, side,
        ),
    )
    (
        tokens_grad, qkv_first_grad, own_total, down_upper_gradient, down_lower_gradient, down_magnitude_grad,
        gate_up_first_grad, output_upper_gradient, output_magnitude_grad, output_first_grad,
    ) = qkv_backward(
        head_grads, normed_all, qkv_base, qkv_other, down_frozen_weight,
        (
            qkv_first_t, qkv_second, qkv_magnitude, q_stat, qkv_drift, r_stat, down_first_t,
            down_upper_map, down_mag, early_sum, down_drift, side_total, tokens, attn_gain[None],
            hidden_grad,
        ),
    )
    (
        qkv_first_grad, qkv_second_grad, qkv_magnitude_grad, output_first_grad, output_upper_gradient,
        output_magnitude_grad, gate_up_first_grad, gate_up_second_grad, gate_up_magnitude_grad,
        down_lower_gradient, down_upper_gradient, down_magnitude_grad,
    ) = results(
        3,
        (
            qkv_first_grad, own_total, output_upper_gradient, output_magnitude_grad, gate_up_first_grad, side_total,
            output_first_grad, down_upper_gradient, down_lower_gradient, down_magnitude_grad,
        ),
    )
    return (
        result,
        tokens_grad,
        jnp.swapaxes(qkv_first_grad, 1, 2),
        qkv_second_grad,
        qkv_magnitude_grad,
        output_first_grad.T,
        output_upper_gradient,
        output_magnitude_grad[0],
        jnp.swapaxes(gate_up_first_grad, 1, 2),
        gate_up_second_grad,
        gate_up_magnitude_grad,
        down_lower_gradient.T,
        down_upper_gradient,
        down_magnitude_grad[0],
    )


def solution(mesh):
    placed = (
        P(("dp", "tensor"), None),
        P(),
        P(),
        P(None, None, "tensor"),
        P(),
        P(None, None, "tensor"),
        P(None, "tensor"),
        P("tensor", None),
        P("tensor", None),
        P(),
        P(),
        P(None, None, "tensor"),
        P(),
        P(None, None, "tensor"),
        P(None, "tensor"),
        P("tensor", None),
        P("tensor", None),
        P(),
        P(),
        P("dp"),
        P(("dp", "tensor"), None),
    )
    return jax.shard_map(
        body,
        mesh=mesh,
        in_specs=placed,
        out_specs=(
            P(("dp", "tensor"), None),
            P(("dp", "tensor"), None),
            P(),
            P(None, None, "tensor"),
            P(None, "tensor"),
            P("tensor", None),
            P(),
            P(),
            P(),
            P(None, None, "tensor"),
            P(None, "tensor"),
            P("tensor", None),
            P(),
            P(),
        ),
        check_vma=False,
    )
```
